32 devices in a mesh: rep: 4 (over y, x), fsdp: 4 (over z), seq: 2 (over core).
Axes of the slice: x: 2, y: 2, z: 4, core: 2. Of those that a mesh axis runs over, the one named last changes fastest.
Arguments:
- block_input: bfloat16 [4096, 1024], P(('rep', 'fsdp', 'seq')), may hold values from -6 to 6
- ln1_gain: bfloat16 [1024], P('fsdp'), may hold values from 0.5 to 1.5
- ln1_shift: bfloat16 [1024], P('fsdp'), may hold values from -1 to 1
- qkv_weight: bfloat16 [1024, 3072], P('fsdp'), may hold values from -0.1875 to 0.1875
- qv_bias: bfloat16 [2048], P('fsdp'), may hold values from -1 to 1
- proj_weight: bfloat16 [1024, 1024], P('fsdp'), may hold values from -0.75 to 0.75
- proj_bias: bfloat16 [1024], P('fsdp'), may hold values from -1 to 1
- ln2_gain: bfloat16 [1024], P('fsdp'), may hold values from 0.5 to 1.5
- ln2_shift: bfloat16 [1024], P('fsdp'), may hold values from -1 to 1
- fc_weight: bfloat16 [4096, 1024], P('fsdp'), may hold values from -0.1875 to 0.1875
- fc_bias: bfloat16 [4096], P('fsdp'), may hold values from -1 to 1
- out_weight: bfloat16 [4096, 1024], P('fsdp'), may hold values from -0.09375 to 0.09375
- out_bias: bfloat16 [1024], P('fsdp'), may hold values from -1 to 1
- cotangent: bfloat16 [4096, 1024], P(('rep', 'fsdp', 'seq')), may hold values from -6 to 6
Outputs:
- block_output: bfloat16 [4096, 1024], P(('rep', 'fsdp', 'seq'))
- input_grad: float32 [4096, 1024], P(('rep', 'fsdp', 'seq'))
- ln1_gain_grad: float32 [1024], P('fsdp')
- ln1_shift_grad: float32 [1024], P('fsdp')
- qkv_weight_grad: float32 [1024, 3072], P('fsdp')
- qv_bias_grad: float32 [2048], P('fsdp')
- proj_weight_grad: float32 [1024, 1024], P('fsdp')
- proj_bias_grad: float32 [1024], P('fsdp')
- ln2_gain_grad: float32 [1024], P('fsdp')
- ln2_shift_grad: float32 [1024], P('fsdp')
- fc_weight_grad: float32 [4096, 1024], P('fsdp')
- fc_bias_grad: float32 [4096], P('fsdp')
- out_weight_grad: float32 [4096, 1024], P('fsdp')
- out_bias_grad: float32 [1024], P('fsdp')
The draws below stay inside these ranges and needn't reach their ends.
All inputs are finite; a program needn't handle non-finite values.
Results may differ from the reference program's by a relative error of at most 0.019.
Values may be sent and summed in bfloat16 or wider, within the bound.
No kernel may reach another device: no remote copies, remote signals or barrier semaphores. Data moves between devices by JAX's collectives and lax.ppermute only.
A program may use at most 192 MiB of HBM per device.

```python
import jax
import jax.numpy as jnp
from jax import lax

D = 1024
HEADS = 16
HEAD_DIM = 64
FF = 4096
LENGTH = 256
SEQS = 16
TOKENS = 4096


def strengthened(array, key, source, target, shards_of, factor):
    def block_of(position):
        return (jnp.arange(array.shape[position]) // (array.shape[position] // shards_of)).reshape((-1,) + (1,) * (array.ndim - 1 - position))

    near = jax.random.permutation(key, shards_of)[block_of(target)]
    far = (block_of(target) + shards_of // 2) % shards_of
    return jnp.where((block_of(source) == near) | (block_of(source) == far), factor * array, array)


def level_of(rng, dims, pieces, least, top_value):
    level = 1.0
    for axis_at, blocks in pieces:
        heights = jax.random.uniform(jax.random.fold_in(jax.random.fold_in(rng, 6), axis_at), (blocks,), jnp.float32, least / len(pieces), top_value / len(pieces))
        level = level * jnp.repeat(jnp.exp(heights), dims[axis_at] // blocks).reshape((-1,) + (1,) * (len(dims) - 1 - axis_at))
    return level


def normal_values(key, extent, scale, reach, pieces=(), kind=jnp.bfloat16):
    entries = jax.random.normal(key, extent, jnp.float32) * scale
    if len(pieces) > 0:
        entries = level_of(key, extent, pieces, -0.22, 0.18) * entries
    return jnp.clip(entries, min=-reach, max=reach).astype(kind)


def bell_draw_with(stream_key, extent, scale, most, split, heavy, held_as=jnp.bfloat16):
    drawn = scale * jax.random.normal(stream_key, extent, jnp.float32)
    if split:
        drawn = drawn * level_of(stream_key, extent, split, -0.22, 0.18)
    return jnp.clip(strengthened(drawn, jax.random.fold_in(stream_key, 3), *heavy), -most, most).astype(held_as)


def setup_inputs(seed: int = 0) -> dict:
    streams_of = jax.random.split(jax.random.key(seed), 15)
    block_input = normal_values(streams_of[0], (TOKENS, D), 1.0, 6.0, ((0, 32),))
    ln1_gain = jnp.clip(1.0 + 0.1 * jax.random.normal(streams_of[1], (D,), jnp.float32), 0.5, 1.5).astype(jnp.bfloat16)
    ln1_shift = normal_values(streams_of[2], (D,), 0.2, 1.0, ((0, 4),))
    qkv_weight = normal_values(streams_of[3], (D, 3 * D), D ** -0.5, 0.1875, ((0, 4),))
    qv_bias = normal_values(streams_of[4], (2 * D,), 0.2, 1.0, ((0, 4),))
    proj_weight = normal_values(streams_of[5], (D, D), (D // 16) ** -0.5, 0.75, ((0, 4),))
    proj_bias = normal_values(streams_of[6], (D,), 0.2, 1.0, ((0, 4),))
    ln2_gain = jnp.clip(1.0 + 0.1 * jax.random.normal(streams_of[7], (D,), jnp.float32), 0.5, 1.5).astype(jnp.bfloat16)
    ln2_shift = normal_values(streams_of[8], (D,), 0.2, 1.0, ((0, 4),))
    fc_weight = normal_values(streams_of[9], (FF, D), D ** -0.5, 0.1875, ((0, 4),))
    fc_bias = normal_values(streams_of[10], (FF,), 0.2, 1.0, ((0, 4),))
    out_weight = normal_values(streams_of[11], (FF, D), FF ** -0.5, 0.09375, ((0, 4),))
    out_bias = normal_values(streams_of[12], (D,), 0.2, 1.0, ((0, 4),))
    cotangent = bell_draw_with(streams_of[13], (TOKENS, D), 1.0, 6.0, ((0, 32),), (0, 1, 32, 2.75))
    return {"block_input": block_input, "ln1_gain": ln1_gain, "ln1_shift": ln1_shift, "qkv_weight": qkv_weight, "qv_bias": qv_bias, "proj_weight": proj_weight, "proj_bias": proj_bias, "ln2_gain": ln2_gain, "ln2_shift": ln2_shift, "fc_weight": fc_weight, "fc_bias": fc_bias, "out_weight": out_weight, "out_bias": out_bias, "cotangent": cotangent}


norm_eps = 1e-05
masked_value = -1e+30
highest = lax.Precision.HIGHEST

@jax.custom_vjp
def low(v):
    return lax.optimization_barrier(v.astype(jnp.bfloat16)).astype(jnp.float32)

@jax.custom_vjp
def low_back(v):
    return v

def low_keep(v):
    return (low(v), None)

def low_pass(kept, grad):
    return (grad,)

def back_keep(v):
    return (v, None)

def back_low(kept, grad):
    return (low(grad),)
low.defvjp(low_keep, low_pass)
low_back.defvjp(back_keep, back_low)

def layer_norm(values, gain, shift):
    centre = lax.optimization_barrier(jnp.mean(values, -1, keepdims=True))
    offsets = values - centre
    spread = lax.optimization_barrier(jnp.mean(offsets * offsets, -1, keepdims=True))
    return offsets * lax.rsqrt(spread + norm_eps) * gain + shift

def gelu_tanh(values):
    return 0.5 * values * (1.0 + jnp.tanh(0.7978845608028654 * (values + 0.044715 * values * values * values)))

def forward(params, inputs):
    gain_one, shift_one, qkv_weight, qv_bias, proj_weight, proj_bias, gain_two, shift_two, fc_weight, fc_bias, out_weight, out_bias = params
    groups, length, width = inputs.shape
    head_shape = (groups, length, HEADS, HEAD_DIM)
    normed = low(layer_norm(inputs, gain_one, shift_one))
    mixed = jnp.einsum('gtd,de->gte', normed, qkv_weight, precision=highest)
    queries = low_back(low(mixed[..., :width] + qv_bias[:width]))
    keys = low_back(low(mixed[..., width:2 * width]))
    values = low_back(low(mixed[..., 2 * width:] + qv_bias[width:]))
    key_heads = keys.reshape(head_shape)
    value_heads = values.reshape(head_shape)
    row_block = min(512, length)
    block_count = length // row_block
    query_blocks = jnp.moveaxis(queries.reshape(groups, block_count, row_block, HEADS, HEAD_DIM), 1, 0)
    starts = jnp.arange(block_count, dtype=jnp.int32) * row_block

    def attend_rows(item):
        block, start = item
        scores = jnp.einsum('gqhd,gkhd->ghqk', block, key_heads, precision=highest) * HEAD_DIM ** (-0.5)
        scores = low_back(scores)
        row_pos = lax.broadcasted_iota(jnp.int32, (row_block, length), 0) + start
        col_pos = lax.broadcasted_iota(jnp.int32, (row_block, length), 1)
        scores = jnp.where(col_pos <= row_pos, scores, masked_value)
        peak = lax.optimization_barrier(jnp.max(scores, -1, keepdims=True))
        exp_scores = jnp.exp(scores - peak)
        probs = low(exp_scores / lax.optimization_barrier(jnp.sum(exp_scores, -1, keepdims=True)))
        return jnp.einsum('ghqk,gkhd->gqhd', probs, value_heads, precision=highest)
    attended = lax.map(jax.checkpoint(attend_rows), (query_blocks, starts))
    attended = jnp.moveaxis(attended, 0, 1).reshape(groups, length, width)
    attended = low_back(low(attended))
    branch = low_back(jnp.einsum('gtd,de->gte', attended, proj_weight, precision=highest) + proj_bias)
    middle = inputs + branch
    normed_two = low(layer_norm(middle, gain_two, shift_two))
    preact = low_back(jnp.einsum('gtd,fd->gtf', normed_two, fc_weight, precision=highest) + fc_bias)
    hidden = low(gelu_tanh(preact))
    output = low_back(jnp.einsum('gtf,fd->gtd', hidden, out_weight, precision=highest) + out_bias)
    return middle + output

def group_size():
    ceiling = max(1, 4096 // LENGTH)
    chosen = 1
    for number in range(1, SEQS + 1):
        if SEQS % number == 0 and number <= ceiling:
            chosen = number
    return chosen

def reference(block_input, ln1_gain, ln1_shift, qkv_weight, qv_bias, proj_weight, proj_bias, ln2_gain, ln2_shift, fc_weight, fc_bias, out_weight, out_bias, cotangent):
    params = tuple((p.astype(jnp.float32) for p in (ln1_gain, ln1_shift, qkv_weight, qv_bias, proj_weight, proj_bias, ln2_gain, ln2_shift, fc_weight, fc_bias, out_weight, out_bias)))
    per_step = group_size()
    steps_count = SEQS // per_step
    inputs = block_input.astype(jnp.float32).reshape(steps_count, per_step, LENGTH, D)
    grads_in = cotangent.astype(jnp.float32).reshape(steps_count, per_step, LENGTH, D)

    def one_step(totals, item):
        inputs_group, grad_group = item
        result, pull = jax.vjp(forward, params, inputs_group)
        param_grads, input_grads = pull(grad_group)
        totals = tuple((a + b for a, b in zip(totals, param_grads)))
        return (totals, (result.astype(jnp.bfloat16), input_grads))
    start = tuple((jnp.zeros(p.shape, jnp.float32) for p in params))
    totals, (outputs, input_grads) = lax.scan(one_step, start, (inputs, grads_in))
    return (outputs.reshape(TOKENS, D), input_grads.reshape(TOKENS, D), totals[0], totals[1], totals[2], totals[3], totals[4], totals[5], totals[6], totals[7], totals[8], totals[9], totals[10], totals[11])
```

```python
import jax
import jax.numpy as jnp
from jax import lax
from jax.sharding import PartitionSpec as P

HEADS = 16
HEAD_DIM = 64

norm_eps = 1e-05
masked_value = -1e30
f32 = jnp.float32
bf16 = jnp.bfloat16


def normalise(values):
    centre = jnp.mean(values, -1, keepdims=True)
    offsets = values - centre
    spread = jnp.mean(offsets * offsets, -1, keepdims=True)
    scale = lax.rsqrt(spread + norm_eps)
    return offsets * scale, scale


def norm_pull(unit, scale, gain, grad):
    inner = grad * gain
    first = jnp.mean(inner, -1, keepdims=True)
    second = jnp.mean(inner * unit, -1, keepdims=True)
    return scale * (inner - first - unit * second), jnp.sum(grad * unit, 0), jnp.sum(grad, 0)


def gelu_and_slope(values):
    rate = 0.7978845608028654
    squared = values * values
    bent = jnp.tanh(rate * (values + 0.044715 * values * squared))
    half = 0.5 * (1.0 + bent)
    slope = half + 0.5 * values * (1.0 - bent * bent) * (rate * (1.0 + 3.0 * 0.044715 * squared))
    return values * half, slope


def contract(left, right, left_axis, right_axis):
    return lax.dot_general(
        left, right, (((left_axis,), (right_axis,)), ((), ())), preferred_element_type=f32
    )


def swap(value, axis, size, offset):
    return lax.ppermute(value, axis, [(i, i ^ offset) for i in range(size)])


def pick(array, index, axis):
    return lax.dynamic_index_in_dim(array, index, axis, keepdims=False)


def place(pieces, positions):
    stacked = jnp.zeros((len(pieces),) + pieces[0].shape, pieces[0].dtype)
    for piece, position in zip(pieces, positions):
        stacked = lax.dynamic_update_index_in_dim(stacked, piece, position, 0)
    return stacked


def make_body(reps, shards, cores):
    def rep_swap(value, offset):
        return swap(value, "rep", reps, offset) if offset else value

    def shard_swap(value, offset):
        return swap(value, "fsdp", shards, offset) if offset else value

    def core_swap(value):
        return swap(value, "seq", cores, 1)

    def plane_gather(value):
        return [rep_swap(value, k) for k in range(reps)]

    def plane_exchange(pieces):
        return [rep_swap(piece, k) for k, piece in enumerate(pieces)]

    def pair_sum(pieces):
        while len(pieces) > 1:
            pieces = [pieces[i] + pieces[i + 1] for i in range(0, len(pieces), 2)]
        return pieces[0]

    def body(
        block_input,
        ln1_gain,
        ln1_shift,
        qkv_weight,
        qv_bias,
        proj_weight,
        proj_bias,
        ln2_gain,
        ln2_shift,
        fc_weight,
        fc_bias,
        out_weight,
        out_bias,
        cotangent,
    ):
        rows, width = block_input.shape
        shard_width = width // shards
        part = width // (reps * cores)
        rep_width = part * cores
        hidden_part = fc_weight.shape[0] // (reps * cores)
        head_scale = HEAD_DIM ** (-0.5)
        rep = lax.axis_index("rep")
        shard = lax.axis_index("fsdp")
        core = lax.axis_index("seq")
        rep_at = [rep ^ k for k in range(reps)]
        shard_at = [shard ^ k for k in range(shards)]

        inputs_all = jnp.concatenate(plane_gather(block_input), 0)

        columns = qkv_weight.reshape(shard_width, 3, reps, cores, part)
        columns = pick(pick(columns, rep, 2), core, 2).reshape(shard_width, 3 * part)
        fc_bias_part = pick(fc_bias.reshape(reps, -1), rep, 0)
        vectors = [
            ln1_gain,
            ln1_shift,
            qv_bias[:shard_width],
            qv_bias[shard_width:],
            proj_bias,
            ln2_gain,
            ln2_shift,
            out_bias,
            fc_bias_part,
        ]
        vectors = [jnp.pad(v, (0, 3 * part - v.shape[0])) for v in vectors]
        vectors = jnp.stack(vectors + [jnp.zeros_like(vectors[0])] * (16 - len(vectors)))
        packed = jnp.concatenate([columns, vectors], 0)
        packed = place([shard_swap(packed, k) for k in range(shards)], shard_at)
        columns = packed[:, :shard_width].reshape(width, 3 * part)
        vectors = packed[:, shard_width:, :].astype(f32)

        def vector(index, size):
            return vectors[:, index, :size].reshape(-1)

        gain_one, shift_one = vector(0, shard_width), vector(1, shard_width)
        qv_full = jnp.stack([vectors[:, 2, :shard_width], vectors[:, 3, :shard_width]], 1)
        qv_full = qv_full.reshape(2, reps, cores * part)
        proj_bias_full = vector(4, shard_width)
        gain_two, shift_two = vector(5, shard_width), vector(6, shard_width)
        out_bias_full = vector(7, shard_width)
        fc_bias_mine = vector(8, fc_bias_part.shape[0])
        qkv_mine = place([columns, core_swap(columns)], [core, 1 - core])
        qkv_mine = jnp.transpose(qkv_mine, (1, 0, 2)).reshape(width, cores * 3 * part)

        fc_part = pick(fc_weight.reshape(reps * cores, hidden_part, width), rep * cores + core, 0)
        out_part = pick(out_weight.reshape(reps * cores, hidden_part, width), rep * cores + core, 0)
        fc_mine = lax.all_gather(fc_part, ("fsdp", "seq"), axis=0, tiled=True)
        out_mine = lax.all_gather(out_part, ("fsdp", "seq"), axis=0, tiled=True)

        proj_full = lax.all_gather(proj_weight, "fsdp", axis=0, tiled=True)

        cot_all = jnp.concatenate(plane_gather(cotangent), 0)

        unit_one, scale_one = normalise(inputs_all.astype(f32))
        normed_all = (unit_one * gain_one + shift_one).astype(bf16)
        mixed = jnp.dot(normed_all, qkv_mine, preferred_element_type=f32)
        mixed = mixed.reshape(reps, rows, cores, 3, part)
        qv_mine = pick(qv_full, rep, 1).reshape(2, cores, part)
        heads = (reps, rows, rep_width // HEAD_DIM, HEAD_DIM)
        queries = (mixed[:, :, :, 0] + qv_mine[0]).astype(bf16).reshape(heads)
        keys = mixed[:, :, :, 1].astype(bf16).reshape(heads)
        values = (mixed[:, :, :, 2] + qv_mine[1]).astype(bf16).reshape(heads)
        far_pair = core_swap(jnp.stack([keys, values]))
        keys_both = jnp.concatenate([keys, far_pair[0]], 1)
        values_both = jnp.concatenate([values, far_pair[1]], 1)

        row_pos = lax.broadcasted_iota(jnp.int32, (rows, 2 * rows), 0)
        col_pos = lax.broadcasted_iota(jnp.int32, (rows, 2 * rows), 1)
        allowed = jnp.where(col_pos < rows, col_pos <= row_pos, core == 1)
        scores = jnp.einsum("sqhd,skhd->shqk", queries, keys_both, preferred_element_type=f32)
        scores = jnp.where(allowed, scores * head_scale, masked_value)
        peak = jnp.max(scores, -1, keepdims=True)
        powers = jnp.exp(scores - peak)
        probs = powers / jnp.sum(powers, -1, keepdims=True)
        probs_low = probs.astype(bf16)
        attended = jnp.einsum("shqk,skhd->sqhd", probs_low, values_both, preferred_element_type=f32)
        attended_low = attended.astype(bf16).reshape(reps, rows, rep_width)
        mine = place(plane_exchange([attended_low[k] for k in range(reps)]), rep_at)
        mine = jnp.transpose(mine, (1, 0, 2)).reshape(rows, width)
        middle = (
            block_input.astype(f32)
            + jnp.dot(mine, proj_full, preferred_element_type=f32)
            + proj_bias_full
        )
        unit_two, scale_two = normalise(middle)
        normed_two = (unit_two * gain_two + shift_two).astype(bf16)
        normed_two_all = jnp.concatenate(plane_gather(normed_two), 0)

        spread = []
        for k in range(reps):
            piece = rep_swap(attended_low, k)
            spread.append(jnp.concatenate([piece[j ^ k] for j in range(reps)], 0))
        attended_all = jnp.transpose(place(spread, rep_at), (1, 0, 2)).reshape(reps * rows, width)

        preact = contract(normed_two_all, fc_mine, 1, 1) + fc_bias_mine
        hidden, slope = gelu_and_slope(preact)
        hidden_low = hidden.astype(bf16)
        hidden_grad = contract(cot_all, out_mine, 1, 1)
        pre_grad = (hidden_grad * slope).astype(bf16)
        normed_grad = jnp.dot(pre_grad, fc_mine, preferred_element_type=f32).astype(bf16)
        normed_grad = normed_grad.reshape(reps, rows, width)
        normed_grad = plane_exchange([normed_grad[k] for k in range(reps)])
        normed_grad = pair_sum([v.astype(f32) for v in normed_grad])
        output = jnp.dot(hidden_low, out_mine, preferred_element_type=f32).astype(bf16)
        output = output.reshape(reps, rows, width)
        output = plane_exchange([output[k] for k in range(reps)])
        output = pair_sum([v.astype(f32) for v in output])
        block_output = (middle + output + out_bias_full).astype(bf16)

        out_grads = contract(hidden_low, cot_all, 0, 0).astype(bf16)
        fc_grads = contract(pre_grad, normed_two_all, 0, 0).astype(bf16)
        out_grads = lax.psum_scatter(out_grads, ("fsdp", "seq"), scatter_dimension=0, tiled=True)
        fc_grads = lax.psum_scatter(fc_grads, ("fsdp", "seq"), scatter_dimension=0, tiled=True)
        out_grads = lax.all_gather(out_grads, ("rep", "seq"), axis=0, tiled=True).astype(f32)
        fc_grads = lax.all_gather(fc_grads, ("rep", "seq"), axis=0, tiled=True).astype(f32)

        middle_part, gain_two_grads, shift_two_grads = norm_pull(
            unit_two, scale_two, gain_two, normed_grad
        )
        middle_grad = cotangent.astype(f32) + middle_part
        branch_grad = middle_grad.astype(bf16)
        attended_grad = contract(branch_grad, proj_full, 1, 1).astype(bf16)
        attended_grad = attended_grad.reshape(rows, reps, rep_width)
        attended_grad = plane_exchange([pick(attended_grad, i, 1) for i in rep_at])
        attended_grad = jnp.stack(attended_grad).reshape(heads)
        branch_cols = branch_grad.reshape(rows, reps, rep_width)
        branch_cols = plane_exchange([pick(branch_cols, i, 1) for i in rep_at])
        branch_cols = jnp.concatenate(branch_cols, 0)
        proj_grads = contract(attended_all, branch_cols, 0, 0).astype(bf16)
        proj_grads = proj_grads.reshape(shards, shard_width, cores, part)
        proj_grads = jnp.transpose(proj_grads, (0, 2, 1, 3)).reshape(-1, part)
        proj_grads = lax.psum_scatter(proj_grads, ("fsdp", "seq"), scatter_dimension=0, tiled=True)
        proj_grads = lax.all_gather(proj_grads, ("rep", "seq"), axis=0)
        proj_grads = jnp.transpose(proj_grads, (1, 0, 2)).reshape(shard_width, width).astype(f32)

        prob_grad = jnp.einsum("sqhd,skhd->shqk", attended_grad, values_both, preferred_element_type=f32)
        row_total = jnp.sum(probs * prob_grad, -1, keepdims=True)
        score_low = (probs * (prob_grad - row_total)).astype(bf16)
        query_grad = (
            jnp.einsum("shqk,skhd->sqhd", score_low, keys_both, preferred_element_type=f32)
            * head_scale
        )
        key_grad = (
            jnp.einsum("shqk,sqhd->skhd", score_low, queries, preferred_element_type=f32)
            * head_scale
        )
        value_grad = jnp.einsum("shqk,sqhd->skhd", probs_low, attended_grad, preferred_element_type=f32)
        far_grads = core_swap(jnp.stack([key_grad[:, rows:], value_grad[:, rows:]]).astype(bf16))
        key_grad = key_grad[:, :rows] + far_grads[0].astype(f32)
        value_grad = value_grad[:, :rows] + far_grads[1].astype(f32)
        mixed_grad = jnp.stack(
            [
                g.astype(bf16).reshape(reps * rows, cores, part)
                for g in (query_grad, key_grad, value_grad)
            ],
            2,
        ).reshape(reps * rows, cores * 3 * part)
        normed_one_grad = contract(mixed_grad, qkv_mine, 1, 1).astype(bf16)
        normed_one_grad = normed_one_grad.reshape(reps, rows, width)
        normed_one_grad = plane_exchange([normed_one_grad[k] for k in range(reps)])
        normed_one_grad = pair_sum([v.astype(f32) for v in normed_one_grad])
        qkv_grads = contract(normed_all, mixed_grad, 0, 0).astype(bf16)
        qkv_grads = qkv_grads.reshape(shards, shard_width, cores, 3 * part)
        qkv_grads = jnp.transpose(qkv_grads, (0, 2, 1, 3)).reshape(-1, 3 * part)
        qkv_grads = lax.psum_scatter(qkv_grads, ("fsdp", "seq"), scatter_dimension=0, tiled=True)
        qkv_grads = lax.all_gather(qkv_grads, ("rep", "seq"), axis=0)
        qkv_grads = qkv_grads.reshape(reps * cores, shard_width, 3, part)
        qkv_grads = jnp.transpose(qkv_grads, (1, 2, 0, 3)).reshape(shard_width, 3 * width)
        qkv_grads = qkv_grads.astype(f32)

        input_part, gain_one_grads, shift_one_grads = norm_pull(
            unit_one[:rows], scale_one[:rows], gain_one, normed_one_grad
        )
        input_grad = middle_grad + input_part

        mixed_sums = jnp.sum(mixed_grad.astype(f32), 0).reshape(cores, 3, part)
        qv_sums = jnp.stack([mixed_sums[:, 0].reshape(-1), mixed_sums[:, 2].reshape(-1)])
        qv_sums = lax.dynamic_update_index_in_dim(
            jnp.zeros((2, reps, rep_width), f32), qv_sums, rep, 1
        )
        fc_sums = jnp.sum(pre_grad.astype(f32), 0).reshape(shards, -1)
        fc_sums = lax.dynamic_update_index_in_dim(
            jnp.zeros((shards, reps, fc_sums.shape[1]), f32), fc_sums, rep, 1
        )
        small = [
            gain_one_grads,
            shift_one_grads,
            qv_sums,
            jnp.sum(branch_grad.astype(f32), 0),
            gain_two_grads,
            shift_two_grads,
            jnp.sum(cotangent.astype(f32), 0),
            fc_sums,
        ]
        small = jnp.concatenate([v.reshape(shards, -1) for v in small], 1)
        small = pair_sum([shard_swap(pick(small, i, 0), k) for k, i in enumerate(shard_at)])
        small = pair_sum(plane_gather(small))
        small = small + core_swap(small)
        sizes = [1, 1, 2, 1, 1, 1, 1]
        ends = [0]
        for size in sizes:
            ends.append(ends[-1] + size * shard_width)
        one = [small[a:b] for a, b in zip(ends[:-1], ends[1:])] + [small[ends[-1] :]]
        return (
            block_output,
            input_grad,
            one[0],
            one[1],
            qkv_grads,
            one[2],
            proj_grads,
            one[3],
            one[4],
            one[5],
            fc_grads,
            one[7],
            out_grads,
            one[6],
        )

    return body


def solution(mesh):
    line, block = P("fsdp"), P("fsdp", None)
    tokens = P(("rep", "fsdp", "seq"), None)
    in_specs = (
        tokens,
        line,
        line,
        block,
        line,
        block,
        line,
        line,
        line,
        block,
        line,
        block,
        line,
        tokens,
    )
    out_specs = (
        tokens,
        tokens,
        line,
        line,
        block,
        line,
        block,
        line,
        line,
        line,
        block,
        line,
        block,
        line,
    )
    body = make_body(mesh.shape["rep"], mesh.shape["fsdp"], mesh.shape["seq"])
    return jax.shard_map(body, mesh=mesh, in_specs=in_specs, out_specs=out_specs, check_vma=False)
```

```python
import math

import jax
import jax.numpy as jnp
from jax import lax
from jax.experimental import pallas as pl
from jax.experimental.pallas import tpu as pltpu
from jax.sharding import PartitionSpec as P

HEADS = 16
HEAD_DIM = 64

norm_eps = 1e-05
masked_value = -1e30
f32 = jnp.float32
bf16 = jnp.bfloat16

REPS, SHARDS, CORES = 4, 4, 2
LANE, ROWS, WIDTH, SHARD, TRIPLE, HIDDEN = 128, 128, 1024, 256, 384, 1024
SCALE = HEAD_DIM ** (-0.5)


def normalise(values):
    centre = jnp.mean(values, -1, keepdims=True)
    offsets = values - centre
    spread = jnp.mean(offsets * offsets, -1, keepdims=True)
    scale = lax.rsqrt(spread + norm_eps)
    return offsets * scale, scale


def norm_pull(unit, scale, gain, grad):
    inner = grad * gain
    first = jnp.mean(inner, -1, keepdims=True)
    second = jnp.mean(inner * unit, -1, keepdims=True)
    return scale * (inner - first - unit * second), jnp.sum(grad * unit, 0), jnp.sum(grad, 0)


def gelu_and_slope(values):
    rate = 0.7978845608028654
    squared = values * values
    bent = jnp.tanh(rate * (values + 0.044715 * values * squared))
    half = 0.5 * (1.0 + bent)
    slope = half + 0.5 * values * (1.0 - bent * bent) * (rate * (1.0 + 3.0 * 0.044715 * squared))
    return values * half, slope


def contract(left, right, left_axis, right_axis):
    return lax.dot_general(
        left, right, (((left_axis,), (right_axis,)), ((), ())), preferred_element_type=f32
    )


def swap(value, axis, size, offset):
    return lax.ppermute(value, axis, [(i, i ^ offset) for i in range(size)])


def pick(array, index, axis):
    return lax.dynamic_index_in_dim(array, index, axis, keepdims=False)


def place(pieces, positions):
    stacked = jnp.zeros((len(pieces),) + pieces[0].shape, pieces[0].dtype)
    for piece, position in zip(pieces, positions):
        stacked = lax.dynamic_update_index_in_dim(stacked, piece, position, 0)
    return stacked


def lanes(start, size):
    return pl.ds(pl.multiple_of(start, LANE), size)


def vmem_call(kernel, outs, args, hbm=(), scratch=(), flops=0):
    moved = sum(a.size * a.dtype.itemsize for a in args)
    moved += sum(math.prod(s) * jnp.dtype(t).itemsize for s, t in outs)
    whole = pl.BlockSpec(memory_space=pltpu.VMEM)
    return pl.pallas_call(
        kernel,
        out_shape=[jax.ShapeDtypeStruct(s, t) for s, t in outs],
        in_specs=[
            pl.BlockSpec(memory_space=pl.ANY) if i in hbm else whole for i in range(len(args))
        ],
        out_specs=[whole] * len(outs),
        scratch_shapes=list(scratch),
        compiler_params=pltpu.CompilerParams(vmem_limit_bytes=40 * 1024 * 1024),
        cost_estimate=pl.CostEstimate(flops=flops, bytes_accessed=moved, transcendentals=0),
    )(*args)


def mesh_place():
    return lax.axis_index("rep"), lax.axis_index("fsdp"), lax.axis_index("seq")


def total(refs, read):
    return (read(refs[0]) + read(refs[1])) + (read(refs[2]) + read(refs[3]))


def pack_kernel(qkv, vectors, packed, sems):
    rep, _, core = mesh_place()
    copies = [
        pltpu.make_async_copy(
            qkv.at[:, lanes(t * WIDTH + (rep * CORES + core) * LANE, LANE)],
            packed.at[pl.ds(0, SHARD), pl.ds(t * LANE, LANE)],
            sems.at[t],
        )
        for t in range(3)
    ]
    for copy in copies:
        copy.start()
    packed[SHARD:, :] = vectors[...]
    for copy in copies:
        copy.wait()


def unit_kernel(x0, x1, x2, x3, cot, fc, out, unit, scale, cot_copy, ff, sems):
    rep, _, core = mesh_place()
    piece = pl.ds(pl.multiple_of((rep * CORES + core) * LANE, LANE), LANE)
    copies = [
        pltpu.make_async_copy(fc.at[piece, :], ff.at[0], sems.at[0]),
        pltpu.make_async_copy(out.at[piece, :], ff.at[1], sems.at[1]),
        pltpu.make_async_copy(cot, cot_copy, sems.at[2]),
    ]
    for copy in copies:
        copy.start()
    for k, x in enumerate((x0, x1, x2, x3)):
        unit[k * ROWS : (k + 1) * ROWS, :], spread = normalise(x[...].astype(f32))
        if k == 0:
            scale[...] = jnp.broadcast_to(spread, (ROWS, LANE))
    for copy in copies:
        copy.wait()


def qkv_kernel(
    unit, p0, p1, p2, p3, f0, f1, f2, f3, qkv, kv_send, normed, weight, vectors, biases
):
    rep, shard, core = mesh_place()
    for k, (own, far) in enumerate(((p0, f0), (p1, f1), (p2, f2), (p3, f3))):
        at = pl.ds(pl.multiple_of((shard ^ k) * SHARD, SHARD), SHARD)
        weight[at, 0:TRIPLE] = own[0:SHARD, :]
        weight[at, TRIPLE : 2 * TRIPLE] = far[0:SHARD, :]
        vectors[:, at] = own[SHARD:, 0:SHARD].astype(f32)
    for p in range(CORES):
        for t, at in ((0, 0), (2, 2)):
            start = (at + rep // 2) * SHARD + (core ^ p) * LANE
            even, odd = vectors[2:3, lanes(start, LANE)], vectors[3:4, lanes(start, LANE)]
            biases[:, pl.ds(p * TRIPLE + t * LANE, LANE)] = jnp.broadcast_to(
                jnp.where(rep % 2 == 0, even, odd), (8, LANE)
            )
        biases[:, pl.ds(p * TRIPLE + LANE, LANE)] = jnp.zeros((8, LANE), f32)

    @pl.loop(0, 2)
    def _(block):
        at = pl.ds(pl.multiple_of(block * 2 * ROWS, 2 * ROWS), 2 * ROWS)
        values = (unit[at, :] * vectors[0:1, :] + vectors[1:2, :]).astype(bf16)
        normed[at, :] = values
        mixed = jnp.dot(values, weight[...], preferred_element_type=f32) + biases[0:1, :]
        mixed = mixed.astype(bf16)
        qkv[at, :] = mixed
        kv_send[at, 0 : 2 * LANE] = mixed[:, TRIPLE + LANE : 2 * TRIPLE]
        kv_send[at, 2 * LANE : 4 * LANE] = mixed[:, LANE:TRIPLE]


def dot_rows(left, right):
    return contract(left, right, 1, 1)


def head_probs(query, key_own, key_far, causal, far_seen):
    own = jnp.where(causal, dot_rows(query, key_own) * SCALE, masked_value)
    far = jnp.where(far_seen, dot_rows(query, key_far) * SCALE, masked_value)
    peak = jnp.maximum(jnp.max(own, -1, keepdims=True), jnp.max(far, -1, keepdims=True))
    own, far = jnp.exp(own - peak), jnp.exp(far - peak)
    share = 1.0 / (jnp.sum(own, -1, keepdims=True) + jnp.sum(far, -1, keepdims=True))
    return own * share, far * share


def head_masks(core):
    causal = lax.broadcasted_iota(jnp.int32, (ROWS, ROWS), 1) <= lax.broadcasted_iota(
        jnp.int32, (ROWS, ROWS), 0
    )
    far_seen = (lax.broadcasted_iota(jnp.int32, (ROWS, ROWS), 0) * 0 + core) == 1
    first = lax.broadcasted_iota(jnp.int32, (ROWS, LANE), 1) < HEAD_DIM
    return causal, far_seen, first


def attend_kernel(qkv, far, attended):
    core = lax.axis_index("seq")
    causal, far_seen, first = head_masks(core)

    @pl.loop(0, REPS)
    def _(sequence):
        at = pl.ds(pl.multiple_of(sequence * ROWS, ROWS), ROWS)
        for p in range(CORES):
            base = p * TRIPLE
            query = qkv[at, base : base + LANE]
            key_own = qkv[at, base + LANE : base + 2 * LANE]
            value_own = qkv[at, base + 2 * LANE : base + 3 * LANE]
            key_far = far[at, 2 * p * LANE : (2 * p + 1) * LANE]
            value_far = far[at, (2 * p + 1) * LANE : (2 * p + 2) * LANE]
            heads = []
            for mask in (first, ~first):
                masked = jnp.where(mask, query, jnp.zeros_like(query))
                own, other = head_probs(masked, key_own, key_far, causal, far_seen)
                heads.append(
                    jnp.dot(own.astype(bf16), value_own, preferred_element_type=f32)
                    + jnp.dot(other.astype(bf16), value_far, preferred_element_type=f32)
                )
            attended[at, p * LANE : (p + 1) * LANE] = jnp.where(first, *heads).astype(bf16)


def branch_kernel(a0, a1, a2, a3, x, proj, vectors, middle, unit, scale, normed, joined):
    rep, _, core = mesh_place()
    for k, a in enumerate((a0, a1, a2, a3)):
        for p in range(CORES):
            at = lanes(((rep ^ k) * CORES + (core ^ p)) * LANE, LANE)
            joined[:, at] = a[:, p * LANE : (p + 1) * LANE]
    branch = jnp.dot(joined[...], proj[...], preferred_element_type=f32)
    values = x[...].astype(f32) + branch + vectors[4:5, :]
    middle[...] = values
    norm, spread = normalise(values)
    unit[...] = norm
    scale[...] = jnp.broadcast_to(spread, (ROWS, LANE))
    normed[...] = (norm * vectors[5:6, :] + vectors[6:7, :]).astype(bf16)


def hidden_kernel(*refs):
    h, c, own, far = refs[0:4], refs[4:8], refs[8:12], refs[12:16]
    vectors, back, hidden, pre_grad, fc, out, h_all, c_all, bias = refs[16:]
    _, shard, core = mesh_place()
    for j, ff in enumerate((own, far)):
        for k in range(SHARDS):
            at = pl.ds((j * SHARDS + k) * LANE, LANE)
            fc[at, :] = ff[k][0]
            out[at, :] = ff[k][1]
            start = (shard ^ k) * SHARD + (core ^ j) * LANE
            bias[:, at] = jnp.broadcast_to(vectors[8:9, lanes(start, LANE)], (8, LANE))
    for k in range(REPS):
        at = pl.ds(k * ROWS, ROWS)
        h_all[at, :] = h[k][...]
        c_all[at, :] = c[k][...]

    @pl.loop(0, 2)
    def _(block):
        at = pl.ds(pl.multiple_of(block * 2 * ROWS, 2 * ROWS), 2 * ROWS)
        for n in range(HIDDEN // 256):
            tile = pl.ds(n * 256, 256)
            preact = dot_rows(h_all[at, :], fc[tile, :]) + bias[0:1, tile]
            value, slope = gelu_and_slope(preact)
            hidden[at, tile] = value.astype(bf16)
            grad = dot_rows(c_all[at, :], out[tile, :])
            pre_grad[at, tile] = (grad * slope).astype(bf16)
        back[at, :] = jnp.dot(pre_grad[at, :], fc[...], preferred_element_type=f32).astype(bf16)


def weights_kernel(hidden, pre_grad, h_all, c_all, out, output, own, far, sums):
    @pl.loop(0, 2)
    def _(block):
        at = pl.ds(pl.multiple_of(block * 2 * ROWS, 2 * ROWS), 2 * ROWS)
        output[at, :] = jnp.dot(hidden[at, :], out[...], preferred_element_type=f32).astype(bf16)

    sums[...] = jnp.broadcast_to(
        jnp.sum(pre_grad[...].astype(f32), 0, keepdims=True), sums.shape
    )
    for j, grads in enumerate((own, far)):
        for k in range(0, SHARDS, 2):
            tile = pl.ds((j * SHARDS + k) * LANE, 2 * LANE)
            for i, (left, right) in enumerate(((pre_grad, h_all), (hidden, c_all))):
                grad = contract(left[:, tile], right[...], 0, 0).astype(bf16)
                grads[k, i] = grad[0:LANE]
                grads[k + 1, i] = grad[LANE:]


def middle_kernel(
    g0, g1, g2, g3, unit, scale, vectors, cot, proj, middle_grad, o0, o1, o2, o3, sums, low, back
):
    rep, _, core = mesh_place()
    grad = total((g0, g1, g2, g3), lambda g: g[...].astype(f32))
    part, gain, shift = norm_pull(unit[...], scale[:, 0:1], vectors[5:6, :], grad)
    cots = cot[...].astype(f32)
    values = cots + part
    middle_grad[...] = values
    branch = values.astype(bf16)
    low[...] = branch
    back[...] = dot_rows(branch, proj[...]).astype(bf16)
    rows = [jnp.sum(branch.astype(f32), 0), gain, shift, jnp.sum(cots, 0)]
    for i, row in enumerate(rows):
        sums[i : i + 1, :] = row[None]
    sums[4:8, :] = jnp.zeros((4, WIDTH), f32)
    for k, o in enumerate((o0, o1, o2, o3)):
        for p in range(CORES):
            at = lanes(((rep ^ k) * CORES + (core ^ p)) * LANE, LANE)
            o[:, p * LANE : (p + 1) * LANE] = back[:, at]
        o[:, SHARD : 2 * SHARD] = low[:, lanes((rep ^ k) * SHARD, SHARD)]


def proj_grad_kernel(attended, b0, b1, b2, b3, grads, cols):
    rep, _, core = mesh_place()
    for k, b in enumerate((b0, b1, b2, b3)):
        cols[k * ROWS : (k + 1) * ROWS, :] = b[:, SHARD : 2 * SHARD]
    for a in range(REPS):
        blocks = [
            cols[pl.ds(pl.multiple_of((a ^ j ^ rep) * ROWS, ROWS), ROWS), :] for j in range(REPS)
        ]
        grad = contract(attended[a], jnp.concatenate(blocks, 0), 0, 0).astype(bf16)
        for p in range(CORES):
            for j in range(CORES):
                start = (a * CORES + j) * SHARD + (core ^ p) * LANE
                grads[pl.ds(pl.multiple_of(start, LANE), LANE), :] = grad[
                    p * LANE : (p + 1) * LANE, j * LANE : (j + 1) * LANE
                ]


def attend_back_kernel(qkv, far, b0, b1, b2, b3, query_grad, own_grad, far_grad, grads):
    core = lax.axis_index("seq")
    causal, far_seen, first = head_masks(core)
    for k, b in enumerate((b0, b1, b2, b3)):
        grads[k * ROWS : (k + 1) * ROWS, :] = b[:, 0 : 2 * LANE]

    @pl.loop(0, REPS)
    def _(sequence):
        at = pl.ds(pl.multiple_of(sequence * ROWS, ROWS), ROWS)
        for p in range(CORES):
            base = p * TRIPLE
            query = qkv[at, base : base + LANE]
            key_own = qkv[at, base + LANE : base + 2 * LANE]
            value_own = qkv[at, base + 2 * LANE : base + 3 * LANE]
            key_far = far[at, 2 * p * LANE : (2 * p + 1) * LANE]
            value_far = far[at, (2 * p + 1) * LANE : (2 * p + 2) * LANE]
            grad = grads[at, p * LANE : (p + 1) * LANE]
            queries, sums = [], [0.0] * 4
            for mask in (first, ~first):
                masked = jnp.where(mask, query, jnp.zeros_like(query))
                back = jnp.where(mask, grad, jnp.zeros_like(grad))
                own, other = head_probs(masked, key_own, key_far, causal, far_seen)
                own_back, other_back = dot_rows(back, value_own), dot_rows(back, value_far)
                row = jnp.sum(own * own_back, -1, keepdims=True) + jnp.sum(
                    other * other_back, -1, keepdims=True
                )
                own_score = (own * (own_back - row)).astype(bf16)
                other_score = (other * (other_back - row)).astype(bf16)
                queries.append(
                    jnp.dot(own_score, key_own, preferred_element_type=f32)
                    + jnp.dot(other_score, key_far, preferred_element_type=f32)
                )
                parts = [
                    contract(own_score, masked, 0, 0) * SCALE,
                    contract(own.astype(bf16), back, 0, 0),
                    contract(other_score, masked, 0, 0) * SCALE,
                    contract(other.astype(bf16), back, 0, 0),
                ]
                sums = [a + b for a, b in zip(sums, parts)]
            query_grad[at, p * LANE : (p + 1) * LANE] = (
                jnp.where(first, *queries) * SCALE
            ).astype(bf16)
            own_at = slice(2 * p * LANE, (2 * p + 1) * LANE)
            own_grad[at, own_at] = sums[0]
            own_grad[at, (2 * p + 1) * LANE : (2 * p + 2) * LANE] = sums[1]
            q = 1 - p
            far_grad[at, 2 * q * LANE : (2 * q + 1) * LANE] = sums[2].astype(bf16)
            far_grad[at, (2 * q + 1) * LANE : (2 * q + 2) * LANE] = sums[3].astype(bf16)


def qkv_back_kernel(
    query_grad, own_grad, far_grad, weight, normed, unit, ff_sums, mid_sums, own, far, joined, small, mixed, sums
):
    rep, shard, core = mesh_place()
    for p in range(CORES):
        base = p * TRIPLE
        mixed[:, base : base + LANE] = query_grad[:, p * LANE : (p + 1) * LANE]
        at = slice(2 * p * LANE, (2 * p + 2) * LANE)
        mixed[:, base + LANE : base + 3 * LANE] = (
            own_grad[:, at] + far_grad[:, at].astype(f32)
        ).astype(bf16)
    for k in range(SHARDS):
        at = lanes((shard ^ k) * SHARD, SHARD)
        grad = contract(normed[:, at], mixed[...], 0, 0).astype(bf16)
        own[k] = grad[:, 0:TRIPLE]
        far[k] = grad[:, TRIPLE:]
    gain = jnp.zeros((1, WIDTH), f32)
    shift = jnp.zeros((1, WIDTH), f32)
    for k in range(REPS):
        at = pl.ds(k * ROWS, ROWS)
        back = dot_rows(mixed[at, :], weight[...])
        joined[at, :] = back.astype(bf16)
        gain = gain + jnp.sum(back * unit[at, :], 0, keepdims=True)
        shift = shift + jnp.sum(back, 0, keepdims=True)
    sums[0:1, :] = gain
    sums[1:2, :] = shift
    mixed_sums = jnp.sum(mixed[...].astype(f32), 0, keepdims=True)
    for p in range(CORES):
        for i in range(2):
            start = i * SHARD + (core ^ p) * LANE
            sums[2:3, lanes(start, LANE)] = mixed_sums[
                :, p * TRIPLE + 2 * i * LANE : p * TRIPLE + (2 * i + 1) * LANE
            ]
    for k in range(SHARDS):
        small[k] = jnp.zeros(small.shape[1:], f32)
        at = lanes((shard ^ k) * SHARD, SHARD)
        small[k, 0:1, 0:SHARD] = sums[0:1, at]
        small[k, 1:2, 0:SHARD] = sums[1:2, at]
        queries = jnp.where((shard ^ k) == rep // 2, sums[2:3, 0:SHARD], 0.0)
        values = jnp.where((shard ^ k) == 2 + rep // 2, sums[2:3, SHARD : 2 * SHARD], 0.0)
        small[k, 2:3, 0:SHARD] = jnp.where(rep % 2 == 0, queries + values, 0.0)
        small[k, 3:4, 0:SHARD] = jnp.where(rep % 2 == 1, queries + values, 0.0)
        for i in range(4):
            small[k, 4 + i : 5 + i, 0:SHARD] = mid_sums[i : i + 1, at]
        for j in range(CORES):
            part = ff_sums[:, (j * SHARDS + k) * LANE : (j * SHARDS + k + 1) * LANE]
            row = lax.broadcasted_iota(jnp.int32, part.shape, 0)
            small[k, 8:16, lanes((core ^ j) * LANE, LANE)] = jnp.where(row == rep, part, 0.0)


def tail_kernel(own, far, small, o0, o1, o2, o3):
    for k, o in enumerate((o0, o1, o2, o3)):
        o[0:SHARD, :] = (own[k].astype(f32) + far[k].astype(f32)).astype(bf16)
        o[SHARD:, :] = small[k].astype(bf16)


def gather_tail_kernel(p0, p1, p2, p3, proj, o):
    o[:, 0:TRIPLE] = total((p0, p1, p2, p3), lambda p: p[...].astype(f32)).astype(bf16)
    o[0:SHARD, TRIPLE:] = proj[...]
    o[SHARD:, TRIPLE:] = jnp.zeros((o.shape[0] - SHARD, LANE), bf16)


def input_kernel(j0, j1, j2, j3, r0, r1, r2, r3, unit, scale, vectors, middle_grad, middle, block, grad):
    back = total((j0, j1, j2, j3), lambda g: g[...].astype(f32))
    output = total((r0, r1, r2, r3), lambda g: g[...].astype(f32))
    block[...] = (middle[...] + output + vectors[7:8, :]).astype(bf16)
    part, _, _ = norm_pull(unit[0:ROWS, :], scale[:, 0:1], vectors[0:1, :], back)
    grad[...] = middle_grad[...] + part


def final_kernel(p0, p1, p2, p3, f0, f1, f2, f3, qkv, proj, small):
    rep, _, core = mesh_place()
    for k, pair in enumerate(((p0, f0), (p1, f1), (p2, f2), (p3, f3))):
        for j, piece in enumerate(pair):
            start = ((rep ^ k) * CORES + (core ^ j)) * LANE
            for t in range(3):
                qkv[:, lanes(t * WIDTH + start, LANE)] = piece[
                    0:SHARD, t * LANE : (t + 1) * LANE
                ].astype(f32)
            proj[:, lanes(start, LANE)] = piece[0:SHARD, TRIPLE:].astype(f32)

    def read(pair):
        return pair[0][SHARD:, 0:SHARD].astype(f32) + pair[1][SHARD:, 0:SHARD].astype(f32)

    small[...] = total(((p0, f0), (p1, f1), (p2, f2), (p3, f3)), read)


def spread_kernel(p0, p1, p2, p3, f0, f1, f2, f3, fc, out):
    rep, _, core = mesh_place()
    for k, pair in enumerate(((p0, f0), (p1, f1), (p2, f2), (p3, f3))):
        for j, piece in enumerate(pair):
            at = pl.ds(pl.multiple_of(((rep ^ k) * CORES + (core ^ j)) * LANE, LANE), LANE)
            fc[at, :] = piece[0].astype(f32)
            out[at, :] = piece[1].astype(f32)


def add_kernel(own, far, o0, o1, o2, o3):
    for k, o in enumerate((o0, o1, o2, o3)):
        o[...] = (own[k].astype(f32) + far[k].astype(f32)).astype(bf16)


def sum_kernel(p0, p1, p2, p3, o):
    o[...] = total((p0, p1, p2, p3), lambda p: p[...].astype(f32)).astype(bf16)


def tiled_body(
    block_input,
    ln1_gain,
    ln1_shift,
    qkv_weight,
    qv_bias,
    proj_weight,
    proj_bias,
    ln2_gain,
    ln2_shift,
    fc_weight,
    fc_bias,
    out_weight,
    out_bias,
    cotangent,
):
    rep, _, core = mesh_place()

    def over_rep(pieces):
        return [swap(p, "rep", REPS, k) if k else p for k, p in enumerate(pieces)]

    def over_shards(pieces):
        return [swap(p, "fsdp", SHARDS, k) if k else p for k, p in enumerate(pieces)]

    def over_cores(value):
        return swap(value, "seq", CORES, 1)

    all_rows = REPS * ROWS
    fc_bias_part = pick(fc_bias.reshape(REPS, -1), rep, 0)
    vectors = [
        ln1_gain,
        ln1_shift,
        qv_bias[:SHARD],
        qv_bias[SHARD:],
        proj_bias,
        ln2_gain,
        ln2_shift,
        out_bias,
        fc_bias_part,
    ]
    vectors = jnp.stack(vectors + [jnp.zeros_like(ln1_gain)] * (16 - len(vectors)))
    vectors = jnp.pad(vectors, ((0, 0), (0, TRIPLE - SHARD)))
    (packed,) = vmem_call(
        pack_kernel,
        [((SHARD + 16, TRIPLE), bf16)],
        [qkv_weight, vectors],
        hbm=(0,),
        scratch=[pltpu.SemaphoreType.DMA((3,))],
    )
    own_packed = over_shards([packed] * SHARDS)
    far_packed = [over_cores(p) for p in own_packed]
    inputs = over_rep([block_input] * REPS)

    proj_part = pick(proj_weight.reshape(REPS * CORES, -1, WIDTH), rep * CORES + core, 0)
    proj_full = lax.all_gather(proj_part, "fsdp", axis=0)
    proj_full = lax.all_gather(proj_full, ("rep", "seq"), axis=1)
    proj_full = proj_full.reshape(WIDTH, WIDTH)

    unit_one, scale_one, own_cot, ff = vmem_call(
        unit_kernel,
        [
            ((all_rows, WIDTH), f32),
            ((ROWS, LANE), f32),
            ((ROWS, WIDTH), bf16),
            ((2, LANE, WIDTH), bf16),
        ],
        inputs + [cotangent, fc_weight, out_weight],
        hbm=(4, 5, 6),
        scratch=[pltpu.SemaphoreType.DMA((3,))],
    )
    cots = over_rep([own_cot] * REPS)
    own_ff = over_shards([ff] * SHARDS)
    far_ff = [over_cores(f) for f in own_ff]

    qkv, kv_send, normed_one, qkv_mine, vectors = vmem_call(
        qkv_kernel,
        [
            ((all_rows, 2 * TRIPLE), bf16),
            ((all_rows, 4 * LANE), bf16),
            ((all_rows, WIDTH), bf16),
            ((WIDTH, 2 * TRIPLE), bf16),
            ((16, WIDTH), f32),
        ],
        [unit_one] + own_packed + far_packed,
        scratch=[pltpu.VMEM((8, 2 * TRIPLE), f32)],
        flops=2 * all_rows * WIDTH * 2 * TRIPLE,
    )
    kv_far = over_cores(kv_send)
    (attended,) = vmem_call(
        attend_kernel,
        [((all_rows, SHARD), bf16)],
        [qkv, kv_far],
        flops=4 * all_rows * 2 * ROWS * SHARD,
    )
    mine = over_rep([attended[k * ROWS : (k + 1) * ROWS] for k in range(REPS)])
    middle, unit_two, scale_two, normed_two = vmem_call(
        branch_kernel,
        [
            ((ROWS, WIDTH), f32),
            ((ROWS, WIDTH), f32),
            ((ROWS, LANE), f32),
            ((ROWS, WIDTH), bf16),
        ],
        mine + [block_input, proj_full, vectors],
        scratch=[pltpu.VMEM((ROWS, WIDTH), bf16)],
        flops=2 * ROWS * WIDTH * WIDTH,
    )
    normed_two = over_rep([normed_two] * REPS)
    attended_all = lax.all_gather(attended, "rep", axis=0)

    back, hidden, pre_grad, _, out_mine, h_all, c_all, _ = vmem_call(
        hidden_kernel,
        [
            ((all_rows, WIDTH), bf16),
            ((all_rows, HIDDEN), bf16),
            ((all_rows, HIDDEN), bf16),
            ((HIDDEN, WIDTH), bf16),
            ((HIDDEN, WIDTH), bf16),
            ((all_rows, WIDTH), bf16),
            ((all_rows, WIDTH), bf16),
            ((8, HIDDEN), f32),
        ],
        normed_two + cots + own_ff + far_ff + [vectors],
        flops=6 * all_rows * WIDTH * HIDDEN,
    )
    back = over_rep([back[k * ROWS : (k + 1) * ROWS] for k in range(REPS)])
    output, ff_own, ff_far, ff_sums = vmem_call(
        weights_kernel,
        [
            ((all_rows, WIDTH), bf16),
            ((SHARDS, 2, LANE, WIDTH), bf16),
            ((SHARDS, 2, LANE, WIDTH), bf16),
            ((8, HIDDEN), f32),
        ],
        [hidden, pre_grad, h_all, c_all, out_mine],
        flops=6 * all_rows * WIDTH * HIDDEN,
    )
    piece = ((2, LANE, WIDTH), bf16)
    ff_pieces = vmem_call(add_kernel, [piece] * SHARDS, [ff_own, over_cores(ff_far)])
    (ff_piece,) = vmem_call(sum_kernel, [piece], over_shards(ff_pieces))
    ff_pieces = over_rep([ff_piece] * REPS)
    fc_grads, out_grads = vmem_call(
        spread_kernel,
        [((2 * REPS * LANE, WIDTH), f32)] * 2,
        ff_pieces + [over_cores(p) for p in ff_pieces],
    )

    middle_grad, o0, o1, o2, o3, mid_sums = vmem_call(
        middle_kernel,
        [((ROWS, WIDTH), f32)] + [((ROWS, 2 * SHARD), bf16)] * REPS + [((8, WIDTH), f32)],
        back + [unit_two, scale_two, vectors, cotangent, proj_full],
        scratch=[pltpu.VMEM((ROWS, WIDTH), bf16)] * 2,
        flops=2 * ROWS * WIDTH * WIDTH,
    )
    pairs = over_rep([o0, o1, o2, o3])
    query_grad, own_grad, far_grad = vmem_call(
        attend_back_kernel,
        [
            ((all_rows, SHARD), bf16),
            ((all_rows, 4 * LANE), f32),
            ((all_rows, 4 * LANE), bf16),
        ],
        [qkv, kv_far] + pairs,
        scratch=[pltpu.VMEM((all_rows, SHARD), bf16)],
        flops=10 * all_rows * 2 * ROWS * SHARD,
    )
    (proj_grads,) = vmem_call(
        proj_grad_kernel,
        [((WIDTH * CORES, LANE), bf16)],
        [attended_all] + pairs,
        scratch=[pltpu.VMEM((all_rows, SHARD), bf16)],
        flops=2 * all_rows * WIDTH * SHARD,
    )
    proj_grads = lax.psum_scatter(proj_grads, ("fsdp", "seq"), scatter_dimension=0, tiled=True)

    qkv_own, qkv_far, joined, small = vmem_call(
        qkv_back_kernel,
        [
            ((SHARDS, SHARD, TRIPLE), bf16),
            ((SHARDS, SHARD, TRIPLE), bf16),
            ((all_rows, WIDTH), bf16),
            ((SHARDS, 16, TRIPLE), f32),
        ],
        [query_grad, own_grad, over_cores(far_grad), qkv_mine, normed_one, unit_one, ff_sums, mid_sums],
        scratch=[pltpu.VMEM((all_rows, 2 * TRIPLE), bf16), pltpu.VMEM((8, WIDTH), f32)],
        flops=4 * all_rows * WIDTH * 2 * TRIPLE,
    )
    tail = vmem_call(
        tail_kernel,
        [((SHARD + 16, TRIPLE), bf16)] * SHARDS,
        [qkv_own, over_cores(qkv_far), small],
    )
    (tail,) = vmem_call(
        gather_tail_kernel,
        [((SHARD + 16, TRIPLE + LANE), bf16)],
        over_shards(tail) + [proj_grads],
    )
    tail = over_rep([tail] * REPS)
    qkv_grads, proj_grads, small = vmem_call(
        final_kernel,
        [((SHARD, 3 * WIDTH), f32), ((SHARD, WIDTH), f32), ((16, SHARD), f32)],
        tail + [over_cores(t) for t in tail],
    )
    joined = over_rep([joined[k * ROWS : (k + 1) * ROWS] for k in range(REPS)])
    output = over_rep([output[k * ROWS : (k + 1) * ROWS] for k in range(REPS)])
    block_output, input_grad = vmem_call(
        input_kernel,
        [((ROWS, WIDTH), bf16), ((ROWS, WIDTH), f32)],
        joined + output + [unit_one, scale_one, vectors, middle_grad, middle],
    )
    return (
        block_output,
        input_grad,
        small[0],
        small[1],
        qkv_grads,
        small[2:4].reshape(-1),
        proj_grads,
        small[4],
        small[5],
        small[6],
        fc_grads,
        small[8:12].reshape(-1),
        out_grads,
        small[7],
    )


def make_body(reps, shards, cores):
    def rep_swap(value, offset):
        return swap(value, "rep", reps, offset) if offset else value

    def shard_swap(value, offset):
        return swap(value, "fsdp", shards, offset) if offset else value

    def core_swap(value):
        return swap(value, "seq", cores, 1)

    def plane_gather(value):
        return [rep_swap(value, k) for k in range(reps)]

    def plane_exchange(pieces):
        return [rep_swap(piece, k) for k, piece in enumerate(pieces)]

    def pair_sum(pieces):
        while len(pieces) > 1:
            pieces = [pieces[i] + pieces[i + 1] for i in range(0, len(pieces), 2)]
        return pieces[0]

    def own_scatter(parts):
        core = lax.axis_index("seq")
        shard = lax.axis_index("fsdp")
        kept = pick(parts, core, 1).astype(f32)
        kept = (kept + core_swap(pick(parts, 1 - core, 1)).astype(f32)).astype(bf16)
        pieces = [shard_swap(pick(kept, shard ^ k, 0), k).astype(f32) for k in range(shards)]
        return pair_sum(pieces).astype(bf16)

    def place_both(pieces):
        core = lax.axis_index("seq")
        rep = lax.axis_index("rep")
        held = jnp.zeros((reps, cores) + pieces[0].shape, pieces[0].dtype)
        zeros = (0,) * pieces[0].ndim
        for k, piece in enumerate(pieces):
            held = lax.dynamic_update_slice(held, piece[None, None], (rep ^ k, core) + zeros)
            far = core_swap(piece)
            held = lax.dynamic_update_slice(held, far[None, None], (rep ^ k, 1 - core) + zeros)
        return held

    def body(
        block_input,
        ln1_gain,
        ln1_shift,
        qkv_weight,
        qv_bias,
        proj_weight,
        proj_bias,
        ln2_gain,
        ln2_shift,
        fc_weight,
        fc_bias,
        out_weight,
        out_bias,
        cotangent,
    ):
        rows, width = block_input.shape
        shard_width = width // shards
        part = width // (reps * cores)
        rep_width = part * cores
        hidden_part = fc_weight.shape[0] // (reps * cores)
        head_scale = HEAD_DIM ** (-0.5)
        rep = lax.axis_index("rep")
        shard = lax.axis_index("fsdp")
        core = lax.axis_index("seq")
        rep_at = [rep ^ k for k in range(reps)]
        shard_at = [shard ^ k for k in range(shards)]

        columns = qkv_weight.reshape(shard_width, 3, reps, cores, part)
        columns = pick(pick(columns, rep, 2), core, 2).reshape(shard_width, 3 * part)
        fc_bias_part = pick(fc_bias.reshape(reps, -1), rep, 0)
        vectors = [
            ln1_gain,
            ln1_shift,
            qv_bias[:shard_width],
            qv_bias[shard_width:],
            proj_bias,
            ln2_gain,
            ln2_shift,
            out_bias,
            fc_bias_part,
        ]
        vectors = [jnp.pad(v, (0, 3 * part - v.shape[0])) for v in vectors]
        vectors = jnp.stack(vectors + [jnp.zeros_like(vectors[0])] * (16 - len(vectors)))
        packed = jnp.concatenate([columns, vectors], 0)
        packed, own_rows = lax.optimization_barrier((packed, block_input))
        packed = place([shard_swap(packed, k) for k in range(shards)], shard_at)
        inputs_all = jnp.concatenate(plane_gather(own_rows), 0)
        columns = packed[:, :shard_width].reshape(width, 3 * part)
        vectors = packed[:, shard_width:, :].astype(f32)

        def vector(index, size):
            return vectors[:, index, :size].reshape(-1)

        gain_one, shift_one = vector(0, shard_width), vector(1, shard_width)
        qv_full = jnp.stack([vectors[:, 2, :shard_width], vectors[:, 3, :shard_width]], 1)
        qv_full = qv_full.reshape(2, reps, cores * part)
        proj_bias_full = vector(4, shard_width)
        gain_two, shift_two = vector(5, shard_width), vector(6, shard_width)
        out_bias_full = vector(7, shard_width)
        fc_bias_mine = vector(8, fc_bias_part.shape[0])
        qkv_mine = place([columns, core_swap(columns)], [core, 1 - core])
        qkv_mine = jnp.transpose(qkv_mine, (1, 0, 2)).reshape(width, cores * 3 * part)

        proj_part = pick(proj_weight.reshape(reps * cores, -1, width), rep * cores + core, 0)
        proj_full = lax.all_gather(proj_part, ("rep", "fsdp", "seq"), axis=0)
        proj_full = proj_full.reshape((reps, shards, cores) + proj_part.shape)
        proj_full = jnp.transpose(proj_full, (1, 0, 2, 3, 4)).reshape(width, width)

        fc_part = pick(fc_weight.reshape(reps * cores, hidden_part, width), rep * cores + core, 0)
        out_part = pick(out_weight.reshape(reps * cores, hidden_part, width), rep * cores + core, 0)
        both_part = jnp.stack([fc_part, out_part])
        both_part, packed = lax.optimization_barrier((both_part, packed))
        both = place([shard_swap(both_part, k) for k in range(shards)], shard_at)
        both = place([both, core_swap(both)], [core, 1 - core])
        fc_mine = jnp.transpose(both[:, :, 0], (1, 0, 2, 3)).reshape(-1, width)
        out_mine = jnp.transpose(both[:, :, 1], (1, 0, 2, 3)).reshape(-1, width)

        own_cot, inputs_all = lax.optimization_barrier((cotangent, inputs_all))
        cot_all = jnp.concatenate(plane_gather(own_cot), 0)

        unit_one, scale_one = normalise(inputs_all.astype(f32))
        normed_all = (unit_one * gain_one + shift_one).astype(bf16)
        mixed = jnp.dot(normed_all, qkv_mine, preferred_element_type=f32)
        mixed = mixed.reshape(reps, rows, cores, 3, part)
        qv_mine = pick(qv_full, rep, 1).reshape(2, cores, part)
        heads = (reps, rows, rep_width // HEAD_DIM, HEAD_DIM)
        queries = (mixed[:, :, :, 0] + qv_mine[0]).astype(bf16).reshape(heads)
        keys = mixed[:, :, :, 1].astype(bf16).reshape(heads)
        values = (mixed[:, :, :, 2] + qv_mine[1]).astype(bf16).reshape(heads)
        far_pair = core_swap(jnp.stack([keys, values]))
        keys_both = jnp.concatenate([keys, far_pair[0]], 1)
        values_both = jnp.concatenate([values, far_pair[1]], 1)

        row_pos = lax.broadcasted_iota(jnp.int32, (rows, 2 * rows), 0)
        col_pos = lax.broadcasted_iota(jnp.int32, (rows, 2 * rows), 1)
        allowed = jnp.where(col_pos < rows, col_pos <= row_pos, core == 1)
        scores = jnp.einsum("sqhd,skhd->shqk", queries, keys_both, preferred_element_type=f32)
        scores = jnp.where(allowed, scores * head_scale, masked_value)
        peak = jnp.max(scores, -1, keepdims=True)
        powers = jnp.exp(scores - peak)
        probs = powers / jnp.sum(powers, -1, keepdims=True)
        probs_low = probs.astype(bf16)
        attended = jnp.einsum("shqk,skhd->sqhd", probs_low, values_both, preferred_element_type=f32)
        attended_low = attended.astype(bf16).reshape(reps, rows, rep_width)
        mine = place(plane_exchange([attended_low[k] for k in range(reps)]), rep_at)
        mine = jnp.transpose(mine, (1, 0, 2)).reshape(rows, width)
        middle = (
            block_input.astype(f32)
            + jnp.dot(mine, proj_full, preferred_element_type=f32)
            + proj_bias_full
        )
        unit_two, scale_two = normalise(middle)
        normed_two = (unit_two * gain_two + shift_two).astype(bf16)
        normed_two_all = jnp.concatenate(plane_gather(normed_two), 0)

        attended_all = place([attended_low[k] for k in range(reps)], rep_at)
        attended_all = lax.all_gather(attended_all.reshape(reps * rows, rep_width), "rep", axis=0)
        attended_all = jnp.transpose(attended_all, (1, 0, 2)).reshape(reps * rows, width)

        hidden_grad = contract(cot_all, out_mine, 1, 1)
        preact = contract(normed_two_all, fc_mine, 1, 1) + fc_bias_mine
        hidden, slope = gelu_and_slope(preact)
        hidden_low = hidden.astype(bf16)
        pre_grad = (hidden_grad * slope).astype(bf16)
        normed_grad = jnp.dot(pre_grad, fc_mine, preferred_element_type=f32).astype(bf16)
        normed_grad = normed_grad.reshape(reps, rows, width)
        normed_grad = plane_exchange([normed_grad[k] for k in range(reps)])
        normed_grad = pair_sum([v.astype(f32) for v in normed_grad])
        output = jnp.dot(hidden_low, out_mine, preferred_element_type=f32).astype(bf16)
        output, normed_grad = lax.optimization_barrier((output, normed_grad))
        output = output.reshape(reps, rows, width)
        output = plane_exchange([output[k] for k in range(reps)])
        output = pair_sum([v.astype(f32) for v in output])
        block_output = (middle + output + out_bias_full).astype(bf16)

        out_grads = contract(hidden_low, cot_all, 0, 0).astype(bf16)
        out_grads = lax.psum_scatter(out_grads, ("fsdp", "seq"), scatter_dimension=0, tiled=True)
        fc_grads = contract(pre_grad, normed_two_all, 0, 0).astype(bf16)
        fc_grads = own_scatter(fc_grads.reshape(shards, cores, hidden_part, width))
        ff_grads = plane_gather(jnp.stack([fc_grads, out_grads]))
        ff_grads = place_both(ff_grads)
        fc_grads = ff_grads[:, :, 0].reshape(-1, width).astype(f32)
        out_grads = ff_grads[:, :, 1].reshape(-1, width).astype(f32)

        middle_part, gain_two_grads, shift_two_grads = norm_pull(
            unit_two, scale_two, gain_two, normed_grad
        )
        middle_grad = cotangent.astype(f32) + middle_part
        branch_grad = middle_grad.astype(bf16)
        attended_grad = contract(branch_grad, proj_full, 1, 1).astype(bf16)
        pair = [v.reshape(rows, reps, rep_width) for v in (attended_grad, branch_grad)]
        pair = jnp.concatenate(pair, 2)
        pair = plane_exchange([pick(pair, i, 1) for i in rep_at])
        attended_grad = jnp.stack([v[:, :rep_width] for v in pair]).reshape(heads)
        branch_cols = place([v[:, rep_width:] for v in pair], rep_at).reshape(-1, rep_width)
        proj_grads = contract(attended_all, branch_cols, 0, 0).astype(bf16)
        proj_grads = proj_grads.reshape(shards, shard_width, cores, part)
        proj_grads = jnp.transpose(proj_grads, (0, 2, 1, 3)).reshape(-1, part)
        proj_grads = lax.psum_scatter(proj_grads, ("fsdp", "seq"), scatter_dimension=0, tiled=True)
        proj_grads = lax.all_gather(proj_grads, ("rep", "seq"), axis=0)
        proj_grads = jnp.transpose(proj_grads, (1, 0, 2)).reshape(shard_width, width).astype(f32)

        prob_grad = jnp.einsum("sqhd,skhd->shqk", attended_grad, values_both, preferred_element_type=f32)
        row_total = jnp.sum(probs * prob_grad, -1, keepdims=True)
        score_low = (probs * (prob_grad - row_total)).astype(bf16)
        query_grad = (
            jnp.einsum("shqk,skhd->sqhd", score_low, keys_both, preferred_element_type=f32)
            * head_scale
        )
        key_grad = (
            jnp.einsum("shqk,sqhd->skhd", score_low, queries, preferred_element_type=f32)
            * head_scale
        )
        value_grad = jnp.einsum("shqk,sqhd->skhd", probs_low, attended_grad, preferred_element_type=f32)
        far_grads = core_swap(jnp.stack([key_grad[:, rows:], value_grad[:, rows:]]).astype(bf16))
        key_grad = key_grad[:, :rows] + far_grads[0].astype(f32)
        value_grad = value_grad[:, :rows] + far_grads[1].astype(f32)
        mixed_grad = jnp.stack(
            [
                g.astype(bf16).reshape(reps * rows, cores, part)
                for g in (query_grad, key_grad, value_grad)
            ],
            2,
        ).reshape(reps * rows, cores * 3 * part)
        qkv_grads = contract(normed_all, mixed_grad, 0, 0).astype(bf16)
        normed_one_grad = contract(mixed_grad, qkv_mine, 1, 1)
        joined = normed_one_grad.astype(bf16).reshape(reps, rows, width)
        joined = plane_exchange([joined[k] for k in range(reps)])
        joined = pair_sum([v.astype(f32) for v in joined])
        input_part = norm_pull(unit_one[:rows], scale_one[:rows], gain_one, joined)[0]
        input_grad = middle_grad + input_part

        gain_one_grads = jnp.sum(normed_one_grad * unit_one, 0)
        shift_one_grads = jnp.sum(normed_one_grad, 0)
        mixed_sums = jnp.sum(mixed_grad.astype(f32), 0).reshape(cores, 3, part)
        qv_sums = jnp.stack([mixed_sums[:, 0].reshape(-1), mixed_sums[:, 2].reshape(-1)])
        qv_sums = lax.dynamic_update_index_in_dim(
            jnp.zeros((2, reps, rep_width), f32), qv_sums, rep, 1
        )
        fc_sums = jnp.sum(pre_grad.astype(f32), 0).reshape(shards, -1)
        fc_sums = lax.dynamic_update_index_in_dim(
            jnp.zeros((shards, reps, fc_sums.shape[1]), f32), fc_sums, rep, 1
        )
        small = [
            gain_one_grads,
            shift_one_grads,
            qv_sums,
            jnp.sum(branch_grad.astype(f32), 0),
            gain_two_grads,
            shift_two_grads,
            jnp.sum(cotangent.astype(f32), 0),
            fc_sums,
        ]
        small = jnp.concatenate([v.reshape(shards, -1) for v in small], 1).astype(bf16)
        small_size = small.shape[1]
        small_rows = -(-small_size // (16 * 3 * part)) * 16
        small = jnp.pad(small, ((0, 0), (0, small_rows * 3 * part - small_size)))
        small = small.reshape(shards, small_rows, 3 * part)

        qkv_grads = qkv_grads.reshape(shards, shard_width, cores, 3 * part)
        tail = pick(qkv_grads, core, 2).astype(f32)
        tail = (tail + core_swap(pick(qkv_grads, 1 - core, 2)).astype(f32)).astype(bf16)
        tail = jnp.concatenate([tail, small], 1)
        tail = [shard_swap(pick(tail, i, 0), k).astype(f32) for k, i in enumerate(shard_at)]
        tail = place_both(plane_gather(pair_sum(tail).astype(bf16)))
        qkv_grads = tail[:, :, :shard_width].reshape(reps * cores, shard_width, 3, part)
        qkv_grads = jnp.transpose(qkv_grads, (1, 2, 0, 3)).reshape(shard_width, 3 * width)
        qkv_grads = qkv_grads.astype(f32)
        small = jnp.sum(tail[:, :, shard_width:].astype(f32), (0, 1)).reshape(-1)
        sizes = [1, 1, 2, 1, 1, 1, 1]
        ends = [0]
        for size in sizes:
            ends.append(ends[-1] + size * shard_width)
        one = [small[a:b] for a, b in zip(ends[:-1], ends[1:])] + [small[ends[-1] : small_size]]
        return (
            block_output,
            input_grad,
            one[0],
            one[1],
            qkv_grads,
            one[2],
            proj_grads,
            one[3],
            one[4],
            one[5],
            fc_grads,
            one[7],
            out_grads,
            one[6],
        )

    return body


def solution(mesh):
    line, block = P("fsdp"), P("fsdp", None)
    tokens = P(("rep", "fsdp", "seq"), None)
    in_specs = (
        tokens,
        line,
        line,
        block,
        line,
        block,
        line,
        line,
        line,
        block,
        line,
        block,
        line,
        tokens,
    )
    out_specs = (
        tokens,
        tokens,
        line,
        line,
        block,
        line,
        block,
        line,
        line,
        line,
        block,
        line,
        block,
        line,
    )
    sizes = mesh.shape["rep"], mesh.shape["fsdp"], mesh.shape["seq"]
    general = make_body(*sizes)

    def body(*args):
        tiled = sizes == (REPS, SHARDS, CORES) and args[0].shape == (ROWS, WIDTH)
        return tiled_body(*args) if tiled else general(*args)

    return jax.shard_map(body, mesh=mesh, in_specs=in_specs, out_specs=out_specs, check_vma=False)
```

```python
import math

import jax
import jax.numpy as jnp
from jax import lax
from jax.experimental import pallas as pl
from jax.experimental.pallas import tpu as pltpu
from jax.sharding import PartitionSpec as P

HEADS = 16
HEAD_DIM = 64

norm_eps = 1e-05
masked_value = -1e30
f32 = jnp.float32
bf16 = jnp.bfloat16

REPS, SHARDS, CORES = 4, 4, 2
LANE, ROWS, WIDTH, SHARD, TRIPLE, HIDDEN = 128, 128, 1024, 256, 384, 1024
SCALE = HEAD_DIM ** (-0.5)


def normalise(values):
    centre = jnp.mean(values, -1, keepdims=True)
    offsets = values - centre
    spread = jnp.mean(offsets * offsets, -1, keepdims=True)
    scale = lax.rsqrt(spread + norm_eps)
    return offsets * scale, scale


def norm_pull(unit, scale, gain, grad):
    inner = grad * gain
    first = jnp.mean(inner, -1, keepdims=True)
    second = jnp.mean(inner * unit, -1, keepdims=True)
    return scale * (inner - first - unit * second), jnp.sum(grad * unit, 0), jnp.sum(grad, 0)


def gelu_and_slope(values):
    rate = 0.7978845608028654
    squared = values * values
    bent = jnp.tanh(rate * (values + 0.044715 * values * squared))
    half = 0.5 * (1.0 + bent)
    slope = half + 0.5 * values * (1.0 - bent * bent) * (rate * (1.0 + 3.0 * 0.044715 * squared))
    return values * half, slope


def contract(left, right, left_axis, right_axis):
    return lax.dot_general(
        left, right, (((left_axis,), (right_axis,)), ((), ())), preferred_element_type=f32
    )


def swap(value, axis, size, offset):
    return lax.ppermute(value, axis, [(i, i ^ offset) for i in range(size)])


def pick(array, index, axis):
    return lax.dynamic_index_in_dim(array, index, axis, keepdims=False)


def place(pieces, positions):
    stacked = jnp.zeros((len(pieces),) + pieces[0].shape, pieces[0].dtype)
    for piece, position in zip(pieces, positions):
        stacked = lax.dynamic_update_index_in_dim(stacked, piece, position, 0)
    return stacked


def lanes(start, size):
    return pl.ds(pl.multiple_of(start, LANE), size)


def vmem_call(kernel, outs, args, hbm=(), staged=(), scratch=(), flops=0, limit=16):
    moved = sum(a.size * a.dtype.itemsize for a in args)
    moved += sum(math.prod(s) * jnp.dtype(t).itemsize for s, t in outs)
    whole = pl.BlockSpec(memory_space=pltpu.VMEM)
    far = pl.BlockSpec(memory_space=pl.ANY)
    n, m, k = len(args), len(outs), len(staged)

    def body(*refs):
        ins, rest, held, sems = list(refs[:n]), refs[n:], refs[n + m : n + m + k], refs[n + m + k]
        copies = [
            pltpu.make_async_copy(ins[i], held[j], sems.at[j]) for j, i in enumerate(staged)
        ]
        for copy in copies:
            copy.start()
        for copy in copies:
            copy.wait()
        for j, i in enumerate(staged):
            ins[i] = held[j]
        kernel(*ins, *rest[:m], *rest[m + k + 1 :])

    copied = [pltpu.VMEM(args[i].shape, args[i].dtype) for i in staged]
    if staged:
        copied.append(pltpu.SemaphoreType.DMA((k,)))
    return pl.pallas_call(
        body if staged else kernel,
        out_shape=[jax.ShapeDtypeStruct(s, t) for s, t in outs],
        in_specs=[far if i in hbm or i in staged else whole for i in range(n)],
        out_specs=[whole] * m,
        scratch_shapes=copied + list(scratch),
        compiler_params=pltpu.CompilerParams(vmem_limit_bytes=limit * 1024 * 1024),
        cost_estimate=pl.CostEstimate(
            flops=flops * 8, bytes_accessed=moved * 8, transcendentals=0
        ),
    )(*args)


def after(value, *others):
    return lax.optimization_barrier((value,) + others)[0]


def mesh_place():
    return lax.axis_index("rep"), lax.axis_index("fsdp"), lax.axis_index("seq")


def total(refs, read):
    return (read(refs[0]) + read(refs[1])) + (read(refs[2]) + read(refs[3]))


def pack_kernel(*refs):
    qkv, proj, x = refs[0:3]
    vectors, (packed, x_copy, held, sems) = refs[3:-4], refs[-4:]
    rep, _, core = mesh_place()
    mine = (rep * CORES + core) * LANE
    parts = [qkv.at[:, lanes(t * WIDTH + mine, LANE)] for t in range(3)]
    parts.append(proj.at[:, lanes(mine, LANE)])
    targets = [packed.at[pl.ds(0, SHARD), pl.ds(t * LANE, LANE)] for t in range(4)]
    parts += [x] * REPS
    targets += [x_copy.at[pl.ds(k * ROWS, ROWS), :] for k in range(REPS)]
    at = 0
    for v in vectors:
        parts.append(v)
        targets.append(held.at[pl.ds(at, v.shape[0])])
        at += v.shape[0]
    copies = [
        pltpu.make_async_copy(part, target, sems.at[i])
        for i, (part, target) in enumerate(zip(parts, targets))
    ]
    for copy in copies:
        copy.start()
    packed[SHARD:, SHARD:] = jnp.zeros((packed.shape[0] - SHARD, SHARD), bf16)
    for copy in copies:
        copy.wait()
    rows = [held[i * SHARD : (i + 1) * SHARD].astype(f32).reshape(1, SHARD) for i in range(8)]
    biases = [held[i * SHARD : (i + 1) * SHARD].astype(f32).reshape(1, SHARD) for i in range(8, 12)]
    rows.append(
        jnp.where(
            rep < 2,
            jnp.where(rep == 0, biases[0], biases[1]),
            jnp.where(rep == 2, biases[2], biases[3]),
        )
    )
    rows.append(jnp.zeros((16 - len(rows), SHARD), f32))
    packed[SHARD:, 0:SHARD] = jnp.concatenate(rows, 0).astype(bf16)


def unit_kernel(x, unit, scale, unit_own):
    for k in range(REPS):
        at = pl.ds(k * ROWS, ROWS)
        unit[at, :], spread = normalise(x[at, :].astype(f32))
        scale[at, :] = jnp.broadcast_to(spread, (ROWS, LANE))
    own = pl.ds(pl.multiple_of(lax.axis_index("rep") * ROWS, ROWS), ROWS)
    unit_own[0] = unit[own, :]
    unit_own[1, :, 0:LANE] = scale[own, :]
    unit_own[1, :, LANE:] = jnp.zeros((ROWS, WIDTH - LANE), f32)


def qkv_kernel(
    unit, p0, p1, p2, p3, f0, f1, f2, f3, qkv, kv_send, normed, weight, vectors, proj, biases
):
    rep, shard, core = mesh_place()
    for k, (own, far) in enumerate(((p0, f0), (p1, f1), (p2, f2), (p3, f3))):
        at = pl.ds(pl.multiple_of((shard ^ k) * SHARD, SHARD), SHARD)
        weight[at, 0:TRIPLE] = own[0:SHARD, 0:TRIPLE]
        weight[at, TRIPLE : 2 * TRIPLE] = far[0:SHARD, 0:TRIPLE]
        for a in range(REPS):
            start = a * WIDTH + (shard ^ k) * SHARD
            proj[pl.ds(pl.multiple_of(start, SHARD), SHARD), :] = own[0:SHARD, TRIPLE:]
        vectors[:, at] = own[SHARD:, 0:SHARD].astype(f32)
    for p in range(CORES):
        for t, at in ((0, 0), (2, 2)):
            start = (at + rep // 2) * SHARD + (core ^ p) * LANE
            even, odd = vectors[2:3, lanes(start, LANE)], vectors[3:4, lanes(start, LANE)]
            biases[:, pl.ds(p * TRIPLE + t * LANE, LANE)] = jnp.broadcast_to(
                jnp.where(rep % 2 == 0, even, odd), (8, LANE)
            )
        biases[:, pl.ds(p * TRIPLE + LANE, LANE)] = jnp.zeros((8, LANE), f32)

    @pl.loop(0, 2)
    def _(block):
        at = pl.ds(pl.multiple_of(block * 2 * ROWS, 2 * ROWS), 2 * ROWS)
        values = (unit[at, :] * vectors[0:1, :] + vectors[1:2, :]).astype(bf16)
        normed[at, :] = values
        mixed = jnp.dot(values, weight[...], preferred_element_type=f32) + biases[0:1, :]
        mixed = mixed.astype(bf16)
        qkv[at, :] = mixed
        kv_send[at, 0 : 2 * LANE] = mixed[:, TRIPLE + LANE : 2 * TRIPLE]
        kv_send[at, 2 * LANE : 4 * LANE] = mixed[:, LANE:TRIPLE]


def dot_rows(left, right):
    return contract(left, right, 1, 1)


def head_probs(query, key_own, key_far, causal, far_seen):
    own = jnp.where(causal, dot_rows(query, key_own) * SCALE, masked_value)
    far = jnp.where(far_seen, dot_rows(query, key_far) * SCALE, masked_value)
    peak = jnp.maximum(jnp.max(own, -1, keepdims=True), jnp.max(far, -1, keepdims=True))
    own, far = jnp.exp(own - peak), jnp.exp(far - peak)
    share = 1.0 / (jnp.sum(own, -1, keepdims=True) + jnp.sum(far, -1, keepdims=True))
    return own * share, far * share


def head_masks(core):
    causal = lax.broadcasted_iota(jnp.int32, (ROWS, ROWS), 1) <= lax.broadcasted_iota(
        jnp.int32, (ROWS, ROWS), 0
    )
    far_seen = (lax.broadcasted_iota(jnp.int32, (ROWS, ROWS), 0) * 0 + core) == 1
    first = lax.broadcasted_iota(jnp.int32, (ROWS, LANE), 1) < HEAD_DIM
    return causal, far_seen, first


def attend_kernel(qkv, far, attended):
    core = lax.axis_index("seq")
    causal, far_seen, first = head_masks(core)

    for sequence in range(REPS):
        at = pl.ds(sequence * ROWS, ROWS)
        for p in range(CORES):
            base = p * TRIPLE
            query = qkv[at, base : base + LANE]
            key_own = qkv[at, base + LANE : base + 2 * LANE]
            value_own = qkv[at, base + 2 * LANE : base + 3 * LANE]
            key_far = far[at, 2 * p * LANE : (2 * p + 1) * LANE]
            value_far = far[at, (2 * p + 1) * LANE : (2 * p + 2) * LANE]
            heads = []
            for mask in (first, ~first):
                masked = jnp.where(mask, query, jnp.zeros_like(query))
                own, other = head_probs(masked, key_own, key_far, causal, far_seen)
                heads.append(
                    jnp.dot(own.astype(bf16), value_own, preferred_element_type=f32)
                    + jnp.dot(other.astype(bf16), value_far, preferred_element_type=f32)
                )
            attended[at, p * LANE : (p + 1) * LANE] = jnp.where(first, *heads).astype(bf16)


def branch_kernel(a, own, far, x, vectors, middle, unit, scale, normed, proj, joined):
    core = lax.axis_index("seq")
    for k in range(REPS):
        for p, piece in enumerate((own, far)):
            proj[:, lanes((k * CORES + (core ^ p)) * LANE, LANE)] = piece[
                k * WIDTH : (k + 1) * WIDTH, :
            ]
    for k in range(REPS):
        for p in range(CORES):
            at = lanes((k * CORES + (core ^ p)) * LANE, LANE)
            joined[:, at] = a[k * ROWS : (k + 1) * ROWS, p * LANE : (p + 1) * LANE]
    branch = jnp.dot(joined[...], proj[...], preferred_element_type=f32)
    values = x[...].astype(f32) + branch + vectors[4:5, :]
    middle[...] = values
    norm, spread = normalise(values)
    unit[...] = norm
    scale[...] = jnp.broadcast_to(spread, (ROWS, LANE))
    low = (norm * vectors[5:6, :] + vectors[6:7, :]).astype(bf16)
    for k in range(REPS):
        normed[k * ROWS : (k + 1) * ROWS, :] = low


def hidden_kernel(h, c0, c1, c2, c3, ff, vectors, back, hidden, pre_grad, c):
    rep = lax.axis_index("rep")
    for k, cot in enumerate((c0, c1, c2, c3)):
        c[pl.ds(pl.multiple_of((rep ^ k) * ROWS, ROWS), ROWS), :] = cot[...]

    @pl.loop(0, 2)
    def _(block):
        at = pl.ds(pl.multiple_of(block * 2 * ROWS, 2 * ROWS), 2 * ROWS)
        for n in range(SHARDS):
            tile = pl.ds(n * 2 * LANE, 2 * LANE)
            pair = pl.ds(n * CORES, CORES)
            fc, out = ff[pair, 0].reshape(-1, WIDTH), ff[pair, 1].reshape(-1, WIDTH)
            preact = dot_rows(h[at, :], fc) + vectors[8:9, tile]
            value, slope = gelu_and_slope(preact)
            hidden[at, tile] = value.astype(bf16)
            grad = dot_rows(c[at, :], out)
            pre_grad[at, tile] = (grad * slope).astype(bf16)
        fc = ff[:, 0].reshape(HIDDEN, WIDTH)
        back[at, :] = jnp.dot(pre_grad[at, :], fc, preferred_element_type=f32).astype(bf16)


def weights_kernel(hidden, pre_grad, h, c, ff, output, grads, sums):
    for n in range(SHARDS):
        tile = pl.ds(n * 2 * LANE, 2 * LANE)
        for i, (left, right) in enumerate(((pre_grad, h), (hidden, c))):
            grad = contract(left[:, tile], right[...], 0, 0).astype(bf16)
            for j in range(CORES):
                grads[(n * CORES + j) * 2 + i] = grad[j * LANE : (j + 1) * LANE]
    sums[...] = jnp.broadcast_to(
        jnp.sum(pre_grad[...].astype(f32), 0, keepdims=True), sums.shape
    )

    @pl.loop(0, REPS)
    def _(block):
        at = pl.ds(pl.multiple_of(block * ROWS, ROWS), ROWS)
        out = ff[:, 1].reshape(HIDDEN, WIDTH)
        output[at, :] = jnp.dot(hidden[at, :], out, preferred_element_type=f32).astype(bf16)


def middle_kernel(
    g, unit, scale, vectors, cot, proj, middle_grad, pairs, sums, low, back
):
    rep, _, core = mesh_place()
    grad = total(range(REPS), lambda k: g[k * ROWS : (k + 1) * ROWS, :].astype(f32))
    part, gain, shift = norm_pull(unit[...], scale[:, 0:1], vectors[5:6, :], grad)
    cots = cot[...].astype(f32)
    values = cots + part
    middle_grad[...] = values
    branch = values.astype(bf16)
    low[...] = branch
    back[...] = dot_rows(branch, proj[...]).astype(bf16)
    rows = [jnp.sum(branch.astype(f32), 0), gain, shift, jnp.sum(cots, 0)]
    for i, row in enumerate(rows):
        sums[i : i + 1, :] = row[None]
    sums[4:8, :] = jnp.zeros((4, WIDTH), f32)
    for k in range(REPS):
        rows = pl.ds(k * ROWS, ROWS)
        for p in range(CORES):
            at = lanes((k * CORES + (core ^ p)) * LANE, LANE)
            pairs[rows, p * LANE : (p + 1) * LANE] = back[:, at]
        pairs[rows, SHARD : 2 * SHARD] = low[:, k * SHARD : (k + 1) * SHARD]


def proj_grad_kernel(a0, a1, a2, a3, pairs, own, far):
    rep, shard, core = mesh_place()
    for k, a in enumerate((a0, a1, a2, a3)):
        grad = contract(a[...], pairs[:, SHARD : 2 * SHARD], 0, 0).astype(bf16)
        mine = jnp.where(core == 0, grad[:, 0:LANE], grad[:, LANE:])
        other = jnp.where(core == 0, grad[:, LANE:], grad[:, 0:LANE])
        for p in range(CORES):
            at = pl.ds(pl.multiple_of((core ^ p) * LANE, LANE), LANE)
            own[rep ^ k ^ shard, at, :] = mine[p * LANE : (p + 1) * LANE]
            far[rep ^ k ^ shard, at, :] = other[p * LANE : (p + 1) * LANE]


def attend_back_kernel(qkv, far, pairs, query_grad, own_grad, far_grad):
    core = lax.axis_index("seq")
    causal, far_seen, first = head_masks(core)

    for sequence in range(REPS):
        at = pl.ds(sequence * ROWS, ROWS)
        for p in range(CORES):
            base = p * TRIPLE
            query = qkv[at, base : base + LANE]
            key_own = qkv[at, base + LANE : base + 2 * LANE]
            value_own = qkv[at, base + 2 * LANE : base + 3 * LANE]
            key_far = far[at, 2 * p * LANE : (2 * p + 1) * LANE]
            value_far = far[at, (2 * p + 1) * LANE : (2 * p + 2) * LANE]
            grad = pairs[at, p * LANE : (p + 1) * LANE]
            queries, sums = [], [0.0] * 4
            for mask in (first, ~first):
                masked = jnp.where(mask, query, jnp.zeros_like(query))
                back = jnp.where(mask, grad, jnp.zeros_like(grad))
                own, other = head_probs(masked, key_own, key_far, causal, far_seen)
                own_back, other_back = dot_rows(back, value_own), dot_rows(back, value_far)
                row = jnp.sum(own * own_back, -1, keepdims=True) + jnp.sum(
                    other * other_back, -1, keepdims=True
                )
                own_score = (own * (own_back - row)).astype(bf16)
                other_score = (other * (other_back - row)).astype(bf16)
                queries.append(
                    jnp.dot(own_score, key_own, preferred_element_type=f32)
                    + jnp.dot(other_score, key_far, preferred_element_type=f32)
                )
                parts = [
                    contract(own_score, masked, 0, 0) * SCALE,
                    contract(own.astype(bf16), back, 0, 0),
                    contract(other_score, masked, 0, 0) * SCALE,
                    contract(other.astype(bf16), back, 0, 0),
                ]
                sums = [a + b for a, b in zip(sums, parts)]
            query_grad[at, p * LANE : (p + 1) * LANE] = (
                jnp.where(first, *queries) * SCALE
            ).astype(bf16)
            own_at = slice(2 * p * LANE, (2 * p + 1) * LANE)
            own_grad[at, own_at] = sums[0]
            own_grad[at, (2 * p + 1) * LANE : (2 * p + 2) * LANE] = sums[1]
            q = 1 - p
            far_grad[at, 2 * q * LANE : (2 * q + 1) * LANE] = sums[2].astype(bf16)
            far_grad[at, (2 * q + 1) * LANE : (2 * q + 2) * LANE] = sums[3].astype(bf16)


def qkv_back_kernel(
    query_grad,
    own_grad,
    far_grad,
    weight,
    normed,
    unit,
    ff_sums,
    mid_sums,
    proj_own,
    proj_far,
    own,
    far,
    joined,
    small,
    mixed,
    sums,
):
    rep, shard, core = mesh_place()
    for p in range(CORES):
        base = p * TRIPLE
        mixed[:, base : base + LANE] = query_grad[:, p * LANE : (p + 1) * LANE]
        at = slice(2 * p * LANE, (2 * p + 2) * LANE)
        mixed[:, base + LANE : base + 3 * LANE] = (
            own_grad[:, at] + far_grad[:, at].astype(f32)
        ).astype(bf16)
    for k in range(SHARDS):
        at = lanes((shard ^ k) * SHARD, SHARD)
        grad = contract(normed[:, at], mixed[...], 0, 0).astype(bf16)
        own[k, :, 0:TRIPLE] = grad[:, 0:TRIPLE]
        far[k, :, 0:TRIPLE] = grad[:, TRIPLE:]
        own[k, :, TRIPLE:] = proj_own[k]
        far[k, :, TRIPLE:] = proj_far[k]
    gain = jnp.zeros((1, WIDTH), f32)
    shift = jnp.zeros((1, WIDTH), f32)
    for k in range(REPS):
        at = pl.ds(k * ROWS, ROWS)
        back = dot_rows(mixed[at, :], weight[...])
        joined[at, :] = back.astype(bf16)
        gain = gain + jnp.sum(back * unit[at, :], 0, keepdims=True)
        shift = shift + jnp.sum(back, 0, keepdims=True)
    sums[0:1, :] = gain
    sums[1:2, :] = shift
    mixed_sums = jnp.sum(mixed[...].astype(f32), 0, keepdims=True)
    for p in range(CORES):
        for i in range(2):
            start = i * SHARD + (core ^ p) * LANE
            sums[2:3, lanes(start, LANE)] = mixed_sums[
                :, p * TRIPLE + 2 * i * LANE : p * TRIPLE + (2 * i + 1) * LANE
            ]
    for k in range(SHARDS):
        small[k] = jnp.zeros(small.shape[1:], f32)
        at = lanes((shard ^ k) * SHARD, SHARD)
        small[k, 0:1, 0:SHARD] = sums[0:1, at]
        small[k, 1:2, 0:SHARD] = sums[1:2, at]
        queries = jnp.where((shard ^ k) == rep // 2, sums[2:3, 0:SHARD], 0.0)
        values = jnp.where((shard ^ k) == 2 + rep // 2, sums[2:3, SHARD : 2 * SHARD], 0.0)
        small[k, 2:3, 0:SHARD] = jnp.where(rep % 2 == 0, queries + values, 0.0)
        small[k, 3:4, 0:SHARD] = jnp.where(rep % 2 == 1, queries + values, 0.0)
        for i in range(4):
            small[k, 4 + i : 5 + i, 0:SHARD] = mid_sums[i : i + 1, at]
        part = ff_sums[:, at]
        row = lax.broadcasted_iota(jnp.int32, part.shape, 0)
        small[k, 8:16, 0:SHARD] = jnp.where(row == rep, part, 0.0)


def tail_kernel(own, far, small, o0, o1, o2, o3):
    for k, o in enumerate((o0, o1, o2, o3)):
        o[0:SHARD, :] = (own[k].astype(f32) + far[k].astype(f32)).astype(bf16)
        o[SHARD:, :] = small[k].astype(bf16)


def input_kernel(j, unit, vectors, middle_grad, grad):
    back = total(range(REPS), lambda k: j[k * ROWS : (k + 1) * ROWS, :].astype(f32))
    part, _, _ = norm_pull(unit[0], unit[1, :, 0:1], vectors[0:1, :], back)
    grad[...] = middle_grad[...] + part


def block_kernel(j, middle, vectors, block):
    output = total(range(REPS), lambda k: j[k * ROWS : (k + 1) * ROWS, :].astype(f32))
    block[...] = (middle[...] + output + vectors[7:8, :]).astype(bf16)


def joined_sum(pieces):
    pieces = [p.astype(f32) for p in pieces]
    return ((pieces[0] + pieces[1]) + (pieces[2] + pieces[3])).astype(bf16)


def final_kernel(p0, p1, p2, p3, f0, f1, f2, f3, qkv, proj, small):
    rep, _, core = mesh_place()
    for k, pair in enumerate(((p0, f0), (p1, f1), (p2, f2), (p3, f3))):
        for j, piece in enumerate(pair):
            start = ((rep ^ k) * CORES + (core ^ j)) * LANE
            for t in range(3):
                qkv[:, lanes(t * WIDTH + start, LANE)] = piece[
                    0:SHARD, t * LANE : (t + 1) * LANE
                ].astype(f32)
            proj[:, lanes(start, LANE)] = piece[0:SHARD, TRIPLE:].astype(f32)

    def read(pair):
        return pair[0][SHARD:, 0:SHARD].astype(f32) + pair[1][SHARD:, 0:SHARD].astype(f32)

    small[...] = total(((p0, f0), (p1, f1), (p2, f2), (p3, f3)), read)


def spread_kernel(p0, p1, p2, p3, f0, f1, f2, f3, fc, out):
    rep, _, core = mesh_place()
    for k, pair in enumerate(((p0, f0), (p1, f1), (p2, f2), (p3, f3))):
        for j, piece in enumerate(pair):
            at = pl.ds(pl.multiple_of(((rep ^ k) * CORES + (core ^ j)) * LANE, LANE), LANE)
            fc[at, :] = piece[0].astype(f32)
            out[at, :] = piece[1].astype(f32)


def tiled_body(
    block_input,
    ln1_gain,
    ln1_shift,
    qkv_weight,
    qv_bias,
    proj_weight,
    proj_bias,
    ln2_gain,
    ln2_shift,
    fc_weight,
    fc_bias,
    out_weight,
    out_bias,
    cotangent,
):
    rep, _, core = mesh_place()

    def over_rep(pieces):
        return [swap(p, "rep", REPS, k) if k else p for k, p in enumerate(pieces)]

    def over_shards(pieces):
        return [swap(p, "fsdp", SHARDS, k) if k else p for k, p in enumerate(pieces)]

    def over_cores(value):
        return swap(value, "seq", CORES, 1)

    all_rows = REPS * ROWS
    vectors = [
        ln1_gain,
        ln1_shift,
        qv_bias,
        proj_bias,
        ln2_gain,
        ln2_shift,
        out_bias,
        fc_bias,
    ]
    packed, own_rows = vmem_call(
        pack_kernel,
        [((SHARD + 16, TRIPLE + LANE), bf16), ((all_rows, WIDTH), bf16)],
        [qkv_weight, proj_weight, block_input] + vectors,
        hbm=tuple(range(11)),
        scratch=[pltpu.VMEM((12 * SHARD,), bf16), pltpu.SemaphoreType.DMA((16,))],
        limit=56,
    )
    own_packed = over_shards([packed] * SHARDS)
    far_packed = [over_cores(p) for p in own_packed]
    inputs = lax.all_to_all(own_rows, "rep", 0, 0, tiled=True)

    unit_one, _, unit_own = vmem_call(
        unit_kernel,
        [((all_rows, WIDTH), f32), ((all_rows, LANE), f32), ((2, ROWS, WIDTH), f32)],
        [inputs],
    )
    cots = over_rep([after(cotangent, unit_one)] * REPS)

    mine = rep * CORES + core
    ff = [pick(w.reshape(REPS * CORES, LANE, WIDTH), mine, 0) for w in (fc_weight, out_weight)]
    ff = after(jnp.stack(ff), *own_packed[1:], inputs)
    ff = lax.all_gather(ff, ("fsdp", "seq"), axis=0)

    qkv, kv_send, normed_one, qkv_mine, vectors, proj_cols = vmem_call(
        qkv_kernel,
        [
            ((all_rows, 2 * TRIPLE), bf16),
            ((all_rows, 4 * LANE), bf16),
            ((all_rows, WIDTH), bf16),
            ((WIDTH, 2 * TRIPLE), bf16),
            ((16, WIDTH), f32),
            ((REPS * WIDTH, LANE), bf16),
        ],
        [unit_one] + own_packed + far_packed,
        scratch=[pltpu.VMEM((8, 2 * TRIPLE), f32)],
        flops=2 * all_rows * WIDTH * 2 * TRIPLE,
    )
    kv_far = over_cores(kv_send)
    proj_cols = lax.all_to_all(proj_cols, "rep", 0, 0, tiled=True)
    (attended,) = vmem_call(
        attend_kernel,
        [((all_rows, SHARD), bf16)],
        [qkv, kv_far],
        flops=4 * all_rows * 2 * ROWS * SHARD,
    )
    mine = lax.all_to_all(attended, "rep", 0, 0, tiled=True)
    middle, unit_two, scale_two, normed_two, proj_full = vmem_call(
        branch_kernel,
        [
            ((ROWS, WIDTH), f32),
            ((ROWS, WIDTH), f32),
            ((ROWS, LANE), f32),
            ((all_rows, WIDTH), bf16),
            ((WIDTH, WIDTH), bf16),
        ],
        [after(mine, *cots[1:]), proj_cols, over_cores(after(proj_cols, attended)), block_input, vectors],
        scratch=[pltpu.VMEM((ROWS, WIDTH), bf16)],
        flops=2 * ROWS * WIDTH * WIDTH,
    )
    normed_two = lax.all_to_all(normed_two, "rep", 0, 0, tiled=True)
    attended_all = over_rep([after(attended, normed_two)] * REPS)

    back, hidden, pre_grad, c_all = vmem_call(
        hidden_kernel,
        [
            ((all_rows, HIDDEN), bf16),
            ((all_rows, HIDDEN), bf16),
            ((all_rows, WIDTH), bf16),
            ((all_rows, WIDTH), bf16),
        ],
        [normed_two] + cots + [ff, vectors],
        flops=6 * all_rows * WIDTH * HIDDEN,
    )
    back = lax.all_to_all(back, "rep", 0, 0, tiled=True)
    output, ff_grads, ff_sums = vmem_call(
        weights_kernel,
        [
            ((all_rows, WIDTH), bf16),
            ((SHARDS * CORES * 2, LANE, WIDTH), bf16),
            ((8, HIDDEN), f32),
        ],
        [after(hidden, *attended_all[1:]), pre_grad, normed_two, c_all, ff],
        flops=6 * all_rows * WIDTH * HIDDEN,
    )
    ff_piece = lax.psum_scatter(ff_grads, ("fsdp", "seq"), scatter_dimension=0, tiled=True)

    middle_grad, pairs, mid_sums = vmem_call(
        middle_kernel,
        [((ROWS, WIDTH), f32), ((all_rows, 2 * SHARD), bf16), ((8, WIDTH), f32)],
        [back, unit_two, scale_two, vectors, cotangent, proj_full],
        scratch=[pltpu.VMEM((ROWS, WIDTH), bf16)] * 2,
        flops=2 * ROWS * WIDTH * WIDTH,
    )
    pairs = lax.all_to_all(pairs, "rep", 0, 0, tiled=True)
    output = lax.all_to_all(after(output, pairs), "rep", 0, 0, tiled=True)
    (block_output,) = vmem_call(block_kernel, [((ROWS, WIDTH), bf16)], [output, middle, vectors])
    query_grad, own_grad, far_grad = vmem_call(
        attend_back_kernel,
        [
            ((all_rows, SHARD), bf16),
            ((all_rows, 4 * LANE), f32),
            ((all_rows, 4 * LANE), bf16),
        ],
        [qkv, kv_far, pairs],
        flops=10 * all_rows * 2 * ROWS * SHARD,
    )
    proj_own, proj_far = vmem_call(
        proj_grad_kernel,
        [((SHARDS, SHARD, LANE), bf16)] * 2,
        attended_all + [pairs],
        flops=2 * all_rows * WIDTH * SHARD,
    )
    qkv_own, qkv_far, joined, small = vmem_call(
        qkv_back_kernel,
        [
            ((SHARDS, SHARD, TRIPLE + LANE), bf16),
            ((SHARDS, SHARD, TRIPLE + LANE), bf16),
            ((all_rows, WIDTH), bf16),
            ((SHARDS, 16, TRIPLE + LANE), f32),
        ],
        [query_grad, own_grad, over_cores(far_grad), qkv_mine, normed_one, unit_one, ff_sums, mid_sums]
        + [proj_own, proj_far],
        scratch=[pltpu.VMEM((all_rows, 2 * TRIPLE), bf16), pltpu.VMEM((8, WIDTH), f32)],
        flops=4 * all_rows * WIDTH * 2 * TRIPLE,
    )
    tail = vmem_call(
        tail_kernel,
        [((SHARD + 16, TRIPLE + LANE), bf16)] * SHARDS,
        [qkv_own, over_cores(qkv_far), after(small, block_output)],
    )
    tail = over_shards(tail)
    joined = lax.all_to_all(joined, "rep", 0, 0, tiled=True)
    ff_pieces = over_rep([ff_piece] * REPS)
    tail = joined_sum([after(tail[0], joined, *ff_pieces[1:])] + tail[1:])
    (input_grad,) = vmem_call(
        input_kernel, [((ROWS, WIDTH), f32)], [joined, unit_own, vectors, middle_grad]
    )
    tail = over_rep([tail] * REPS)
    fc_grads, out_grads = vmem_call(
        spread_kernel,
        [((2 * REPS * LANE, WIDTH), f32)] * 2,
        ff_pieces + [over_cores(after(p, tail[1])) for p in ff_pieces],
    )
    qkv_grads, proj_grads, small = vmem_call(
        final_kernel,
        [((SHARD, 3 * WIDTH), f32), ((SHARD, WIDTH), f32), ((16, SHARD), f32)],
        tail + [over_cores(t) for t in tail],
    )
    return (
        block_output,
        input_grad,
        small[0],
        small[1],
        qkv_grads,
        small[2:4].reshape(-1),
        proj_grads,
        small[4],
        small[5],
        small[6],
        fc_grads,
        small[8:12].reshape(-1),
        out_grads,
        small[7],
    )


def make_body(reps, shards, cores):
    def rep_swap(value, offset):
        return swap(value, "rep", reps, offset) if offset else value

    def shard_swap(value, offset):
        return swap(value, "fsdp", shards, offset) if offset else value

    def core_swap(value):
        return swap(value, "seq", cores, 1)

    def plane_gather(value):
        return [rep_swap(value, k) for k in range(reps)]

    def plane_exchange(pieces):
        return [rep_swap(piece, k) for k, piece in enumerate(pieces)]

    def pair_sum(pieces):
        while len(pieces) > 1:
            pieces = [pieces[i] + pieces[i + 1] for i in range(0, len(pieces), 2)]
        return pieces[0]

    def own_scatter(parts):
        core = lax.axis_index("seq")
        shard = lax.axis_index("fsdp")
        kept = pick(parts, core, 1).astype(f32)
        kept = (kept + core_swap(pick(parts, 1 - core, 1)).astype(f32)).astype(bf16)
        pieces = [shard_swap(pick(kept, shard ^ k, 0), k).astype(f32) for k in range(shards)]
        return pair_sum(pieces).astype(bf16)

    def place_both(pieces):
        core = lax.axis_index("seq")
        rep = lax.axis_index("rep")
        held = jnp.zeros((reps, cores) + pieces[0].shape, pieces[0].dtype)
        zeros = (0,) * pieces[0].ndim
        for k, piece in enumerate(pieces):
            held = lax.dynamic_update_slice(held, piece[None, None], (rep ^ k, core) + zeros)
            far = core_swap(piece)
            held = lax.dynamic_update_slice(held, far[None, None], (rep ^ k, 1 - core) + zeros)
        return held

    def body(
        block_input,
        ln1_gain,
        ln1_shift,
        qkv_weight,
        qv_bias,
        proj_weight,
        proj_bias,
        ln2_gain,
        ln2_shift,
        fc_weight,
        fc_bias,
        out_weight,
        out_bias,
        cotangent,
    ):
        rows, width = block_input.shape
        shard_width = width // shards
        part = width // (reps * cores)
        rep_width = part * cores
        hidden_part = fc_weight.shape[0] // (reps * cores)
        head_scale = HEAD_DIM ** (-0.5)
        rep = lax.axis_index("rep")
        shard = lax.axis_index("fsdp")
        core = lax.axis_index("seq")
        rep_at = [rep ^ k for k in range(reps)]
        shard_at = [shard ^ k for k in range(shards)]

        columns = qkv_weight.reshape(shard_width, 3, reps, cores, part)
        columns = pick(pick(columns, rep, 2), core, 2).reshape(shard_width, 3 * part)
        fc_bias_part = pick(fc_bias.reshape(reps, -1), rep, 0)
        vectors = [
            ln1_gain,
            ln1_shift,
            qv_bias[:shard_width],
            qv_bias[shard_width:],
            proj_bias,
            ln2_gain,
            ln2_shift,
            out_bias,
            fc_bias_part,
        ]
        vectors = [jnp.pad(v, (0, 3 * part - v.shape[0])) for v in vectors]
        vectors = jnp.stack(vectors + [jnp.zeros_like(vectors[0])] * (16 - len(vectors)))
        packed = jnp.concatenate([columns, vectors], 0)
        packed, own_rows = lax.optimization_barrier((packed, block_input))
        packed = place([shard_swap(packed, k) for k in range(shards)], shard_at)
        inputs_all = jnp.concatenate(plane_gather(own_rows), 0)
        columns = packed[:, :shard_width].reshape(width, 3 * part)
        vectors = packed[:, shard_width:, :].astype(f32)

        def vector(index, size):
            return vectors[:, index, :size].reshape(-1)

        gain_one, shift_one = vector(0, shard_width), vector(1, shard_width)
        qv_full = jnp.stack([vectors[:, 2, :shard_width], vectors[:, 3, :shard_width]], 1)
        qv_full = qv_full.reshape(2, reps, cores * part)
        proj_bias_full = vector(4, shard_width)
        gain_two, shift_two = vector(5, shard_width), vector(6, shard_width)
        out_bias_full = vector(7, shard_width)
        fc_bias_mine = vector(8, fc_bias_part.shape[0])
        qkv_mine = place([columns, core_swap(columns)], [core, 1 - core])
        qkv_mine = jnp.transpose(qkv_mine, (1, 0, 2)).reshape(width, cores * 3 * part)

        proj_part = pick(proj_weight.reshape(reps * cores, -1, width), rep * cores + core, 0)
        proj_full = lax.all_gather(proj_part, ("rep", "fsdp", "seq"), axis=0)
        proj_full = proj_full.reshape((reps, shards, cores) + proj_part.shape)
        proj_full = jnp.transpose(proj_full, (1, 0, 2, 3, 4)).reshape(width, width)

        fc_part = pick(fc_weight.reshape(reps * cores, hidden_part, width), rep * cores + core, 0)
        out_part = pick(out_weight.reshape(reps * cores, hidden_part, width), rep * cores + core, 0)
        both_part = jnp.stack([fc_part, out_part])
        both_part, packed = lax.optimization_barrier((both_part, packed))
        both = place([shard_swap(both_part, k) for k in range(shards)], shard_at)
        both = place([both, core_swap(both)], [core, 1 - core])
        fc_mine = jnp.transpose(both[:, :, 0], (1, 0, 2, 3)).reshape(-1, width)
        out_mine = jnp.transpose(both[:, :, 1], (1, 0, 2, 3)).reshape(-1, width)

        own_cot, inputs_all = lax.optimization_barrier((cotangent, inputs_all))
        cot_all = jnp.concatenate(plane_gather(own_cot), 0)

        unit_one, scale_one = normalise(inputs_all.astype(f32))
        normed_all = (unit_one * gain_one + shift_one).astype(bf16)
        mixed = jnp.dot(normed_all, qkv_mine, preferred_element_type=f32)
        mixed = mixed.reshape(reps, rows, cores, 3, part)
        qv_mine = pick(qv_full, rep, 1).reshape(2, cores, part)
        heads = (reps, rows, rep_width // HEAD_DIM, HEAD_DIM)
        queries = (mixed[:, :, :, 0] + qv_mine[0]).astype(bf16).reshape(heads)
        keys = mixed[:, :, :, 1].astype(bf16).reshape(heads)
        values = (mixed[:, :, :, 2] + qv_mine[1]).astype(bf16).reshape(heads)
        far_pair = core_swap(jnp.stack([keys, values]))
        keys_both = jnp.concatenate([keys, far_pair[0]], 1)
        values_both = jnp.concatenate([values, far_pair[1]], 1)

        row_pos = lax.broadcasted_iota(jnp.int32, (rows, 2 * rows), 0)
        col_pos = lax.broadcasted_iota(jnp.int32, (rows, 2 * rows), 1)
        allowed = jnp.where(col_pos < rows, col_pos <= row_pos, core == 1)
        scores = jnp.einsum("sqhd,skhd->shqk", queries, keys_both, preferred_element_type=f32)
        scores = jnp.where(allowed, scores * head_scale, masked_value)
        peak = jnp.max(scores, -1, keepdims=True)
        powers = jnp.exp(scores - peak)
        probs = powers / jnp.sum(powers, -1, keepdims=True)
        probs_low = probs.astype(bf16)
        attended = jnp.einsum("shqk,skhd->sqhd", probs_low, values_both, preferred_element_type=f32)
        attended_low = attended.astype(bf16).reshape(reps, rows, rep_width)
        mine = place(plane_exchange([attended_low[k] for k in range(reps)]), rep_at)
        mine = jnp.transpose(mine, (1, 0, 2)).reshape(rows, width)
        middle = (
            block_input.astype(f32)
            + jnp.dot(mine, proj_full, preferred_element_type=f32)
            + proj_bias_full
        )
        unit_two, scale_two = normalise(middle)
        normed_two = (unit_two * gain_two + shift_two).astype(bf16)
        normed_two_all = jnp.concatenate(plane_gather(normed_two), 0)

        attended_all = place([attended_low[k] for k in range(reps)], rep_at)
        attended_all = lax.all_gather(attended_all.reshape(reps * rows, rep_width), "rep", axis=0)
        attended_all = jnp.transpose(attended_all, (1, 0, 2)).reshape(reps * rows, width)

        hidden_grad = contract(cot_all, out_mine, 1, 1)
        preact = contract(normed_two_all, fc_mine, 1, 1) + fc_bias_mine
        hidden, slope = gelu_and_slope(preact)
        hidden_low = hidden.astype(bf16)
        pre_grad = (hidden_grad * slope).astype(bf16)
        normed_grad = jnp.dot(pre_grad, fc_mine, preferred_element_type=f32).astype(bf16)
        normed_grad = normed_grad.reshape(reps, rows, width)
        normed_grad = plane_exchange([normed_grad[k] for k in range(reps)])
        normed_grad = pair_sum([v.astype(f32) for v in normed_grad])
        output = jnp.dot(hidden_low, out_mine, preferred_element_type=f32).astype(bf16)
        output, normed_grad = lax.optimization_barrier((output, normed_grad))
        output = output.reshape(reps, rows, width)
        output = plane_exchange([output[k] for k in range(reps)])
        output = pair_sum([v.astype(f32) for v in output])
        block_output = (middle + output + out_bias_full).astype(bf16)

        out_grads = contract(hidden_low, cot_all, 0, 0).astype(bf16)
        out_grads = lax.psum_scatter(out_grads, ("fsdp", "seq"), scatter_dimension=0, tiled=True)
        fc_grads = contract(pre_grad, normed_two_all, 0, 0).astype(bf16)
        fc_grads = own_scatter(fc_grads.reshape(shards, cores, hidden_part, width))
        ff_grads = plane_gather(jnp.stack([fc_grads, out_grads]))
        ff_grads = place_both(ff_grads)
        fc_grads = ff_grads[:, :, 0].reshape(-1, width).astype(f32)
        out_grads = ff_grads[:, :, 1].reshape(-1, width).astype(f32)

        middle_part, gain_two_grads, shift_two_grads = norm_pull(
            unit_two, scale_two, gain_two, normed_grad
        )
        middle_grad = cotangent.astype(f32) + middle_part
        branch_grad = middle_grad.astype(bf16)
        attended_grad = contract(branch_grad, proj_full, 1, 1).astype(bf16)
        pair = [v.reshape(rows, reps, rep_width) for v in (attended_grad, branch_grad)]
        pair = jnp.concatenate(pair, 2)
        pair = plane_exchange([pick(pair, i, 1) for i in rep_at])
        attended_grad = jnp.stack([v[:, :rep_width] for v in pair]).reshape(heads)
        branch_cols = place([v[:, rep_width:] for v in pair], rep_at).reshape(-1, rep_width)
        proj_grads = contract(attended_all, branch_cols, 0, 0).astype(bf16)
        proj_grads = proj_grads.reshape(shards, shard_width, cores, part)
        proj_grads = jnp.transpose(proj_grads, (0, 2, 1, 3)).reshape(-1, part)
        proj_grads = lax.psum_scatter(proj_grads, ("fsdp", "seq"), scatter_dimension=0, tiled=True)
        proj_grads = lax.all_gather(proj_grads, ("rep", "seq"), axis=0)
        proj_grads = jnp.transpose(proj_grads, (1, 0, 2)).reshape(shard_width, width).astype(f32)

        prob_grad = jnp.einsum("sqhd,skhd->shqk", attended_grad, values_both, preferred_element_type=f32)
        row_total = jnp.sum(probs * prob_grad, -1, keepdims=True)
        score_low = (probs * (prob_grad - row_total)).astype(bf16)
        query_grad = (
            jnp.einsum("shqk,skhd->sqhd", score_low, keys_both, preferred_element_type=f32)
            * head_scale
        )
        key_grad = (
            jnp.einsum("shqk,sqhd->skhd", score_low, queries, preferred_element_type=f32)
            * head_scale
        )
        value_grad = jnp.einsum("shqk,sqhd->skhd", probs_low, attended_grad, preferred_element_type=f32)
        far_grads = core_swap(jnp.stack([key_grad[:, rows:], value_grad[:, rows:]]).astype(bf16))
        key_grad = key_grad[:, :rows] + far_grads[0].astype(f32)
        value_grad = value_grad[:, :rows] + far_grads[1].astype(f32)
        mixed_grad = jnp.stack(
            [
                g.astype(bf16).reshape(reps * rows, cores, part)
                for g in (query_grad, key_grad, value_grad)
            ],
            2,
        ).reshape(reps * rows, cores * 3 * part)
        qkv_grads = contract(normed_all, mixed_grad, 0, 0).astype(bf16)
        normed_one_grad = contract(mixed_grad, qkv_mine, 1, 1)
        joined = normed_one_grad.astype(bf16).reshape(reps, rows, width)
        joined = plane_exchange([joined[k] for k in range(reps)])
        joined = pair_sum([v.astype(f32) for v in joined])
        input_part = norm_pull(unit_one[:rows], scale_one[:rows], gain_one, joined)[0]
        input_grad = middle_grad + input_part

        gain_one_grads = jnp.sum(normed_one_grad * unit_one, 0)
        shift_one_grads = jnp.sum(normed_one_grad, 0)
        mixed_sums = jnp.sum(mixed_grad.astype(f32), 0).reshape(cores, 3, part)
        qv_sums = jnp.stack([mixed_sums[:, 0].reshape(-1), mixed_sums[:, 2].reshape(-1)])
        qv_sums = lax.dynamic_update_index_in_dim(
            jnp.zeros((2, reps, rep_width), f32), qv_sums, rep, 1
        )
        fc_sums = jnp.sum(pre_grad.astype(f32), 0).reshape(shards, -1)
        fc_sums = lax.dynamic_update_index_in_dim(
            jnp.zeros((shards, reps, fc_sums.shape[1]), f32), fc_sums, rep, 1
        )
        small = [
            gain_one_grads,
            shift_one_grads,
            qv_sums,
            jnp.sum(branch_grad.astype(f32), 0),
            gain_two_grads,
            shift_two_grads,
            jnp.sum(cotangent.astype(f32), 0),
            fc_sums,
        ]
        small = jnp.concatenate([v.reshape(shards, -1) for v in small], 1).astype(bf16)
        small_size = small.shape[1]
        small_rows = -(-small_size // (16 * 3 * part)) * 16
        small = jnp.pad(small, ((0, 0), (0, small_rows * 3 * part - small_size)))
        small = small.reshape(shards, small_rows, 3 * part)

        qkv_grads = qkv_grads.reshape(shards, shard_width, cores, 3 * part)
        tail = pick(qkv_grads, core, 2).astype(f32)
        tail = (tail + core_swap(pick(qkv_grads, 1 - core, 2)).astype(f32)).astype(bf16)
        tail = jnp.concatenate([tail, small], 1)
        tail = [shard_swap(pick(tail, i, 0), k).astype(f32) for k, i in enumerate(shard_at)]
        tail = place_both(plane_gather(pair_sum(tail).astype(bf16)))
        qkv_grads = tail[:, :, :shard_width].reshape(reps * cores, shard_width, 3, part)
        qkv_grads = jnp.transpose(qkv_grads, (1, 2, 0, 3)).reshape(shard_width, 3 * width)
        qkv_grads = qkv_grads.astype(f32)
        small = jnp.sum(tail[:, :, shard_width:].astype(f32), (0, 1)).reshape(-1)
        sizes = [1, 1, 2, 1, 1, 1, 1]
        ends = [0]
        for size in sizes:
            ends.append(ends[-1] + size * shard_width)
        one = [small[a:b] for a, b in zip(ends[:-1], ends[1:])] + [small[ends[-1] : small_size]]
        return (
            block_output,
            input_grad,
            one[0],
            one[1],
            qkv_grads,
            one[2],
            proj_grads,
            one[3],
            one[4],
            one[5],
            fc_grads,
            one[7],
            out_grads,
            one[6],
        )

    return body


def solution(mesh):
    line, block = P("fsdp"), P("fsdp", None)
    tokens = P(("rep", "fsdp", "seq"), None)
    in_specs = (
        tokens,
        line,
        line,
        block,
        line,
        block,
        line,
        line,
        line,
        block,
        line,
        block,
        line,
        tokens,
    )
    out_specs = (
        tokens,
        tokens,
        line,
        line,
        block,
        line,
        block,
        line,
        line,
        line,
        block,
        line,
        block,
        line,
    )
    sizes = mesh.shape["rep"], mesh.shape["fsdp"], mesh.shape["seq"]
    general = make_body(*sizes)

    def body(*args):
        tiled = sizes == (REPS, SHARDS, CORES) and args[0].shape == (ROWS, WIDTH)
        return tiled_body(*args) if tiled else general(*args)

    return jax.shard_map(body, mesh=mesh, in_specs=in_specs, out_specs=out_specs, check_vma=False)
```

```python
import math

import jax
import jax.numpy as jnp
from jax import lax
from jax.experimental import pallas as pl
from jax.experimental.pallas import tpu as pltpu
from jax.sharding import PartitionSpec as P

HEADS = 16
HEAD_DIM = 64

norm_eps = 1e-05
masked_value = -1e30
f32 = jnp.float32
bf16 = jnp.bfloat16

REPS, SHARDS, CORES = 4, 4, 2
LANE, ROWS, WIDTH, SHARD, TRIPLE, HIDDEN = 128, 128, 1024, 256, 384, 1024
SCALE = HEAD_DIM ** (-0.5)


def normalise(values):
    centre = jnp.mean(values, -1, keepdims=True)
    offsets = values - centre
    spread = jnp.mean(offsets * offsets, -1, keepdims=True)
    scale = lax.rsqrt(spread + norm_eps)
    return offsets * scale, scale


def norm_pull(unit, scale, gain, grad):
    inner = grad * gain
    first = jnp.mean(inner, -1, keepdims=True)
    second = jnp.mean(inner * unit, -1, keepdims=True)
    return scale * (inner - first - unit * second), jnp.sum(grad * unit, 0), jnp.sum(grad, 0)


def gelu_and_slope(values):
    rate = 0.7978845608028654
    squared = values * values
    bent = jnp.tanh(rate * (values + 0.044715 * values * squared))
    half = 0.5 * (1.0 + bent)
    slope = half + 0.5 * values * (1.0 - bent * bent) * (rate * (1.0 + 3.0 * 0.044715 * squared))
    return values * half, slope


def contract(left, right, left_axis, right_axis):
    return lax.dot_general(
        left, right, (((left_axis,), (right_axis,)), ((), ())), preferred_element_type=f32
    )


def swap(value, axis, size, offset):
    return lax.ppermute(value, axis, [(i, i ^ offset) for i in range(size)])


def pick(array, index, axis):
    return lax.dynamic_index_in_dim(array, index, axis, keepdims=False)


def place(pieces, positions):
    stacked = jnp.zeros((len(pieces),) + pieces[0].shape, pieces[0].dtype)
    for piece, position in zip(pieces, positions):
        stacked = lax.dynamic_update_index_in_dim(stacked, piece, position, 0)
    return stacked


def lanes(start, size):
    return pl.ds(pl.multiple_of(start, LANE), size)


def vmem_call(kernel, outs, args, hbm=(), staged=(), scratch=(), flops=0, limit=16, away=(), weight=8):
    moved = sum(a.size * a.dtype.itemsize for a in args)
    moved += sum(math.prod(s) * jnp.dtype(t).itemsize for s, t in outs)
    whole = pl.BlockSpec(memory_space=pltpu.VMEM)
    far = pl.BlockSpec(memory_space=pltpu.HBM)
    n, m, k = len(args), len(outs), len(staged)

    def body(*refs):
        ins, rest, held, sems = list(refs[:n]), refs[n:], refs[n + m : n + m + k], refs[n + m + k]
        copies = [
            pltpu.make_async_copy(ins[i], held[j], sems.at[j]) for j, i in enumerate(staged)
        ]
        for copy in copies:
            copy.start()
        for copy in copies:
            copy.wait()
        for j, i in enumerate(staged):
            ins[i] = held[j]
        kernel(*ins, *rest[:m], *rest[m + k + 1 :])

    copied = [pltpu.VMEM(args[i].shape, args[i].dtype) for i in staged]
    if staged:
        copied.append(pltpu.SemaphoreType.DMA((k,)))
    return pl.pallas_call(
        body if staged else kernel,
        out_shape=[jax.ShapeDtypeStruct(s, t) for s, t in outs],
        in_specs=[far if i in hbm or i in staged else whole for i in range(n)],
        out_specs=[far if i in away else whole for i in range(m)],
        scratch_shapes=copied + list(scratch),
        compiler_params=pltpu.CompilerParams(vmem_limit_bytes=limit * 1024 * 1024),
        cost_estimate=pl.CostEstimate(
            flops=flops * weight, bytes_accessed=moved * weight, transcendentals=0
        ),
    )(*args)


def after(value, *others):
    return lax.optimization_barrier((value,) + others)[0]


def mesh_place():
    return lax.axis_index("rep"), lax.axis_index("fsdp"), lax.axis_index("seq")


def total(refs, read):
    return (read(refs[0]) + read(refs[1])) + (read(refs[2]) + read(refs[3]))


def pack_kernel(*refs):
    qkv, proj, x = refs[0:3]
    vectors, (packed, x_copy, held, sems) = refs[3:-4], refs[-4:]
    rep, _, core = mesh_place()
    mine = (rep * CORES + core) * LANE
    parts = [qkv.at[:, lanes(t * WIDTH + mine, LANE)] for t in range(3)]
    parts.append(proj.at[:, lanes(mine, LANE)])
    targets = [packed.at[pl.ds(0, SHARD), pl.ds(t * LANE, LANE)] for t in range(4)]
    parts += [x] * REPS
    targets += [x_copy.at[pl.ds(k * ROWS, ROWS), :] for k in range(REPS)]
    at = 0
    for v in vectors:
        parts.append(v)
        targets.append(held.at[pl.ds(at, v.shape[0])])
        at += v.shape[0]
    copies = [
        pltpu.make_async_copy(part, target, sems.at[i])
        for i, (part, target) in enumerate(zip(parts, targets))
    ]
    for copy in copies:
        copy.start()
    packed[SHARD:, SHARD:] = jnp.zeros((packed.shape[0] - SHARD, SHARD), bf16)
    for copy in copies:
        copy.wait()
    rows = [held[i * SHARD : (i + 1) * SHARD].astype(f32).reshape(1, SHARD) for i in range(8)]
    biases = [held[i * SHARD : (i + 1) * SHARD].astype(f32).reshape(1, SHARD) for i in range(8, 12)]
    rows.append(
        jnp.where(
            rep < 2,
            jnp.where(rep == 0, biases[0], biases[1]),
            jnp.where(rep == 2, biases[2], biases[3]),
        )
    )
    rows.append(jnp.zeros((16 - len(rows), SHARD), f32))
    packed[SHARD:, 0:SHARD] = jnp.concatenate(rows, 0).astype(bf16)


def unit_kernel(x, unit, scale, unit_own):
    for k in range(REPS):
        at = pl.ds(k * ROWS, ROWS)
        unit[at, :], spread = normalise(x[at, :].astype(f32))
        scale[at, :] = jnp.broadcast_to(spread, (ROWS, LANE))
    own = pl.ds(pl.multiple_of(lax.axis_index("rep") * ROWS, ROWS), ROWS)
    unit_own[0] = unit[own, :]
    unit_own[1, :, 0:LANE] = scale[own, :]
    unit_own[1, :, LANE:] = jnp.zeros((ROWS, WIDTH - LANE), f32)


def qkv_kernel(
    unit, p0, p1, p2, p3, f0, f1, f2, f3, qkv, kv_send, normed, weight, vectors, proj, biases
):
    rep, shard, core = mesh_place()
    for k, (own, far) in enumerate(((p0, f0), (p1, f1), (p2, f2), (p3, f3))):
        at = pl.ds(pl.multiple_of((shard ^ k) * SHARD, SHARD), SHARD)
        weight[at, 0:TRIPLE] = own[0:SHARD, 0:TRIPLE]
        weight[at, TRIPLE : 2 * TRIPLE] = far[0:SHARD, 0:TRIPLE]
        proj[at, :] = own[0:SHARD, TRIPLE:]
        vectors[:, at] = own[SHARD:, 0:SHARD].astype(f32)
    for p in range(CORES):
        for t, at in ((0, 0), (2, 2)):
            start = (at + rep // 2) * SHARD + (core ^ p) * LANE
            even, odd = vectors[2:3, lanes(start, LANE)], vectors[3:4, lanes(start, LANE)]
            biases[:, pl.ds(p * TRIPLE + t * LANE, LANE)] = jnp.broadcast_to(
                jnp.where(rep % 2 == 0, even, odd), (8, LANE)
            )
        biases[:, pl.ds(p * TRIPLE + LANE, LANE)] = jnp.zeros((8, LANE), f32)

    @pl.loop(0, 2)
    def _(block):
        at = pl.ds(pl.multiple_of(block * 2 * ROWS, 2 * ROWS), 2 * ROWS)
        values = (unit[at, :] * vectors[0:1, :] + vectors[1:2, :]).astype(bf16)
        normed[at, :] = values
        mixed = jnp.dot(values, weight[...], preferred_element_type=f32) + biases[0:1, :]
        mixed = mixed.astype(bf16)
        qkv[at, :] = mixed
        kv_send[at, 0 : 2 * LANE] = mixed[:, TRIPLE + LANE : 2 * TRIPLE]
        kv_send[at, 2 * LANE : 4 * LANE] = mixed[:, LANE:TRIPLE]


def dot_rows(left, right):
    return contract(left, right, 1, 1)


def head_probs(query, key_own, key_far, causal, far_seen):
    own = jnp.where(causal, dot_rows(query, key_own) * SCALE, masked_value)
    far = jnp.where(far_seen, dot_rows(query, key_far) * SCALE, masked_value)
    peak = jnp.maximum(jnp.max(own, -1, keepdims=True), jnp.max(far, -1, keepdims=True))
    own, far = jnp.exp(own - peak), jnp.exp(far - peak)
    share = 1.0 / (jnp.sum(own, -1, keepdims=True) + jnp.sum(far, -1, keepdims=True))
    return own * share, far * share


def head_masks(core):
    causal = lax.broadcasted_iota(jnp.int32, (ROWS, ROWS), 1) <= lax.broadcasted_iota(
        jnp.int32, (ROWS, ROWS), 0
    )
    far_seen = (lax.broadcasted_iota(jnp.int32, (ROWS, ROWS), 0) * 0 + core) == 1
    first = lax.broadcasted_iota(jnp.int32, (ROWS, LANE), 1) < HEAD_DIM
    return causal, far_seen, first


def attend_kernel(qkv, far, attended):
    core = lax.axis_index("seq")
    causal, far_seen, first = head_masks(core)

    for sequence in range(REPS):
        at = pl.ds(sequence * ROWS, ROWS)
        for p in range(CORES):
            base = p * TRIPLE
            query = qkv[at, base : base + LANE]
            key_own = qkv[at, base + LANE : base + 2 * LANE]
            value_own = qkv[at, base + 2 * LANE : base + 3 * LANE]
            key_far = far[at, 2 * p * LANE : (2 * p + 1) * LANE]
            value_far = far[at, (2 * p + 1) * LANE : (2 * p + 2) * LANE]
            heads = []
            for mask in (first, ~first):
                masked = jnp.where(mask, query, jnp.zeros_like(query))
                own, other = head_probs(masked, key_own, key_far, causal, far_seen)
                heads.append(
                    jnp.dot(own.astype(bf16), value_own, preferred_element_type=f32)
                    + jnp.dot(other.astype(bf16), value_far, preferred_element_type=f32)
                )
            attended[at, p * LANE : (p + 1) * LANE] = jnp.where(first, *heads).astype(bf16)


def branch_kernel(
    a, p0, p1, p2, p3, f0, f1, f2, f3, x, vectors, middle, unit, scale, normed, proj, joined
):
    rep, _, core = mesh_place()
    for k, pair in enumerate(((p0, f0), (p1, f1), (p2, f2), (p3, f3))):
        for p, piece in enumerate(pair):
            proj[:, lanes(((rep ^ k) * CORES + (core ^ p)) * LANE, LANE)] = piece[...]
    for k in range(REPS):
        for p in range(CORES):
            at = lanes((k * CORES + (core ^ p)) * LANE, LANE)
            joined[:, at] = a[k * ROWS : (k + 1) * ROWS, p * LANE : (p + 1) * LANE]
    branch = jnp.dot(joined[...], proj[...], preferred_element_type=f32)
    values = x[...].astype(f32) + branch + vectors[4:5, :]
    middle[...] = values
    norm, spread = normalise(values)
    unit[...] = norm
    scale[...] = jnp.broadcast_to(spread, (ROWS, LANE))
    low = (norm * vectors[5:6, :] + vectors[6:7, :]).astype(bf16)
    for k in range(REPS):
        normed[k * ROWS : (k + 1) * ROWS, :] = low


def hidden_kernel(h, c, ff, vectors, back, hidden, pre_grad):
    @pl.loop(0, 2)
    def _(block):
        at = pl.ds(pl.multiple_of(block * 2 * ROWS, 2 * ROWS), 2 * ROWS)
        for n in range(SHARDS):
            tile = pl.ds(n * 2 * LANE, 2 * LANE)
            pair = pl.ds(n * CORES, CORES)
            fc, out = ff[pair, 0].reshape(-1, WIDTH), ff[pair, 1].reshape(-1, WIDTH)
            preact = dot_rows(h[at, :], fc) + vectors[8:9, tile]
            value, slope = gelu_and_slope(preact)
            hidden[at, tile] = value.astype(bf16)
            grad = dot_rows(c[at, :], out)
            pre_grad[at, tile] = (grad * slope).astype(bf16)
        fc = ff[:, 0].reshape(HIDDEN, WIDTH)
        back[at, :] = jnp.dot(pre_grad[at, :], fc, preferred_element_type=f32).astype(bf16)


def weights_kernel(hidden, pre_grad, h, c, ff, output, grads, sums, held, sems):
    copies = []
    for n in range(SHARDS):
        tile = pl.ds(n * 2 * LANE, 2 * LANE)
        for i, (left, right) in enumerate(((pre_grad, h), (hidden, c))):
            grad = contract(left[:, tile], right[...], 0, 0).astype(bf16)
            for j in range(CORES):
                held[(n * CORES + j) * 2 + i] = grad[j * LANE : (j + 1) * LANE]
        part = pl.ds(n * CORES * 2, CORES * 2)
        copies.append(pltpu.make_async_copy(held.at[part], grads.at[part], sems.at[n]))
        copies[-1].start()
    sums[...] = jnp.broadcast_to(
        jnp.sum(pre_grad[...].astype(f32), 0, keepdims=True), sums.shape
    )

    @pl.loop(0, 2)
    def _(block):
        at = pl.ds(pl.multiple_of(block * 2 * ROWS, 2 * ROWS), 2 * ROWS)
        out = ff[:, 1].reshape(HIDDEN, WIDTH)
        output[at, :] = jnp.dot(hidden[at, :], out, preferred_element_type=f32).astype(bf16)

    for copy in copies:
        copy.wait()


def middle_kernel(
    g, unit, scale, vectors, cot, proj, middle_grad, pairs, sums, low, back
):
    rep, _, core = mesh_place()
    grad = total(range(REPS), lambda k: g[k * ROWS : (k + 1) * ROWS, :].astype(f32))
    part, gain, shift = norm_pull(unit[...], scale[:, 0:1], vectors[5:6, :], grad)
    cots = cot[...].astype(f32)
    values = cots + part
    middle_grad[...] = values
    branch = values.astype(bf16)
    low[...] = branch
    back[...] = dot_rows(branch, proj[...]).astype(bf16)
    rows = [jnp.sum(branch.astype(f32), 0), gain, shift, jnp.sum(cots, 0)]
    for i, row in enumerate(rows):
        sums[i : i + 1, :] = row[None]
    sums[4:8, :] = jnp.zeros((4, WIDTH), f32)
    for k in range(REPS):
        rows = pl.ds(k * ROWS, ROWS)
        for p in range(CORES):
            at = lanes((k * CORES + (core ^ p)) * LANE, LANE)
            pairs[rows, p * LANE : (p + 1) * LANE] = back[:, at]
        pairs[rows, SHARD : 2 * SHARD] = low[:, k * SHARD : (k + 1) * SHARD]


def proj_grad_kernel(a0, a1, a2, a3, pairs, own, far):
    rep, shard, core = mesh_place()
    for k, a in enumerate((a0, a1, a2, a3)):
        grad = contract(a[...], pairs[:, SHARD : 2 * SHARD], 0, 0).astype(bf16)
        mine = jnp.where(core == 0, grad[:, 0:LANE], grad[:, LANE:])
        other = jnp.where(core == 0, grad[:, LANE:], grad[:, 0:LANE])
        for p in range(CORES):
            at = pl.ds(pl.multiple_of((core ^ p) * LANE, LANE), LANE)
            own[rep ^ k ^ shard, at, :] = mine[p * LANE : (p + 1) * LANE]
            far[rep ^ k ^ shard, at, :] = other[p * LANE : (p + 1) * LANE]


def attend_back_kernel(qkv, far, pairs, query_grad, own_grad, far_grad):
    core = lax.axis_index("seq")
    causal, far_seen, first = head_masks(core)

    for sequence in range(REPS):
        at = pl.ds(sequence * ROWS, ROWS)
        for p in range(CORES):
            base = p * TRIPLE
            query = qkv[at, base : base + LANE]
            key_own = qkv[at, base + LANE : base + 2 * LANE]
            value_own = qkv[at, base + 2 * LANE : base + 3 * LANE]
            key_far = far[at, 2 * p * LANE : (2 * p + 1) * LANE]
            value_far = far[at, (2 * p + 1) * LANE : (2 * p + 2) * LANE]
            grad = pairs[at, p * LANE : (p + 1) * LANE]
            queries, sums = [], [0.0] * 4
            for mask in (first, ~first):
                masked = jnp.where(mask, query, jnp.zeros_like(query))
                back = jnp.where(mask, grad, jnp.zeros_like(grad))
                own, other = head_probs(masked, key_own, key_far, causal, far_seen)
                own_back, other_back = dot_rows(back, value_own), dot_rows(back, value_far)
                row = jnp.sum(own * own_back, -1, keepdims=True) + jnp.sum(
                    other * other_back, -1, keepdims=True
                )
                own_score = (own * (own_back - row)).astype(bf16)
                other_score = (other * (other_back - row)).astype(bf16)
                queries.append(
                    jnp.dot(own_score, key_own, preferred_element_type=f32)
                    + jnp.dot(other_score, key_far, preferred_element_type=f32)
                )
                parts = [
                    contract(own_score, masked, 0, 0) * SCALE,
                    contract(own.astype(bf16), back, 0, 0),
                    contract(other_score, masked, 0, 0) * SCALE,
                    contract(other.astype(bf16), back, 0, 0),
                ]
                sums = [a + b for a, b in zip(sums, parts)]
            query_grad[at, p * LANE : (p + 1) * LANE] = (
                jnp.where(first, *queries) * SCALE
            ).astype(bf16)
            own_at = slice(2 * p * LANE, (2 * p + 1) * LANE)
            own_grad[at, own_at] = sums[0]
            own_grad[at, (2 * p + 1) * LANE : (2 * p + 2) * LANE] = sums[1]
            q = 1 - p
            far_grad[at, 2 * q * LANE : (2 * q + 1) * LANE] = sums[2].astype(bf16)
            far_grad[at, (2 * q + 1) * LANE : (2 * q + 2) * LANE] = sums[3].astype(bf16)


def qkv_back_kernel(
    query_grad,
    own_grad,
    far_grad,
    weight,
    normed,
    unit,
    ff_sums,
    mid_sums,
    proj_own,
    proj_far,
    own,
    far,
    joined,
    small,
    mixed,
    sums,
):
    rep, shard, core = mesh_place()
    for p in range(CORES):
        base = p * TRIPLE
        mixed[:, base : base + LANE] = query_grad[:, p * LANE : (p + 1) * LANE]
        at = slice(2 * p * LANE, (2 * p + 2) * LANE)
        mixed[:, base + LANE : base + 3 * LANE] = (
            own_grad[:, at] + far_grad[:, at].astype(f32)
        ).astype(bf16)
    for k in range(SHARDS):
        at = lanes((shard ^ k) * SHARD, SHARD)
        grad = contract(normed[:, at], mixed[...], 0, 0).astype(bf16)
        own[k, :, 0:TRIPLE] = grad[:, 0:TRIPLE]
        far[k, :, 0:TRIPLE] = grad[:, TRIPLE:]
        own[k, :, TRIPLE:] = proj_own[k]
        far[k, :, TRIPLE:] = proj_far[k]
    gain = jnp.zeros((1, WIDTH), f32)
    shift = jnp.zeros((1, WIDTH), f32)
    for k in range(REPS):
        at = pl.ds(k * ROWS, ROWS)
        back = dot_rows(mixed[at, :], weight[...])
        joined[at, :] = back.astype(bf16)
        gain = gain + jnp.sum(back * unit[at, :], 0, keepdims=True)
        shift = shift + jnp.sum(back, 0, keepdims=True)
    sums[0:1, :] = gain
    sums[1:2, :] = shift
    mixed_sums = jnp.sum(mixed[...].astype(f32), 0, keepdims=True)
    for p in range(CORES):
        for i in range(2):
            start = i * SHARD + (core ^ p) * LANE
            sums[2:3, lanes(start, LANE)] = mixed_sums[
                :, p * TRIPLE + 2 * i * LANE : p * TRIPLE + (2 * i + 1) * LANE
            ]
    for k in range(SHARDS):
        small[k] = jnp.zeros(small.shape[1:], f32)
        at = lanes((shard ^ k) * SHARD, SHARD)
        small[k, 0:1, 0:SHARD] = sums[0:1, at]
        small[k, 1:2, 0:SHARD] = sums[1:2, at]
        queries = jnp.where((shard ^ k) == rep // 2, sums[2:3, 0:SHARD], 0.0)
        values = jnp.where((shard ^ k) == 2 + rep // 2, sums[2:3, SHARD : 2 * SHARD], 0.0)
        small[k, 2:3, 0:SHARD] = jnp.where(rep % 2 == 0, queries + values, 0.0)
        small[k, 3:4, 0:SHARD] = jnp.where(rep % 2 == 1, queries + values, 0.0)
        for i in range(4):
            small[k, 4 + i : 5 + i, 0:SHARD] = mid_sums[i : i + 1, at]
        part = ff_sums[:, at]
        row = lax.broadcasted_iota(jnp.int32, part.shape, 0)
        small[k, 8:16, 0:SHARD] = jnp.where(row == rep, part, 0.0)


def tail_kernel(own, far, small, o0, o1, o2, o3):
    for k, o in enumerate((o0, o1, o2, o3)):
        o[0:SHARD, :] = (own[k].astype(f32) + far[k].astype(f32)).astype(bf16)
        o[SHARD:, :] = small[k].astype(bf16)


def input_kernel(j, unit, vectors, middle_grad, grad):
    back = total(range(REPS), lambda k: j[k * ROWS : (k + 1) * ROWS, :].astype(f32))
    part, _, _ = norm_pull(unit[0], unit[1, :, 0:1], vectors[0:1, :], back)
    grad[...] = middle_grad[...] + part


def block_kernel(j, middle, vectors, block):
    output = total(range(REPS), lambda k: j[k * ROWS : (k + 1) * ROWS, :].astype(f32))
    block[...] = (middle[...] + output + vectors[7:8, :]).astype(bf16)


def joined_sum(pieces):
    pieces = [p.astype(f32) for p in pieces]
    return ((pieces[0] + pieces[1]) + (pieces[2] + pieces[3])).astype(bf16)


def final_kernel(p0, p1, p2, p3, f0, f1, f2, f3, qkv, proj, small):
    rep, _, core = mesh_place()
    for k, pair in enumerate(((p0, f0), (p1, f1), (p2, f2), (p3, f3))):
        for j, piece in enumerate(pair):
            start = ((rep ^ k) * CORES + (core ^ j)) * LANE
            for t in range(3):
                qkv[:, lanes(t * WIDTH + start, LANE)] = piece[
                    0:SHARD, t * LANE : (t + 1) * LANE
                ].astype(f32)
            proj[:, lanes(start, LANE)] = piece[0:SHARD, TRIPLE:].astype(f32)

    def read(pair):
        return pair[0][SHARD:, 0:SHARD].astype(f32) + pair[1][SHARD:, 0:SHARD].astype(f32)

    small[...] = total(((p0, f0), (p1, f1), (p2, f2), (p3, f3)), read)


def spread_kernel(p0, p1, p2, p3, f0, f1, f2, f3, fc, out):
    rep, _, core = mesh_place()
    for k, pair in enumerate(((p0, f0), (p1, f1), (p2, f2), (p3, f3))):
        for j, piece in enumerate(pair):
            at = pl.ds(pl.multiple_of(((rep ^ k) * CORES + (core ^ j)) * LANE, LANE), LANE)
            fc[at, :] = piece[0].astype(f32)
            out[at, :] = piece[1].astype(f32)


def tiled_body(
    block_input,
    ln1_gain,
    ln1_shift,
    qkv_weight,
    qv_bias,
    proj_weight,
    proj_bias,
    ln2_gain,
    ln2_shift,
    fc_weight,
    fc_bias,
    out_weight,
    out_bias,
    cotangent,
):
    rep, _, core = mesh_place()

    def over_rep(pieces):
        return [swap(p, "rep", REPS, k) if k else p for k, p in enumerate(pieces)]

    def over_shards(pieces):
        return [swap(p, "fsdp", SHARDS, k) if k else p for k, p in enumerate(pieces)]

    def over_cores(value):
        return swap(value, "seq", CORES, 1)

    all_rows = REPS * ROWS
    vectors = [
        ln1_gain,
        ln1_shift,
        qv_bias,
        proj_bias,
        ln2_gain,
        ln2_shift,
        out_bias,
        fc_bias,
    ]
    packed, own_rows = vmem_call(
        pack_kernel,
        [((SHARD + 16, TRIPLE + LANE), bf16), ((all_rows, WIDTH), bf16)],
        [qkv_weight, proj_weight, block_input] + vectors,
        hbm=tuple(range(11)),
        scratch=[pltpu.VMEM((12 * SHARD,), bf16), pltpu.SemaphoreType.DMA((16,))],
        limit=56,
    )
    own_packed = over_shards([packed] * SHARDS)
    far_packed = [over_cores(p) for p in own_packed]
    inputs = lax.all_to_all(own_rows, "rep", 0, 0, tiled=True)

    unit_one, _, unit_own = vmem_call(
        unit_kernel,
        [((all_rows, WIDTH), f32), ((all_rows, LANE), f32), ((2, ROWS, WIDTH), f32)],
        [inputs],
    )
    cots = lax.all_gather(cotangent, "rep", axis=0, tiled=True)

    mine = rep * CORES + core
    ff = [pick(w.reshape(REPS * CORES, LANE, WIDTH), mine, 0) for w in (fc_weight, out_weight)]
    ff = after(jnp.stack(ff), *own_packed[1:], inputs)
    ff = lax.all_gather(ff, ("fsdp", "seq"), axis=0)

    qkv, kv_send, normed_one, qkv_mine, vectors, proj_cols = vmem_call(
        qkv_kernel,
        [
            ((all_rows, 2 * TRIPLE), bf16),
            ((all_rows, 4 * LANE), bf16),
            ((all_rows, WIDTH), bf16),
            ((WIDTH, 2 * TRIPLE), bf16),
            ((16, WIDTH), f32),
            ((WIDTH, LANE), bf16),
        ],
        [unit_one] + own_packed + far_packed,
        scratch=[pltpu.VMEM((8, 2 * TRIPLE), f32)],
        flops=2 * all_rows * WIDTH * 2 * TRIPLE,
    )
    kv_far = over_cores(kv_send)
    proj_cols = over_rep([proj_cols] * REPS)
    (attended,) = vmem_call(
        attend_kernel,
        [((all_rows, SHARD), bf16)],
        [qkv, kv_far],
        flops=4 * all_rows * 2 * ROWS * SHARD,
    )
    mine = lax.all_to_all(attended, "rep", 0, 0, tiled=True)
    marker = over_cores(attended[:16, :LANE])
    middle, unit_two, scale_two, normed_two, proj_full = vmem_call(
        branch_kernel,
        [
            ((ROWS, WIDTH), f32),
            ((ROWS, WIDTH), f32),
            ((ROWS, LANE), f32),
            ((all_rows, WIDTH), bf16),
            ((WIDTH, WIDTH), bf16),
        ],
        [mine]
        + proj_cols
        + [over_cores(after(p, marker)) for p in proj_cols]
        + [block_input, vectors],
        scratch=[pltpu.VMEM((ROWS, WIDTH), bf16)],
        flops=2 * ROWS * WIDTH * WIDTH,
    )
    normed_two = lax.all_to_all(normed_two, "rep", 0, 0, tiled=True)
    attended_all = over_rep([after(attended, normed_two)] * REPS)

    back, hidden, pre_grad = vmem_call(
        hidden_kernel,
        [
            ((all_rows, WIDTH), bf16),
            ((all_rows, HIDDEN), bf16),
            ((all_rows, HIDDEN), bf16),
        ],
        [normed_two, cots, ff, vectors],
        flops=6 * all_rows * WIDTH * HIDDEN,
    )
    back = lax.all_to_all(back, "rep", 0, 0, tiled=True)
    output, ff_grads, ff_sums = vmem_call(
        weights_kernel,
        [
            ((all_rows, WIDTH), bf16),
            ((SHARDS * CORES * 2, LANE, WIDTH), bf16),
            ((8, HIDDEN), f32),
        ],
        [after(hidden, *attended_all[1:]), pre_grad, normed_two, cots, ff],
        scratch=[
            pltpu.VMEM((SHARDS * CORES * 2, LANE, WIDTH), bf16),
            pltpu.SemaphoreType.DMA((SHARDS,)),
        ],
        away=(1,),
        flops=6 * all_rows * WIDTH * HIDDEN,
    )
    ff_piece = lax.psum_scatter(ff_grads, ("fsdp", "seq"), scatter_dimension=0, tiled=True)

    middle_grad, pairs, mid_sums = vmem_call(
        middle_kernel,
        [((ROWS, WIDTH), f32), ((all_rows, 2 * SHARD), bf16), ((8, WIDTH), f32)],
        [back, unit_two, scale_two, vectors, cotangent, proj_full],
        scratch=[pltpu.VMEM((ROWS, WIDTH), bf16)] * 2,
        flops=2 * ROWS * WIDTH * WIDTH,
    )
    pairs = lax.all_to_all(pairs, "rep", 0, 0, tiled=True)
    output = lax.all_to_all(after(output, pairs), "rep", 0, 0, tiled=True)
    (block_output,) = vmem_call(block_kernel, [((ROWS, WIDTH), bf16)], [output, middle, vectors])
    query_grad, own_grad, far_grad = vmem_call(
        attend_back_kernel,
        [
            ((all_rows, SHARD), bf16),
            ((all_rows, 4 * LANE), f32),
            ((all_rows, 4 * LANE), bf16),
        ],
        [qkv, kv_far, pairs],
        weight=1,
        flops=10 * all_rows * 2 * ROWS * SHARD,
    )
    proj_own, proj_far = vmem_call(
        proj_grad_kernel,
        [((SHARDS, SHARD, LANE), bf16)] * 2,
        attended_all + [pairs],
        flops=2 * all_rows * WIDTH * SHARD,
    )
    qkv_own, qkv_far, joined, small = vmem_call(
        qkv_back_kernel,
        [
            ((SHARDS, SHARD, TRIPLE + LANE), bf16),
            ((SHARDS, SHARD, TRIPLE + LANE), bf16),
            ((all_rows, WIDTH), bf16),
            ((SHARDS, 16, TRIPLE + LANE), f32),
        ],
        [query_grad, own_grad, over_cores(far_grad), qkv_mine, normed_one, unit_one, ff_sums, mid_sums]
        + [proj_own, proj_far],
        scratch=[pltpu.VMEM((all_rows, 2 * TRIPLE), bf16), pltpu.VMEM((8, WIDTH), f32)],
        flops=4 * all_rows * WIDTH * 2 * TRIPLE,
    )
    tail = vmem_call(
        tail_kernel,
        [((SHARD + 16, TRIPLE + LANE), bf16)] * SHARDS,
        [qkv_own, over_cores(qkv_far), small],
    )
    tail = over_shards(tail)
    joined = lax.all_to_all(joined, "rep", 0, 0, tiled=True)
    ff_pieces = over_rep([ff_piece] * REPS)
    tail = joined_sum([after(tail[0], joined, block_output, *ff_pieces[1:])] + tail[1:])
    (input_grad,) = vmem_call(
        input_kernel, [((ROWS, WIDTH), f32)], [joined, unit_own, vectors, middle_grad]
    )
    whole_tail, tail = tail, over_rep([tail] * REPS)
    fc_grads, out_grads = vmem_call(
        spread_kernel,
        [((2 * REPS * LANE, WIDTH), f32)] * 2,
        ff_pieces + [over_cores(after(p, whole_tail)) for p in ff_pieces],
    )
    qkv_grads, proj_grads, small = vmem_call(
        final_kernel,
        [((SHARD, 3 * WIDTH), f32), ((SHARD, WIDTH), f32), ((16, SHARD), f32)],
        [after(tail[0], fc_grads)] + tail[1:] + [over_cores(t) for t in tail],
    )
    return (
        block_output,
        input_grad,
        small[0],
        small[1],
        qkv_grads,
        small[2:4].reshape(-1),
        proj_grads,
        small[4],
        small[5],
        small[6],
        fc_grads,
        small[8:12].reshape(-1),
        out_grads,
        small[7],
    )


def make_body(reps, shards, cores):
    def rep_swap(value, offset):
        return swap(value, "rep", reps, offset) if offset else value

    def shard_swap(value, offset):
        return swap(value, "fsdp", shards, offset) if offset else value

    def core_swap(value):
        return swap(value, "seq", cores, 1)

    def plane_gather(value):
        return [rep_swap(value, k) for k in range(reps)]

    def plane_exchange(pieces):
        return [rep_swap(piece, k) for k, piece in enumerate(pieces)]

    def pair_sum(pieces):
        while len(pieces) > 1:
            pieces = [pieces[i] + pieces[i + 1] for i in range(0, len(pieces), 2)]
        return pieces[0]

    def own_scatter(parts):
        core = lax.axis_index("seq")
        shard = lax.axis_index("fsdp")
        kept = pick(parts, core, 1).astype(f32)
        kept = (kept + core_swap(pick(parts, 1 - core, 1)).astype(f32)).astype(bf16)
        pieces = [shard_swap(pick(kept, shard ^ k, 0), k).astype(f32) for k in range(shards)]
        return pair_sum(pieces).astype(bf16)

    def place_both(pieces):
        core = lax.axis_index("seq")
        rep = lax.axis_index("rep")
        held = jnp.zeros((reps, cores) + pieces[0].shape, pieces[0].dtype)
        zeros = (0,) * pieces[0].ndim
        for k, piece in enumerate(pieces):
            held = lax.dynamic_update_slice(held, piece[None, None], (rep ^ k, core) + zeros)
            far = core_swap(piece)
            held = lax.dynamic_update_slice(held, far[None, None], (rep ^ k, 1 - core) + zeros)
        return held

    def body(
        block_input,
        ln1_gain,
        ln1_shift,
        qkv_weight,
        qv_bias,
        proj_weight,
        proj_bias,
        ln2_gain,
        ln2_shift,
        fc_weight,
        fc_bias,
        out_weight,
        out_bias,
        cotangent,
    ):
        rows, width = block_input.shape
        shard_width = width // shards
        part = width // (reps * cores)
        rep_width = part * cores
        hidden_part = fc_weight.shape[0] // (reps * cores)
        head_scale = HEAD_DIM ** (-0.5)
        rep = lax.axis_index("rep")
        shard = lax.axis_index("fsdp")
        core = lax.axis_index("seq")
        rep_at = [rep ^ k for k in range(reps)]
        shard_at = [shard ^ k for k in range(shards)]

        columns = qkv_weight.reshape(shard_width, 3, reps, cores, part)
        columns = pick(pick(columns, rep, 2), core, 2).reshape(shard_width, 3 * part)
        fc_bias_part = pick(fc_bias.reshape(reps, -1), rep, 0)
        vectors = [
            ln1_gain,
            ln1_shift,
            qv_bias[:shard_width],
            qv_bias[shard_width:],
            proj_bias,
            ln2_gain,
            ln2_shift,
            out_bias,
            fc_bias_part,
        ]
        vectors = [jnp.pad(v, (0, 3 * part - v.shape[0])) for v in vectors]
        vectors = jnp.stack(vectors + [jnp.zeros_like(vectors[0])] * (16 - len(vectors)))
        packed = jnp.concatenate([columns, vectors], 0)
        packed, own_rows = lax.optimization_barrier((packed, block_input))
        packed = place([shard_swap(packed, k) for k in range(shards)], shard_at)
        inputs_all = jnp.concatenate(plane_gather(own_rows), 0)
        columns = packed[:, :shard_width].reshape(width, 3 * part)
        vectors = packed[:, shard_width:, :].astype(f32)

        def vector(index, size):
            return vectors[:, index, :size].reshape(-1)

        gain_one, shift_one = vector(0, shard_width), vector(1, shard_width)
        qv_full = jnp.stack([vectors[:, 2, :shard_width], vectors[:, 3, :shard_width]], 1)
        qv_full = qv_full.reshape(2, reps, cores * part)
        proj_bias_full = vector(4, shard_width)
        gain_two, shift_two = vector(5, shard_width), vector(6, shard_width)
        out_bias_full = vector(7, shard_width)
        fc_bias_mine = vector(8, fc_bias_part.shape[0])
        qkv_mine = place([columns, core_swap(columns)], [core, 1 - core])
        qkv_mine = jnp.transpose(qkv_mine, (1, 0, 2)).reshape(width, cores * 3 * part)

        proj_part = pick(proj_weight.reshape(reps * cores, -1, width), rep * cores + core, 0)
        proj_full = lax.all_gather(proj_part, ("rep", "fsdp", "seq"), axis=0)
        proj_full = proj_full.reshape((reps, shards, cores) + proj_part.shape)
        proj_full = jnp.transpose(proj_full, (1, 0, 2, 3, 4)).reshape(width, width)

        fc_part = pick(fc_weight.reshape(reps * cores, hidden_part, width), rep * cores + core, 0)
        out_part = pick(out_weight.reshape(reps * cores, hidden_part, width), rep * cores + core, 0)
        both_part = jnp.stack([fc_part, out_part])
        both_part, packed = lax.optimization_barrier((both_part, packed))
        both = place([shard_swap(both_part, k) for k in range(shards)], shard_at)
        both = place([both, core_swap(both)], [core, 1 - core])
        fc_mine = jnp.transpose(both[:, :, 0], (1, 0, 2, 3)).reshape(-1, width)
        out_mine = jnp.transpose(both[:, :, 1], (1, 0, 2, 3)).reshape(-1, width)

        own_cot, inputs_all = lax.optimization_barrier((cotangent, inputs_all))
        cot_all = jnp.concatenate(plane_gather(own_cot), 0)

        unit_one, scale_one = normalise(inputs_all.astype(f32))
        normed_all = (unit_one * gain_one + shift_one).astype(bf16)
        mixed = jnp.dot(normed_all, qkv_mine, preferred_element_type=f32)
        mixed = mixed.reshape(reps, rows, cores, 3, part)
        qv_mine = pick(qv_full, rep, 1).reshape(2, cores, part)
        heads = (reps, rows, rep_width // HEAD_DIM, HEAD_DIM)
        queries = (mixed[:, :, :, 0] + qv_mine[0]).astype(bf16).reshape(heads)
        keys = mixed[:, :, :, 1].astype(bf16).reshape(heads)
        values = (mixed[:, :, :, 2] + qv_mine[1]).astype(bf16).reshape(heads)
        far_pair = core_swap(jnp.stack([keys, values]))
        keys_both = jnp.concatenate([keys, far_pair[0]], 1)
        values_both = jnp.concatenate([values, far_pair[1]], 1)

        row_pos = lax.broadcasted_iota(jnp.int32, (rows, 2 * rows), 0)
        col_pos = lax.broadcasted_iota(jnp.int32, (rows, 2 * rows), 1)
        allowed = jnp.where(col_pos < rows, col_pos <= row_pos, core == 1)
        scores = jnp.einsum("sqhd,skhd->shqk", queries, keys_both, preferred_element_type=f32)
        scores = jnp.where(allowed, scores * head_scale, masked_value)
        peak = jnp.max(scores, -1, keepdims=True)
        powers = jnp.exp(scores - peak)
        probs = powers / jnp.sum(powers, -1, keepdims=True)
        probs_low = probs.astype(bf16)
        attended = jnp.einsum("shqk,skhd->sqhd", probs_low, values_both, preferred_element_type=f32)
        attended_low = attended.astype(bf16).reshape(reps, rows, rep_width)
        mine = place(plane_exchange([attended_low[k] for k in range(reps)]), rep_at)
        mine = jnp.transpose(mine, (1, 0, 2)).reshape(rows, width)
        middle = (
            block_input.astype(f32)
            + jnp.dot(mine, proj_full, preferred_element_type=f32)
            + proj_bias_full
        )
        unit_two, scale_two = normalise(middle)
        normed_two = (unit_two * gain_two + shift_two).astype(bf16)
        normed_two_all = jnp.concatenate(plane_gather(normed_two), 0)

        attended_all = place([attended_low[k] for k in range(reps)], rep_at)
        attended_all = lax.all_gather(attended_all.reshape(reps * rows, rep_width), "rep", axis=0)
        attended_all = jnp.transpose(attended_all, (1, 0, 2)).reshape(reps * rows, width)

        hidden_grad = contract(cot_all, out_mine, 1, 1)
        preact = contract(normed_two_all, fc_mine, 1, 1) + fc_bias_mine
        hidden, slope = gelu_and_slope(preact)
        hidden_low = hidden.astype(bf16)
        pre_grad = (hidden_grad * slope).astype(bf16)
        normed_grad = jnp.dot(pre_grad, fc_mine, preferred_element_type=f32).astype(bf16)
        normed_grad = normed_grad.reshape(reps, rows, width)
        normed_grad = plane_exchange([normed_grad[k] for k in range(reps)])
        normed_grad = pair_sum([v.astype(f32) for v in normed_grad])
        output = jnp.dot(hidden_low, out_mine, preferred_element_type=f32).astype(bf16)
        output, normed_grad = lax.optimization_barrier((output, normed_grad))
        output = output.reshape(reps, rows, width)
        output = plane_exchange([output[k] for k in range(reps)])
        output = pair_sum([v.astype(f32) for v in output])
        block_output = (middle + output + out_bias_full).astype(bf16)

        out_grads = contract(hidden_low, cot_all, 0, 0).astype(bf16)
        out_grads = lax.psum_scatter(out_grads, ("fsdp", "seq"), scatter_dimension=0, tiled=True)
        fc_grads = contract(pre_grad, normed_two_all, 0, 0).astype(bf16)
        fc_grads = own_scatter(fc_grads.reshape(shards, cores, hidden_part, width))
        ff_grads = plane_gather(jnp.stack([fc_grads, out_grads]))
        ff_grads = place_both(ff_grads)
        fc_grads = ff_grads[:, :, 0].reshape(-1, width).astype(f32)
        out_grads = ff_grads[:, :, 1].reshape(-1, width).astype(f32)

        middle_part, gain_two_grads, shift_two_grads = norm_pull(
            unit_two, scale_two, gain_two, normed_grad
        )
        middle_grad = cotangent.astype(f32) + middle_part
        branch_grad = middle_grad.astype(bf16)
        attended_grad = contract(branch_grad, proj_full, 1, 1).astype(bf16)
        pair = [v.reshape(rows, reps, rep_width) for v in (attended_grad, branch_grad)]
        pair = jnp.concatenate(pair, 2)
        pair = plane_exchange([pick(pair, i, 1) for i in rep_at])
        attended_grad = jnp.stack([v[:, :rep_width] for v in pair]).reshape(heads)
        branch_cols = place([v[:, rep_width:] for v in pair], rep_at).reshape(-1, rep_width)
        proj_grads = contract(attended_all, branch_cols, 0, 0).astype(bf16)
        proj_grads = proj_grads.reshape(shards, shard_width, cores, part)
        proj_grads = jnp.transpose(proj_grads, (0, 2, 1, 3)).reshape(-1, part)
        proj_grads = lax.psum_scatter(proj_grads, ("fsdp", "seq"), scatter_dimension=0, tiled=True)
        proj_grads = lax.all_gather(proj_grads, ("rep", "seq"), axis=0)
        proj_grads = jnp.transpose(proj_grads, (1, 0, 2)).reshape(shard_width, width).astype(f32)

        prob_grad = jnp.einsum("sqhd,skhd->shqk", attended_grad, values_both, preferred_element_type=f32)
        row_total = jnp.sum(probs * prob_grad, -1, keepdims=True)
        score_low = (probs * (prob_grad - row_total)).astype(bf16)
        query_grad = (
            jnp.einsum("shqk,skhd->sqhd", score_low, keys_both, preferred_element_type=f32)
            * head_scale
        )
        key_grad = (
            jnp.einsum("shqk,sqhd->skhd", score_low, queries, preferred_element_type=f32)
            * head_scale
        )
        value_grad = jnp.einsum("shqk,sqhd->skhd", probs_low, attended_grad, preferred_element_type=f32)
        far_grads = core_swap(jnp.stack([key_grad[:, rows:], value_grad[:, rows:]]).astype(bf16))
        key_grad = key_grad[:, :rows] + far_grads[0].astype(f32)
        value_grad = value_grad[:, :rows] + far_grads[1].astype(f32)
        mixed_grad = jnp.stack(
            [
                g.astype(bf16).reshape(reps * rows, cores, part)
                for g in (query_grad, key_grad, value_grad)
            ],
            2,
        ).reshape(reps * rows, cores * 3 * part)
        qkv_grads = contract(normed_all, mixed_grad, 0, 0).astype(bf16)
        normed_one_grad = contract(mixed_grad, qkv_mine, 1, 1)
        joined = normed_one_grad.astype(bf16).reshape(reps, rows, width)
        joined = plane_exchange([joined[k] for k in range(reps)])
        joined = pair_sum([v.astype(f32) for v in joined])
        input_part = norm_pull(unit_one[:rows], scale_one[:rows], gain_one, joined)[0]
        input_grad = middle_grad + input_part

        gain_one_grads = jnp.sum(normed_one_grad * unit_one, 0)
        shift_one_grads = jnp.sum(normed_one_grad, 0)
        mixed_sums = jnp.sum(mixed_grad.astype(f32), 0).reshape(cores, 3, part)
        qv_sums = jnp.stack([mixed_sums[:, 0].reshape(-1), mixed_sums[:, 2].reshape(-1)])
        qv_sums = lax.dynamic_update_index_in_dim(
            jnp.zeros((2, reps, rep_width), f32), qv_sums, rep, 1
        )
        fc_sums = jnp.sum(pre_grad.astype(f32), 0).reshape(shards, -1)
        fc_sums = lax.dynamic_update_index_in_dim(
            jnp.zeros((shards, reps, fc_sums.shape[1]), f32), fc_sums, rep, 1
        )
        small = [
            gain_one_grads,
            shift_one_grads,
            qv_sums,
            jnp.sum(branch_grad.astype(f32), 0),
            gain_two_grads,
            shift_two_grads,
            jnp.sum(cotangent.astype(f32), 0),
            fc_sums,
        ]
        small = jnp.concatenate([v.reshape(shards, -1) for v in small], 1).astype(bf16)
        small_size = small.shape[1]
        small_rows = -(-small_size // (16 * 3 * part)) * 16
        small = jnp.pad(small, ((0, 0), (0, small_rows * 3 * part - small_size)))
        small = small.reshape(shards, small_rows, 3 * part)

        qkv_grads = qkv_grads.reshape(shards, shard_width, cores, 3 * part)
        tail = pick(qkv_grads, core, 2).astype(f32)
        tail = (tail + core_swap(pick(qkv_grads, 1 - core, 2)).astype(f32)).astype(bf16)
        tail = jnp.concatenate([tail, small], 1)
        tail = [shard_swap(pick(tail, i, 0), k).astype(f32) for k, i in enumerate(shard_at)]
        tail = place_both(plane_gather(pair_sum(tail).astype(bf16)))
        qkv_grads = tail[:, :, :shard_width].reshape(reps * cores, shard_width, 3, part)
        qkv_grads = jnp.transpose(qkv_grads, (1, 2, 0, 3)).reshape(shard_width, 3 * width)
        qkv_grads = qkv_grads.astype(f32)
        small = jnp.sum(tail[:, :, shard_width:].astype(f32), (0, 1)).reshape(-1)
        sizes = [1, 1, 2, 1, 1, 1, 1]
        ends = [0]
        for size in sizes:
            ends.append(ends[-1] + size * shard_width)
        one = [small[a:b] for a, b in zip(ends[:-1], ends[1:])] + [small[ends[-1] : small_size]]
        return (
            block_output,
            input_grad,
            one[0],
            one[1],
            qkv_grads,
            one[2],
            proj_grads,
            one[3],
            one[4],
            one[5],
            fc_grads,
            one[7],
            out_grads,
            one[6],
        )

    return body


def solution(mesh):
    line, block = P("fsdp"), P("fsdp", None)
    tokens = P(("rep", "fsdp", "seq"), None)
    in_specs = (
        tokens,
        line,
        line,
        block,
        line,
        block,
        line,
        line,
        line,
        block,
        line,
        block,
        line,
        tokens,
    )
    out_specs = (
        tokens,
        tokens,
        line,
        line,
        block,
        line,
        block,
        line,
        line,
        line,
        block,
        line,
        block,
        line,
    )
    sizes = mesh.shape["rep"], mesh.shape["fsdp"], mesh.shape["seq"]
    general = make_body(*sizes)

    def body(*args):
        tiled = sizes == (REPS, SHARDS, CORES) and args[0].shape == (ROWS, WIDTH)
        return tiled_body(*args) if tiled else general(*args)

    return jax.shard_map(body, mesh=mesh, in_specs=in_specs, out_specs=out_specs, check_vma=False)
```

```python
import math

import jax
import jax.numpy as jnp
from jax import lax
from jax.experimental import pallas as pl
from jax.experimental.pallas import tpu as pltpu
from jax.sharding import PartitionSpec as P

HEADS = 16
HEAD_DIM = 64

norm_eps = 1e-05
masked_value = -1e30
f32 = jnp.float32
bf16 = jnp.bfloat16

REPS, SHARDS, CORES = 4, 4, 2
LANE, ROWS, WIDTH, SHARD, TRIPLE, HIDDEN = 128, 128, 1024, 256, 384, 1024
SCALE = HEAD_DIM ** (-0.5)


def normalise(values):
    centre = jnp.mean(values, -1, keepdims=True)
    offsets = values - centre
    spread = jnp.mean(offsets * offsets, -1, keepdims=True)
    scale = lax.rsqrt(spread + norm_eps)
    return offsets * scale, scale


def norm_pull(unit, scale, gain, grad):
    inner = grad * gain
    first = jnp.mean(inner, -1, keepdims=True)
    second = jnp.mean(inner * unit, -1, keepdims=True)
    return scale * (inner - first - unit * second), jnp.sum(grad * unit, 0), jnp.sum(grad, 0)


def gelu_and_slope(values):
    rate = 0.7978845608028654
    squared = values * values
    bent = jnp.tanh(rate * (values + 0.044715 * values * squared))
    half = 0.5 * (1.0 + bent)
    slope = half + 0.5 * values * (1.0 - bent * bent) * (rate * (1.0 + 3.0 * 0.044715 * squared))
    return values * half, slope


def contract(left, right, left_axis, right_axis):
    return lax.dot_general(
        left, right, (((left_axis,), (right_axis,)), ((), ())), preferred_element_type=f32
    )


def swap(value, axis, size, offset):
    return lax.ppermute(value, axis, [(i, i ^ offset) for i in range(size)])


def pick(array, index, axis):
    return lax.dynamic_index_in_dim(array, index, axis, keepdims=False)


def place(pieces, positions):
    stacked = jnp.zeros((len(pieces),) + pieces[0].shape, pieces[0].dtype)
    for piece, position in zip(pieces, positions):
        stacked = lax.dynamic_update_index_in_dim(stacked, piece, position, 0)
    return stacked


def lanes(start, size):
    return pl.ds(pl.multiple_of(start, LANE), size)


def vmem_call(kernel, outs, args, hbm=(), staged=(), scratch=(), flops=0, limit=16, away=(), weight=8):
    moved = sum(a.size * a.dtype.itemsize for a in args)
    moved += sum(math.prod(s) * jnp.dtype(t).itemsize for s, t in outs)
    whole = pl.BlockSpec(memory_space=pltpu.VMEM)
    far = pl.BlockSpec(memory_space=pltpu.HBM)
    n, m, k = len(args), len(outs), len(staged)

    def body(*refs):
        ins, rest, held, sems = list(refs[:n]), refs[n:], refs[n + m : n + m + k], refs[n + m + k]
        copies = [
            pltpu.make_async_copy(ins[i], held[j], sems.at[j]) for j, i in enumerate(staged)
        ]
        for copy in copies:
            copy.start()
        for copy in copies:
            copy.wait()
        for j, i in enumerate(staged):
            ins[i] = held[j]
        kernel(*ins, *rest[:m], *rest[m + k + 1 :])

    copied = [pltpu.VMEM(args[i].shape, args[i].dtype) for i in staged]
    if staged:
        copied.append(pltpu.SemaphoreType.DMA((k,)))
    return pl.pallas_call(
        body if staged else kernel,
        out_shape=[jax.ShapeDtypeStruct(s, t) for s, t in outs],
        in_specs=[far if i in hbm or i in staged else whole for i in range(n)],
        out_specs=[far if i in away else whole for i in range(m)],
        scratch_shapes=copied + list(scratch),
        compiler_params=pltpu.CompilerParams(vmem_limit_bytes=limit * 1024 * 1024),
        cost_estimate=pl.CostEstimate(
            flops=flops * weight, bytes_accessed=moved * weight, transcendentals=0
        ),
    )(*args)


def after(value, *others):
    return lax.optimization_barrier((value,) + others)[0]


def mesh_place():
    return lax.axis_index("rep"), lax.axis_index("fsdp"), lax.axis_index("seq")


def total(refs, read):
    return (read(refs[0]) + read(refs[1])) + (read(refs[2]) + read(refs[3]))


def pack_kernel(*refs):
    qkv, proj, x = refs[0:3]
    vectors, (packed, x_copy, held, sems) = refs[3:-4], refs[-4:]
    rep, _, core = mesh_place()
    mine = (rep * CORES + core) * LANE
    parts = [qkv.at[:, lanes(t * WIDTH + mine, LANE)] for t in range(3)]
    parts.append(proj.at[:, lanes(mine, LANE)])
    targets = [packed.at[pl.ds(0, SHARD), pl.ds(t * LANE, LANE)] for t in range(4)]
    parts += [x] * REPS
    targets += [x_copy.at[pl.ds(k * ROWS, ROWS), :] for k in range(REPS)]
    at = 0
    for v in vectors:
        parts.append(v)
        targets.append(held.at[pl.ds(at, v.shape[0])])
        at += v.shape[0]
    copies = [
        pltpu.make_async_copy(part, target, sems.at[i])
        for i, (part, target) in enumerate(zip(parts, targets))
    ]
    for copy in copies:
        copy.start()
    packed[SHARD:, SHARD:] = jnp.zeros((packed.shape[0] - SHARD, SHARD), bf16)
    for copy in copies:
        copy.wait()
    rows = [held[i * SHARD : (i + 1) * SHARD].astype(f32).reshape(1, SHARD) for i in range(8)]
    biases = [held[i * SHARD : (i + 1) * SHARD].astype(f32).reshape(1, SHARD) for i in range(8, 12)]
    rows.append(
        jnp.where(
            rep < 2,
            jnp.where(rep == 0, biases[0], biases[1]),
            jnp.where(rep == 2, biases[2], biases[3]),
        )
    )
    rows.append(jnp.zeros((16 - len(rows), SHARD), f32))
    packed[SHARD:, 0:SHARD] = jnp.concatenate(rows, 0).astype(bf16)


def unit_kernel(x, unit, scale, unit_own):
    for k in range(REPS):
        at = pl.ds(k * ROWS, ROWS)
        unit[at, :], spread = normalise(x[at, :].astype(f32))
        scale[at, :] = jnp.broadcast_to(spread, (ROWS, LANE))
    own = pl.ds(pl.multiple_of(lax.axis_index("rep") * ROWS, ROWS), ROWS)
    unit_own[0] = unit[own, :]
    unit_own[1, :, 0:LANE] = scale[own, :]
    unit_own[1, :, LANE:] = jnp.zeros((ROWS, WIDTH - LANE), f32)


def qkv_kernel(
    unit, p0, p1, p2, p3, f0, f1, f2, f3, qkv, kv_send, normed, weight, vectors, proj, biases
):
    rep, shard, core = mesh_place()
    for k, (own, far) in enumerate(((p0, f0), (p1, f1), (p2, f2), (p3, f3))):
        at = pl.ds(pl.multiple_of((shard ^ k) * SHARD, SHARD), SHARD)
        weight[at, 0:TRIPLE] = own[0:SHARD, 0:TRIPLE]
        weight[at, TRIPLE : 2 * TRIPLE] = far[0:SHARD, 0:TRIPLE]
        proj[at, :] = own[0:SHARD, TRIPLE:]
        vectors[:, at] = own[SHARD:, 0:SHARD].astype(f32)
    for p in range(CORES):
        for t, at in ((0, 0), (2, 2)):
            start = (at + rep // 2) * SHARD + (core ^ p) * LANE
            even, odd = vectors[2:3, lanes(start, LANE)], vectors[3:4, lanes(start, LANE)]
            biases[:, pl.ds(p * TRIPLE + t * LANE, LANE)] = jnp.broadcast_to(
                jnp.where(rep % 2 == 0, even, odd), (8, LANE)
            )
        biases[:, pl.ds(p * TRIPLE + LANE, LANE)] = jnp.zeros((8, LANE), f32)

    @pl.loop(0, 2)
    def _(block):
        at = pl.ds(pl.multiple_of(block * 2 * ROWS, 2 * ROWS), 2 * ROWS)
        values = (unit[at, :] * vectors[0:1, :] + vectors[1:2, :]).astype(bf16)
        normed[at, :] = values
        mixed = jnp.dot(values, weight[...], preferred_element_type=f32) + biases[0:1, :]
        mixed = mixed.astype(bf16)
        qkv[at, :] = mixed
        kv_send[at, 0 : 2 * LANE] = mixed[:, TRIPLE + LANE : 2 * TRIPLE]
        kv_send[at, 2 * LANE : 4 * LANE] = mixed[:, LANE:TRIPLE]


def dot_rows(left, right):
    return contract(left, right, 1, 1)


def head_scores(query, key_own, key_far, causal, far_seen):
    own = jnp.where(causal, dot_rows(query, key_own) * SCALE, masked_value)
    far = jnp.where(far_seen, dot_rows(query, key_far) * SCALE, masked_value)
    return own, far


def head_masks(core):
    causal = lax.broadcasted_iota(jnp.int32, (ROWS, ROWS), 1) <= lax.broadcasted_iota(
        jnp.int32, (ROWS, ROWS), 0
    )
    far_seen = (lax.broadcasted_iota(jnp.int32, (ROWS, ROWS), 0) * 0 + core) == 1
    first = lax.broadcasted_iota(jnp.int32, (ROWS, LANE), 1) < HEAD_DIM
    return causal, far_seen, first


def attend_kernel(qkv, far, attended, logs):
    core = lax.axis_index("seq")
    causal, far_seen, first = head_masks(core)
    lane = lax.broadcasted_iota(jnp.int32, (ROWS, LANE), 1)

    for sequence in range(REPS):
        at = pl.ds(sequence * ROWS, ROWS)
        for p in range(CORES):
            base = p * TRIPLE
            query = qkv[at, base : base + LANE]
            key_own = qkv[at, base + LANE : base + 2 * LANE]
            value_own = qkv[at, base + 2 * LANE : base + 3 * LANE]
            key_far = far[at, 2 * p * LANE : (2 * p + 1) * LANE]
            value_far = far[at, (2 * p + 1) * LANE : (2 * p + 2) * LANE]
            heads = []
            for h, mask in enumerate((first, ~first)):
                masked = jnp.where(mask, query, jnp.zeros_like(query))
                own, other = head_scores(masked, key_own, key_far, causal, far_seen)
                peak = jnp.max(jnp.maximum(own, other), -1, keepdims=True)
                own, other = jnp.exp(own - peak), jnp.exp(other - peak)
                whole = jnp.sum(own + other, -1, keepdims=True)
                share = 1.0 / whole
                own, other = own * share, other * share
                log = jnp.broadcast_to(peak + jnp.log(whole), (ROWS, LANE))
                kept = log if p + h == 0 else jnp.where(lane == 2 * p + h, log, kept)
                heads.append(
                    jnp.dot(own.astype(bf16), value_own, preferred_element_type=f32)
                    + jnp.dot(other.astype(bf16), value_far, preferred_element_type=f32)
                )
            if p == CORES - 1:
                logs[at, :] = kept
            attended[at, p * LANE : (p + 1) * LANE] = jnp.where(first, *heads).astype(bf16)


def branch_kernel(
    a, p0, p1, p2, p3, f0, f1, f2, f3, x, vectors, middle, unit, scale, normed, proj, joined
):
    rep, _, core = mesh_place()
    for k, pair in enumerate(((p0, f0), (p1, f1), (p2, f2), (p3, f3))):
        for p, piece in enumerate(pair):
            proj[:, lanes(((rep ^ k) * CORES + (core ^ p)) * LANE, LANE)] = piece[...]
    for k in range(REPS):
        for p in range(CORES):
            at = lanes((k * CORES + (core ^ p)) * LANE, LANE)
            joined[:, at] = a[k * ROWS : (k + 1) * ROWS, p * LANE : (p + 1) * LANE]
    branch = jnp.dot(joined[...], proj[...], preferred_element_type=f32)
    values = x[...].astype(f32) + branch + vectors[4:5, :]
    middle[...] = values
    norm, spread = normalise(values)
    unit[...] = norm
    scale[...] = jnp.broadcast_to(spread, (ROWS, LANE))
    low = (norm * vectors[5:6, :] + vectors[6:7, :]).astype(bf16)
    for k in range(REPS):
        normed[k * ROWS : (k + 1) * ROWS, :] = low


def hidden_kernel(h, c0, c1, c2, c3, ff, vectors, back, hidden, pre_grad, c):
    rep = lax.axis_index("rep")
    for k, cot in enumerate((c0, c1, c2, c3)):
        c[pl.ds(pl.multiple_of((rep ^ k) * ROWS, ROWS), ROWS), :] = cot[...]

    @pl.loop(0, 2)
    def _(block):
        at = pl.ds(pl.multiple_of(block * 2 * ROWS, 2 * ROWS), 2 * ROWS)
        for n in range(SHARDS):
            tile = pl.ds(n * 2 * LANE, 2 * LANE)
            pair = pl.ds(n * CORES, CORES)
            fc, out = ff[pair, 0].reshape(-1, WIDTH), ff[pair, 1].reshape(-1, WIDTH)
            preact = dot_rows(h[at, :], fc) + vectors[8:9, tile]
            value, slope = gelu_and_slope(preact)
            hidden[at, tile] = value.astype(bf16)
            grad = dot_rows(c[at, :], out)
            pre_grad[at, tile] = (grad * slope).astype(bf16)
        fc = ff[:, 0].reshape(HIDDEN, WIDTH)
        back[at, :] = jnp.dot(pre_grad[at, :], fc, preferred_element_type=f32).astype(bf16)


def weights_kernel(hidden, pre_grad, h, c, ff, output, grads, sums, held, sems):
    copies = []
    for n in range(SHARDS):
        tile = pl.ds(n * 2 * LANE, 2 * LANE)
        for i, (left, right) in enumerate(((pre_grad, h), (hidden, c))):
            grad = contract(left[:, tile], right[...], 0, 0).astype(bf16)
            for j in range(CORES):
                held[(n * CORES + j) * 2 + i] = grad[j * LANE : (j + 1) * LANE]
        part = pl.ds(n * CORES * 2, CORES * 2)
        copies.append(pltpu.make_async_copy(held.at[part], grads.at[part], sems.at[n]))
        copies[-1].start()
    sums[...] = jnp.broadcast_to(
        jnp.sum(pre_grad[...].astype(f32), 0, keepdims=True), sums.shape
    )

    @pl.loop(0, 2)
    def _(block):
        at = pl.ds(pl.multiple_of(block * 2 * ROWS, 2 * ROWS), 2 * ROWS)
        out = ff[:, 1].reshape(HIDDEN, WIDTH)
        output[at, :] = jnp.dot(hidden[at, :], out, preferred_element_type=f32).astype(bf16)

    for copy in copies:
        copy.wait()


def middle_kernel(
    g, unit, scale, vectors, cot, proj, middle_grad, pairs, sums, low, back
):
    rep, _, core = mesh_place()
    grad = total(range(REPS), lambda k: g[k * ROWS : (k + 1) * ROWS, :].astype(f32))
    part, gain, shift = norm_pull(unit[...], scale[:, 0:1], vectors[5:6, :], grad)
    cots = cot[...].astype(f32)
    values = cots + part
    middle_grad[...] = values
    branch = values.astype(bf16)
    low[...] = branch
    back[...] = dot_rows(branch, proj[...]).astype(bf16)
    rows = [jnp.sum(branch.astype(f32), 0), gain, shift, jnp.sum(cots, 0)]
    for i, row in enumerate(rows):
        sums[i : i + 1, :] = row[None]
    sums[4:8, :] = jnp.zeros((4, WIDTH), f32)
    for k in range(REPS):
        rows = pl.ds(k * ROWS, ROWS)
        for p in range(CORES):
            at = lanes((k * CORES + (core ^ p)) * LANE, LANE)
            pairs[rows, p * LANE : (p + 1) * LANE] = back[:, at]
        pairs[rows, SHARD : 2 * SHARD] = low[:, k * SHARD : (k + 1) * SHARD]


def proj_grad_kernel(a0, a1, a2, a3, pairs, own, far):
    rep, shard, core = mesh_place()
    for k, a in enumerate((a0, a1, a2, a3)):
        grad = contract(a[...], pairs[:, SHARD : 2 * SHARD], 0, 0).astype(bf16)
        mine = jnp.where(core == 0, grad[:, 0:LANE], grad[:, LANE:])
        other = jnp.where(core == 0, grad[:, LANE:], grad[:, 0:LANE])
        for p in range(CORES):
            at = pl.ds(pl.multiple_of((core ^ p) * LANE, LANE), LANE)
            own[rep ^ k ^ shard, at, :] = mine[p * LANE : (p + 1) * LANE]
            far[rep ^ k ^ shard, at, :] = other[p * LANE : (p + 1) * LANE]


def attend_back_kernel(qkv, far, logs, pairs, query_grad, own_grad, far_grad):
    core = lax.axis_index("seq")
    causal, far_seen, first = head_masks(core)

    for sequence in range(REPS):
        at = pl.ds(sequence * ROWS, ROWS)
        for p in range(CORES):
            base = p * TRIPLE
            query = qkv[at, base : base + LANE]
            key_own = qkv[at, base + LANE : base + 2 * LANE]
            value_own = qkv[at, base + 2 * LANE : base + 3 * LANE]
            key_far = far[at, 2 * p * LANE : (2 * p + 1) * LANE]
            value_far = far[at, (2 * p + 1) * LANE : (2 * p + 2) * LANE]
            grad = pairs[at, p * LANE : (p + 1) * LANE]
            queries, sums = [], [0.0] * 4
            for h, mask in enumerate((first, ~first)):
                masked = jnp.where(mask, query, jnp.zeros_like(query))
                back = jnp.where(mask, grad, jnp.zeros_like(grad))
                own, other = head_scores(masked, key_own, key_far, causal, far_seen)
                log = logs[at, 2 * p + h : 2 * p + h + 1]
                own, other = jnp.exp(own - log), jnp.exp(other - log)
                own_back, other_back = dot_rows(back, value_own), dot_rows(back, value_far)
                row = jnp.sum(own * own_back + other * other_back, -1, keepdims=True)
                own_score = (own * (own_back - row)).astype(bf16)
                other_score = (other * (other_back - row)).astype(bf16)
                queries.append(
                    jnp.dot(own_score, key_own, preferred_element_type=f32)
                    + jnp.dot(other_score, key_far, preferred_element_type=f32)
                )
                parts = [
                    contract(own_score, masked, 0, 0) * SCALE,
                    contract(own.astype(bf16), back, 0, 0),
                    contract(other_score, masked, 0, 0) * SCALE,
                    contract(other.astype(bf16), back, 0, 0),
                ]
                sums = [a + b for a, b in zip(sums, parts)]
            query_grad[at, p * LANE : (p + 1) * LANE] = (
                jnp.where(first, *queries) * SCALE
            ).astype(bf16)
            own_at = slice(2 * p * LANE, (2 * p + 1) * LANE)
            own_grad[at, own_at] = sums[0]
            own_grad[at, (2 * p + 1) * LANE : (2 * p + 2) * LANE] = sums[1]
            q = 1 - p
            far_grad[at, 2 * q * LANE : (2 * q + 1) * LANE] = sums[2].astype(bf16)
            far_grad[at, (2 * q + 1) * LANE : (2 * q + 2) * LANE] = sums[3].astype(bf16)


def qkv_back_kernel(
    query_grad,
    own_grad,
    far_grad,
    weight,
    normed,
    unit,
    ff_sums,
    mid_sums,
    proj_own,
    proj_far,
    own,
    far,
    joined,
    small,
    mixed,
    sums,
):
    rep, shard, core = mesh_place()
    for p in range(CORES):
        base = p * TRIPLE
        mixed[:, base : base + LANE] = query_grad[:, p * LANE : (p + 1) * LANE]
        at = slice(2 * p * LANE, (2 * p + 2) * LANE)
        mixed[:, base + LANE : base + 3 * LANE] = (
            own_grad[:, at] + far_grad[:, at].astype(f32)
        ).astype(bf16)
    for k in range(SHARDS):
        at = lanes((shard ^ k) * SHARD, SHARD)
        grad = contract(normed[:, at], mixed[...], 0, 0).astype(bf16)
        own[k, :, 0:TRIPLE] = grad[:, 0:TRIPLE]
        far[k, :, 0:TRIPLE] = grad[:, TRIPLE:]
        own[k, :, TRIPLE:] = proj_own[k]
        far[k, :, TRIPLE:] = proj_far[k]
    gain = jnp.zeros((1, WIDTH), f32)
    shift = jnp.zeros((1, WIDTH), f32)
    for k in range(REPS):
        at = pl.ds(k * ROWS, ROWS)
        back = dot_rows(mixed[at, :], weight[...])
        joined[at, :] = back.astype(bf16)
        gain = gain + jnp.sum(back * unit[at, :], 0, keepdims=True)
        shift = shift + jnp.sum(back, 0, keepdims=True)
    sums[0:1, :] = gain
    sums[1:2, :] = shift
    mixed_sums = jnp.sum(mixed[...].astype(f32), 0, keepdims=True)
    for p in range(CORES):
        for i in range(2):
            start = i * SHARD + (core ^ p) * LANE
            sums[2:3, lanes(start, LANE)] = mixed_sums[
                :, p * TRIPLE + 2 * i * LANE : p * TRIPLE + (2 * i + 1) * LANE
            ]
    for k in range(SHARDS):
        small[k] = jnp.zeros(small.shape[1:], f32)
        at = lanes((shard ^ k) * SHARD, SHARD)
        small[k, 0:1, 0:SHARD] = sums[0:1, at]
        small[k, 1:2, 0:SHARD] = sums[1:2, at]
        queries = jnp.where((shard ^ k) == rep // 2, sums[2:3, 0:SHARD], 0.0)
        values = jnp.where((shard ^ k) == 2 + rep // 2, sums[2:3, SHARD : 2 * SHARD], 0.0)
        small[k, 2:3, 0:SHARD] = jnp.where(rep % 2 == 0, queries + values, 0.0)
        small[k, 3:4, 0:SHARD] = jnp.where(rep % 2 == 1, queries + values, 0.0)
        for i in range(4):
            small[k, 4 + i : 5 + i, 0:SHARD] = mid_sums[i : i + 1, at]
        part = ff_sums[:, at]
        row = lax.broadcasted_iota(jnp.int32, part.shape, 0)
        small[k, 8:16, 0:SHARD] = jnp.where(row == rep, part, 0.0)


def tail_kernel(own, far, small, o0, o1, o2, o3):
    for k, o in enumerate((o0, o1, o2, o3)):
        o[0:SHARD, :] = (own[k].astype(f32) + far[k].astype(f32)).astype(bf16)
        o[SHARD:, :] = small[k].astype(bf16)


def input_kernel(j, unit, vectors, middle_grad, grad):
    back = total(range(REPS), lambda k: j[k * ROWS : (k + 1) * ROWS, :].astype(f32))
    part, _, _ = norm_pull(unit[0], unit[1, :, 0:1], vectors[0:1, :], back)
    grad[...] = middle_grad[...] + part


def block_kernel(j, middle, vectors, block):
    output = total(range(REPS), lambda k: j[k * ROWS : (k + 1) * ROWS, :].astype(f32))
    block[...] = (middle[...] + output + vectors[7:8, :]).astype(bf16)


def joined_sum(pieces):
    pieces = [p.astype(f32) for p in pieces]
    return ((pieces[0] + pieces[1]) + (pieces[2] + pieces[3])).astype(bf16)


def final_kernel(p0, p1, p2, p3, f0, f1, f2, f3, qkv, proj, small):
    rep, _, core = mesh_place()
    for k, pair in enumerate(((p0, f0), (p1, f1), (p2, f2), (p3, f3))):
        for j, piece in enumerate(pair):
            start = ((rep ^ k) * CORES + (core ^ j)) * LANE
            for t in range(3):
                qkv[:, lanes(t * WIDTH + start, LANE)] = piece[
                    0:SHARD, t * LANE : (t + 1) * LANE
                ].astype(f32)
            proj[:, lanes(start, LANE)] = piece[0:SHARD, TRIPLE:].astype(f32)

    def read(pair):
        return pair[0][SHARD:, 0:SHARD].astype(f32) + pair[1][SHARD:, 0:SHARD].astype(f32)

    small[...] = total(((p0, f0), (p1, f1), (p2, f2), (p3, f3)), read)


def spread_kernel(p0, p1, p2, p3, f0, f1, f2, f3, fc, out):
    rep, _, core = mesh_place()
    for k, pair in enumerate(((p0, f0), (p1, f1), (p2, f2), (p3, f3))):
        for j, piece in enumerate(pair):
            at = pl.ds(pl.multiple_of(((rep ^ k) * CORES + (core ^ j)) * LANE, LANE), LANE)
            fc[at, :] = piece[0].astype(f32)
            out[at, :] = piece[1].astype(f32)


def tiled_body(
    block_input,
    ln1_gain,
    ln1_shift,
    qkv_weight,
    qv_bias,
    proj_weight,
    proj_bias,
    ln2_gain,
    ln2_shift,
    fc_weight,
    fc_bias,
    out_weight,
    out_bias,
    cotangent,
):
    rep, _, core = mesh_place()

    def over_rep(pieces):
        return [swap(p, "rep", REPS, k) if k else p for k, p in enumerate(pieces)]

    def over_shards(pieces):
        return [swap(p, "fsdp", SHARDS, k) if k else p for k, p in enumerate(pieces)]

    def over_cores(value):
        return swap(value, "seq", CORES, 1)

    all_rows = REPS * ROWS
    vectors = [
        ln1_gain,
        ln1_shift,
        qv_bias,
        proj_bias,
        ln2_gain,
        ln2_shift,
        out_bias,
        fc_bias,
    ]
    packed, own_rows = vmem_call(
        pack_kernel,
        [((SHARD + 16, TRIPLE + LANE), bf16), ((all_rows, WIDTH), bf16)],
        [qkv_weight, proj_weight, block_input] + vectors,
        hbm=tuple(range(11)),
        scratch=[pltpu.VMEM((12 * SHARD,), bf16), pltpu.SemaphoreType.DMA((16,))],
        limit=56,
    )
    own_packed = over_shards([packed] * SHARDS)
    far_packed = [over_cores(p) for p in own_packed]
    inputs = lax.all_to_all(own_rows, "rep", 0, 0, tiled=True)

    unit_one, _, unit_own = vmem_call(
        unit_kernel,
        [((all_rows, WIDTH), f32), ((all_rows, LANE), f32), ((2, ROWS, WIDTH), f32)],
        [inputs],
    )
    cots = over_rep([cotangent] * REPS)

    mine = rep * CORES + core
    ff = [pick(w.reshape(REPS * CORES, LANE, WIDTH), mine, 0) for w in (fc_weight, out_weight)]
    ff = after(jnp.stack(ff), *own_packed[1:], inputs, *cots[1:])
    ff = lax.all_gather(ff, ("fsdp", "seq"), axis=0)

    qkv, kv_send, normed_one, qkv_mine, vectors, proj_cols = vmem_call(
        qkv_kernel,
        [
            ((all_rows, 2 * TRIPLE), bf16),
            ((all_rows, 4 * LANE), bf16),
            ((all_rows, WIDTH), bf16),
            ((WIDTH, 2 * TRIPLE), bf16),
            ((16, WIDTH), f32),
            ((WIDTH, LANE), bf16),
        ],
        [unit_one] + own_packed + far_packed,
        scratch=[pltpu.VMEM((8, 2 * TRIPLE), f32)],
        flops=2 * all_rows * WIDTH * 2 * TRIPLE,
    )
    kv_far = over_cores(kv_send)
    proj_cols = over_rep([proj_cols] * REPS)
    attended, logs = vmem_call(
        attend_kernel,
        [((all_rows, SHARD), bf16), ((all_rows, LANE), f32)],
        [qkv, kv_far],
        flops=4 * all_rows * 2 * ROWS * SHARD,
    )
    mine = lax.all_to_all(attended, "rep", 0, 0, tiled=True)
    middle, unit_two, scale_two, normed_two, proj_full = vmem_call(
        branch_kernel,
        [
            ((ROWS, WIDTH), f32),
            ((ROWS, WIDTH), f32),
            ((ROWS, LANE), f32),
            ((all_rows, WIDTH), bf16),
            ((WIDTH, WIDTH), bf16),
        ],
        [mine]
        + proj_cols
        + [over_cores(after(p, mine)) for p in proj_cols]
        + [block_input, vectors],
        scratch=[pltpu.VMEM((ROWS, WIDTH), bf16)],
        flops=2 * ROWS * WIDTH * WIDTH,
    )
    normed_two = lax.all_to_all(normed_two, "rep", 0, 0, tiled=True)
    attended_all = over_rep([after(attended, normed_two)] * REPS)

    back, hidden, pre_grad, c_all = vmem_call(
        hidden_kernel,
        [
            ((all_rows, WIDTH), bf16),
            ((all_rows, HIDDEN), bf16),
            ((all_rows, HIDDEN), bf16),
            ((all_rows, WIDTH), bf16),
        ],
        [normed_two] + cots + [ff, vectors],
        flops=6 * all_rows * WIDTH * HIDDEN,
    )
    back = lax.all_to_all(back, "rep", 0, 0, tiled=True)
    output, ff_grads, ff_sums = vmem_call(
        weights_kernel,
        [
            ((all_rows, WIDTH), bf16),
            ((SHARDS * CORES * 2, LANE, WIDTH), bf16),
            ((8, HIDDEN), f32),
        ],
        [after(hidden, *attended_all[1:]), pre_grad, normed_two, c_all, ff],
        scratch=[
            pltpu.VMEM((SHARDS * CORES * 2, LANE, WIDTH), bf16),
            pltpu.SemaphoreType.DMA((SHARDS,)),
        ],
        away=(1,),
        flops=6 * all_rows * WIDTH * HIDDEN,
    )
    ff_piece = lax.psum_scatter(ff_grads, ("fsdp", "seq"), scatter_dimension=0, tiled=True)

    middle_grad, pairs, mid_sums = vmem_call(
        middle_kernel,
        [((ROWS, WIDTH), f32), ((all_rows, 2 * SHARD), bf16), ((8, WIDTH), f32)],
        [back, unit_two, scale_two, vectors, cotangent, proj_full],
        scratch=[pltpu.VMEM((ROWS, WIDTH), bf16)] * 2,
        flops=2 * ROWS * WIDTH * WIDTH,
    )
    pairs = lax.all_to_all(pairs, "rep", 0, 0, tiled=True)
    output = lax.all_to_all(after(output, pairs), "rep", 0, 0, tiled=True)
    (block_output,) = vmem_call(block_kernel, [((ROWS, WIDTH), bf16)], [output, middle, vectors])
    query_grad, own_grad, far_grad = vmem_call(
        attend_back_kernel,
        [
            ((all_rows, SHARD), bf16),
            ((all_rows, 4 * LANE), f32),
            ((all_rows, 4 * LANE), bf16),
        ],
        [qkv, kv_far, logs, pairs],
        weight=1,
        flops=10 * all_rows * 2 * ROWS * SHARD,
    )
    proj_own, proj_far = vmem_call(
        proj_grad_kernel,
        [((SHARDS, SHARD, LANE), bf16)] * 2,
        attended_all + [pairs],
        flops=2 * all_rows * WIDTH * SHARD,
    )
    qkv_own, qkv_far, joined, small = vmem_call(
        qkv_back_kernel,
        [
            ((SHARDS, SHARD, TRIPLE + LANE), bf16),
            ((SHARDS, SHARD, TRIPLE + LANE), bf16),
            ((all_rows, WIDTH), bf16),
            ((SHARDS, 16, TRIPLE + LANE), f32),
        ],
        [query_grad, own_grad, over_cores(far_grad), qkv_mine, normed_one, unit_one, ff_sums, mid_sums]
        + [proj_own, proj_far],
        scratch=[pltpu.VMEM((all_rows, 2 * TRIPLE), bf16), pltpu.VMEM((8, WIDTH), f32)],
        flops=4 * all_rows * WIDTH * 2 * TRIPLE,
    )
    tail = vmem_call(
        tail_kernel,
        [((SHARD + 16, TRIPLE + LANE), bf16)] * SHARDS,
        [qkv_own, over_cores(qkv_far), small],
    )
    tail = over_shards(tail)
    joined = lax.all_to_all(joined, "rep", 0, 0, tiled=True)
    ff_pieces = over_rep([ff_piece] * REPS)
    tail = joined_sum([after(tail[0], joined, block_output, *ff_pieces[1:])] + tail[1:])
    (input_grad,) = vmem_call(
        input_kernel, [((ROWS, WIDTH), f32)], [joined, unit_own, vectors, middle_grad]
    )
    whole_tail, tail = tail, over_rep([tail] * REPS)
    fc_grads, out_grads = vmem_call(
        spread_kernel,
        [((2 * REPS * LANE, WIDTH), f32)] * 2,
        ff_pieces + [over_cores(after(p, whole_tail)) for p in ff_pieces],
    )
    qkv_grads, proj_grads, small = vmem_call(
        final_kernel,
        [((SHARD, 3 * WIDTH), f32), ((SHARD, WIDTH), f32), ((16, SHARD), f32)],
        tail + [over_cores(after(t, fc_grads, input_grad)) for t in tail],
    )
    return (
        block_output,
        input_grad,
        small[0],
        small[1],
        qkv_grads,
        small[2:4].reshape(-1),
        proj_grads,
        small[4],
        small[5],
        small[6],
        fc_grads,
        small[8:12].reshape(-1),
        out_grads,
        small[7],
    )


def make_body(reps, shards, cores):
    def rep_swap(value, offset):
        return swap(value, "rep", reps, offset) if offset else value

    def shard_swap(value, offset):
        return swap(value, "fsdp", shards, offset) if offset else value

    def core_swap(value):
        return swap(value, "seq", cores, 1)

    def plane_gather(value):
        return [rep_swap(value, k) for k in range(reps)]

    def plane_exchange(pieces):
        return [rep_swap(piece, k) for k, piece in enumerate(pieces)]

    def pair_sum(pieces):
        while len(pieces) > 1:
            pieces = [pieces[i] + pieces[i + 1] for i in range(0, len(pieces), 2)]
        return pieces[0]

    def own_scatter(parts):
        core = lax.axis_index("seq")
        shard = lax.axis_index("fsdp")
        kept = pick(parts, core, 1).astype(f32)
        kept = (kept + core_swap(pick(parts, 1 - core, 1)).astype(f32)).astype(bf16)
        pieces = [shard_swap(pick(kept, shard ^ k, 0), k).astype(f32) for k in range(shards)]
        return pair_sum(pieces).astype(bf16)

    def place_both(pieces):
        core = lax.axis_index("seq")
        rep = lax.axis_index("rep")
        held = jnp.zeros((reps, cores) + pieces[0].shape, pieces[0].dtype)
        zeros = (0,) * pieces[0].ndim
        for k, piece in enumerate(pieces):
            held = lax.dynamic_update_slice(held, piece[None, None], (rep ^ k, core) + zeros)
            far = core_swap(piece)
            held = lax.dynamic_update_slice(held, far[None, None], (rep ^ k, 1 - core) + zeros)
        return held

    def body(
        block_input,
        ln1_gain,
        ln1_shift,
        qkv_weight,
        qv_bias,
        proj_weight,
        proj_bias,
        ln2_gain,
        ln2_shift,
        fc_weight,
        fc_bias,
        out_weight,
        out_bias,
        cotangent,
    ):
        rows, width = block_input.shape
        shard_width = width // shards
        part = width // (reps * cores)
        rep_width = part * cores
        hidden_part = fc_weight.shape[0] // (reps * cores)
        head_scale = HEAD_DIM ** (-0.5)
        rep = lax.axis_index("rep")
        shard = lax.axis_index("fsdp")
        core = lax.axis_index("seq")
        rep_at = [rep ^ k for k in range(reps)]
        shard_at = [shard ^ k for k in range(shards)]

        columns = qkv_weight.reshape(shard_width, 3, reps, cores, part)
        columns = pick(pick(columns, rep, 2), core, 2).reshape(shard_width, 3 * part)
        fc_bias_part = pick(fc_bias.reshape(reps, -1), rep, 0)
        vectors = [
            ln1_gain,
            ln1_shift,
            qv_bias[:shard_width],
            qv_bias[shard_width:],
            proj_bias,
            ln2_gain,
            ln2_shift,
            out_bias,
            fc_bias_part,
        ]
        vectors = [jnp.pad(v, (0, 3 * part - v.shape[0])) for v in vectors]
        vectors = jnp.stack(vectors + [jnp.zeros_like(vectors[0])] * (16 - len(vectors)))
        packed = jnp.concatenate([columns, vectors], 0)
        packed, own_rows = lax.optimization_barrier((packed, block_input))
        packed = place([shard_swap(packed, k) for k in range(shards)], shard_at)
        inputs_all = jnp.concatenate(plane_gather(own_rows), 0)
        columns = packed[:, :shard_width].reshape(width, 3 * part)
        vectors = packed[:, shard_width:, :].astype(f32)

        def vector(index, size):
            return vectors[:, index, :size].reshape(-1)

        gain_one, shift_one = vector(0, shard_width), vector(1, shard_width)
        qv_full = jnp.stack([vectors[:, 2, :shard_width], vectors[:, 3, :shard_width]], 1)
        qv_full = qv_full.reshape(2, reps, cores * part)
        proj_bias_full = vector(4, shard_width)
        gain_two, shift_two = vector(5, shard_width), vector(6, shard_width)
        out_bias_full = vector(7, shard_width)
        fc_bias_mine = vector(8, fc_bias_part.shape[0])
        qkv_mine = place([columns, core_swap(columns)], [core, 1 - core])
        qkv_mine = jnp.transpose(qkv_mine, (1, 0, 2)).reshape(width, cores * 3 * part)

        proj_part = pick(proj_weight.reshape(reps * cores, -1, width), rep * cores + core, 0)
        proj_full = lax.all_gather(proj_part, ("rep", "fsdp", "seq"), axis=0)
        proj_full = proj_full.reshape((reps, shards, cores) + proj_part.shape)
        proj_full = jnp.transpose(proj_full, (1, 0, 2, 3, 4)).reshape(width, width)

        fc_part = pick(fc_weight.reshape(reps * cores, hidden_part, width), rep * cores + core, 0)
        out_part = pick(out_weight.reshape(reps * cores, hidden_part, width), rep * cores + core, 0)
        both_part = jnp.stack([fc_part, out_part])
        both_part, packed = lax.optimization_barrier((both_part, packed))
        both = place([shard_swap(both_part, k) for k in range(shards)], shard_at)
        both = place([both, core_swap(both)], [core, 1 - core])
        fc_mine = jnp.transpose(both[:, :, 0], (1, 0, 2, 3)).reshape(-1, width)
        out_mine = jnp.transpose(both[:, :, 1], (1, 0, 2, 3)).reshape(-1, width)

        own_cot, inputs_all = lax.optimization_barrier((cotangent, inputs_all))
        cot_all = jnp.concatenate(plane_gather(own_cot), 0)

        unit_one, scale_one = normalise(inputs_all.astype(f32))
        normed_all = (unit_one * gain_one + shift_one).astype(bf16)
        mixed = jnp.dot(normed_all, qkv_mine, preferred_element_type=f32)
        mixed = mixed.reshape(reps, rows, cores, 3, part)
        qv_mine = pick(qv_full, rep, 1).reshape(2, cores, part)
        heads = (reps, rows, rep_width // HEAD_DIM, HEAD_DIM)
        queries = (mixed[:, :, :, 0] + qv_mine[0]).astype(bf16).reshape(heads)
        keys = mixed[:, :, :, 1].astype(bf16).reshape(heads)
        values = (mixed[:, :, :, 2] + qv_mine[1]).astype(bf16).reshape(heads)
        far_pair = core_swap(jnp.stack([keys, values]))
        keys_both = jnp.concatenate([keys, far_pair[0]], 1)
        values_both = jnp.concatenate([values, far_pair[1]], 1)

        row_pos = lax.broadcasted_iota(jnp.int32, (rows, 2 * rows), 0)
        col_pos = lax.broadcasted_iota(jnp.int32, (rows, 2 * rows), 1)
        allowed = jnp.where(col_pos < rows, col_pos <= row_pos, core == 1)
        scores = jnp.einsum("sqhd,skhd->shqk", queries, keys_both, preferred_element_type=f32)
        scores = jnp.where(allowed, scores * head_scale, masked_value)
        peak = jnp.max(scores, -1, keepdims=True)
        powers = jnp.exp(scores - peak)
        probs = powers / jnp.sum(powers, -1, keepdims=True)
        probs_low = probs.astype(bf16)
        attended = jnp.einsum("shqk,skhd->sqhd", probs_low, values_both, preferred_element_type=f32)
        attended_low = attended.astype(bf16).reshape(reps, rows, rep_width)
        mine = place(plane_exchange([attended_low[k] for k in range(reps)]), rep_at)
        mine = jnp.transpose(mine, (1, 0, 2)).reshape(rows, width)
        middle = (
            block_input.astype(f32)
            + jnp.dot(mine, proj_full, preferred_element_type=f32)
            + proj_bias_full
        )
        unit_two, scale_two = normalise(middle)
        normed_two = (unit_two * gain_two + shift_two).astype(bf16)
        normed_two_all = jnp.concatenate(plane_gather(normed_two), 0)

        attended_all = place([attended_low[k] for k in range(reps)], rep_at)
        attended_all = lax.all_gather(attended_all.reshape(reps * rows, rep_width), "rep", axis=0)
        attended_all = jnp.transpose(attended_all, (1, 0, 2)).reshape(reps * rows, width)

        hidden_grad = contract(cot_all, out_mine, 1, 1)
        preact = contract(normed_two_all, fc_mine, 1, 1) + fc_bias_mine
        hidden, slope = gelu_and_slope(preact)
        hidden_low = hidden.astype(bf16)
        pre_grad = (hidden_grad * slope).astype(bf16)
        normed_grad = jnp.dot(pre_grad, fc_mine, preferred_element_type=f32).astype(bf16)
        normed_grad = normed_grad.reshape(reps, rows, width)
        normed_grad = plane_exchange([normed_grad[k] for k in range(reps)])
        normed_grad = pair_sum([v.astype(f32) for v in normed_grad])
        output = jnp.dot(hidden_low, out_mine, preferred_element_type=f32).astype(bf16)
        output, normed_grad = lax.optimization_barrier((output, normed_grad))
        output = output.reshape(reps, rows, width)
        output = plane_exchange([output[k] for k in range(reps)])
        output = pair_sum([v.astype(f32) for v in output])
        block_output = (middle + output + out_bias_full).astype(bf16)

        out_grads = contract(hidden_low, cot_all, 0, 0).astype(bf16)
        out_grads = lax.psum_scatter(out_grads, ("fsdp", "seq"), scatter_dimension=0, tiled=True)
        fc_grads = contract(pre_grad, normed_two_all, 0, 0).astype(bf16)
        fc_grads = own_scatter(fc_grads.reshape(shards, cores, hidden_part, width))
        ff_grads = plane_gather(jnp.stack([fc_grads, out_grads]))
        ff_grads = place_both(ff_grads)
        fc_grads = ff_grads[:, :, 0].reshape(-1, width).astype(f32)
        out_grads = ff_grads[:, :, 1].reshape(-1, width).astype(f32)

        middle_part, gain_two_grads, shift_two_grads = norm_pull(
            unit_two, scale_two, gain_two, normed_grad
        )
        middle_grad = cotangent.astype(f32) + middle_part
        branch_grad = middle_grad.astype(bf16)
        attended_grad = contract(branch_grad, proj_full, 1, 1).astype(bf16)
        pair = [v.reshape(rows, reps, rep_width) for v in (attended_grad, branch_grad)]
        pair = jnp.concatenate(pair, 2)
        pair = plane_exchange([pick(pair, i, 1) for i in rep_at])
        attended_grad = jnp.stack([v[:, :rep_width] for v in pair]).reshape(heads)
        branch_cols = place([v[:, rep_width:] for v in pair], rep_at).reshape(-1, rep_width)
        proj_grads = contract(attended_all, branch_cols, 0, 0).astype(bf16)
        proj_grads = proj_grads.reshape(shards, shard_width, cores, part)
        proj_grads = jnp.transpose(proj_grads, (0, 2, 1, 3)).reshape(-1, part)
        proj_grads = lax.psum_scatter(proj_grads, ("fsdp", "seq"), scatter_dimension=0, tiled=True)
        proj_grads = lax.all_gather(proj_grads, ("rep", "seq"), axis=0)
        proj_grads = jnp.transpose(proj_grads, (1, 0, 2)).reshape(shard_width, width).astype(f32)

        prob_grad = jnp.einsum("sqhd,skhd->shqk", attended_grad, values_both, preferred_element_type=f32)
        row_total = jnp.sum(probs * prob_grad, -1, keepdims=True)
        score_low = (probs * (prob_grad - row_total)).astype(bf16)
        query_grad = (
            jnp.einsum("shqk,skhd->sqhd", score_low, keys_both, preferred_element_type=f32)
            * head_scale
        )
        key_grad = (
            jnp.einsum("shqk,sqhd->skhd", score_low, queries, preferred_element_type=f32)
            * head_scale
        )
        value_grad = jnp.einsum("shqk,sqhd->skhd", probs_low, attended_grad, preferred_element_type=f32)
        far_grads = core_swap(jnp.stack([key_grad[:, rows:], value_grad[:, rows:]]).astype(bf16))
        key_grad = key_grad[:, :rows] + far_grads[0].astype(f32)
        value_grad = value_grad[:, :rows] + far_grads[1].astype(f32)
        mixed_grad = jnp.stack(
            [
                g.astype(bf16).reshape(reps * rows, cores, part)
                for g in (query_grad, key_grad, value_grad)
            ],
            2,
        ).reshape(reps * rows, cores * 3 * part)
        qkv_grads = contract(normed_all, mixed_grad, 0, 0).astype(bf16)
        normed_one_grad = contract(mixed_grad, qkv_mine, 1, 1)
        joined = normed_one_grad.astype(bf16).reshape(reps, rows, width)
        joined = plane_exchange([joined[k] for k in range(reps)])
        joined = pair_sum([v.astype(f32) for v in joined])
        input_part = norm_pull(unit_one[:rows], scale_one[:rows], gain_one, joined)[0]
        input_grad = middle_grad + input_part

        gain_one_grads = jnp.sum(normed_one_grad * unit_one, 0)
        shift_one_grads = jnp.sum(normed_one_grad, 0)
        mixed_sums = jnp.sum(mixed_grad.astype(f32), 0).reshape(cores, 3, part)
        qv_sums = jnp.stack([mixed_sums[:, 0].reshape(-1), mixed_sums[:, 2].reshape(-1)])
        qv_sums = lax.dynamic_update_index_in_dim(
            jnp.zeros((2, reps, rep_width), f32), qv_sums, rep, 1
        )
        fc_sums = jnp.sum(pre_grad.astype(f32), 0).reshape(shards, -1)
        fc_sums = lax.dynamic_update_index_in_dim(
            jnp.zeros((shards, reps, fc_sums.shape[1]), f32), fc_sums, rep, 1
        )
        small = [
            gain_one_grads,
            shift_one_grads,
            qv_sums,
            jnp.sum(branch_grad.astype(f32), 0),
            gain_two_grads,
            shift_two_grads,
            jnp.sum(cotangent.astype(f32), 0),
            fc_sums,
        ]
        small = jnp.concatenate([v.reshape(shards, -1) for v in small], 1).astype(bf16)
        small_size = small.shape[1]
        small_rows = -(-small_size // (16 * 3 * part)) * 16
        small = jnp.pad(small, ((0, 0), (0, small_rows * 3 * part - small_size)))
        small = small.reshape(shards, small_rows, 3 * part)

        qkv_grads = qkv_grads.reshape(shards, shard_width, cores, 3 * part)
        tail = pick(qkv_grads, core, 2).astype(f32)
        tail = (tail + core_swap(pick(qkv_grads, 1 - core, 2)).astype(f32)).astype(bf16)
        tail = jnp.concatenate([tail, small], 1)
        tail = [shard_swap(pick(tail, i, 0), k).astype(f32) for k, i in enumerate(shard_at)]
        tail = place_both(plane_gather(pair_sum(tail).astype(bf16)))
        qkv_grads = tail[:, :, :shard_width].reshape(reps * cores, shard_width, 3, part)
        qkv_grads = jnp.transpose(qkv_grads, (1, 2, 0, 3)).reshape(shard_width, 3 * width)
        qkv_grads = qkv_grads.astype(f32)
        small = jnp.sum(tail[:, :, shard_width:].astype(f32), (0, 1)).reshape(-1)
        sizes = [1, 1, 2, 1, 1, 1, 1]
        ends = [0]
        for size in sizes:
            ends.append(ends[-1] + size * shard_width)
        one = [small[a:b] for a, b in zip(ends[:-1], ends[1:])] + [small[ends[-1] : small_size]]
        return (
            block_output,
            input_grad,
            one[0],
            one[1],
            qkv_grads,
            one[2],
            proj_grads,
            one[3],
            one[4],
            one[5],
            fc_grads,
            one[7],
            out_grads,
            one[6],
        )

    return body


def solution(mesh):
    line, block = P("fsdp"), P("fsdp", None)
    tokens = P(("rep", "fsdp", "seq"), None)
    in_specs = (
        tokens,
        line,
        line,
        block,
        line,
        block,
        line,
        line,
        line,
        block,
        line,
        block,
        line,
        tokens,
    )
    out_specs = (
        tokens,
        tokens,
        line,
        line,
        block,
        line,
        block,
        line,
        line,
        line,
        block,
        line,
        block,
        line,
    )
    sizes = mesh.shape["rep"], mesh.shape["fsdp"], mesh.shape["seq"]
    general = make_body(*sizes)

    def body(*args):
        tiled = sizes == (REPS, SHARDS, CORES) and args[0].shape == (ROWS, WIDTH)
        return tiled_body(*args) if tiled else general(*args)

    return jax.shard_map(body, mesh=mesh, in_specs=in_specs, out_specs=out_specs, check_vma=False)
```

```python
import math

import jax
import jax.numpy as jnp
from jax import lax
from jax.experimental import pallas as pl
from jax.experimental.pallas import tpu as pltpu
from jax.sharding import PartitionSpec as P

HEADS = 16
HEAD_DIM = 64

norm_eps = 1e-05
masked_value = -1e30
f32 = jnp.float32
bf16 = jnp.bfloat16

REPS, SHARDS, CORES = 4, 4, 2
LANE, ROWS, WIDTH, SHARD, TRIPLE, HIDDEN = 128, 128, 1024, 256, 384, 1024
SCALE = HEAD_DIM ** (-0.5)


def normalise(values):
    centre = jnp.mean(values, -1, keepdims=True)
    offsets = values - centre
    spread = jnp.mean(offsets * offsets, -1, keepdims=True)
    scale = lax.rsqrt(spread + norm_eps)
    return offsets * scale, scale


def norm_pull(unit, scale, gain, grad):
    inner = grad * gain
    first = jnp.mean(inner, -1, keepdims=True)
    second = jnp.mean(inner * unit, -1, keepdims=True)
    return scale * (inner - first - unit * second), jnp.sum(grad * unit, 0), jnp.sum(grad, 0)


def gelu_and_slope(values):
    rate = 0.7978845608028654
    squared = values * values
    bent = jnp.tanh(rate * (values + 0.044715 * values * squared))
    half = 0.5 * (1.0 + bent)
    slope = half + 0.5 * values * (1.0 - bent * bent) * (rate * (1.0 + 3.0 * 0.044715 * squared))
    return values * half, slope


def contract(left, right, left_axis, right_axis):
    return lax.dot_general(
        left, right, (((left_axis,), (right_axis,)), ((), ())), preferred_element_type=f32
    )


def swap(value, axis, size, offset):
    return lax.ppermute(value, axis, [(i, i ^ offset) for i in range(size)])


def pick(array, index, axis):
    return lax.dynamic_index_in_dim(array, index, axis, keepdims=False)


def place(pieces, positions):
    stacked = jnp.zeros((len(pieces),) + pieces[0].shape, pieces[0].dtype)
    for piece, position in zip(pieces, positions):
        stacked = lax.dynamic_update_index_in_dim(stacked, piece, position, 0)
    return stacked


def lanes(start, size):
    return pl.ds(pl.multiple_of(start, LANE), size)


def vmem_call(kernel, outs, args, hbm=(), staged=(), scratch=(), flops=0, limit=16, away=(), weight=24):
    moved = sum(a.size * a.dtype.itemsize for a in args)
    moved += sum(math.prod(s) * jnp.dtype(t).itemsize for s, t in outs)
    whole = pl.BlockSpec(memory_space=pltpu.VMEM)
    far = pl.BlockSpec(memory_space=pltpu.HBM)
    n, m, k = len(args), len(outs), len(staged)

    def body(*refs):
        ins, rest, held, sems = list(refs[:n]), refs[n:], refs[n + m : n + m + k], refs[n + m + k]
        copies = [
            pltpu.make_async_copy(ins[i], held[j], sems.at[j]) for j, i in enumerate(staged)
        ]
        for copy in copies:
            copy.start()
        for copy in copies:
            copy.wait()
        for j, i in enumerate(staged):
            ins[i] = held[j]
        kernel(*ins, *rest[:m], *rest[m + k + 1 :])

    copied = [pltpu.VMEM(args[i].shape, args[i].dtype) for i in staged]
    if staged:
        copied.append(pltpu.SemaphoreType.DMA((k,)))
    return pl.pallas_call(
        body if staged else kernel,
        out_shape=[jax.ShapeDtypeStruct(s, t) for s, t in outs],
        in_specs=[far if i in hbm or i in staged else whole for i in range(n)],
        out_specs=[far if i in away else whole for i in range(m)],
        scratch_shapes=copied + list(scratch),
        compiler_params=pltpu.CompilerParams(vmem_limit_bytes=limit * 1024 * 1024),
        cost_estimate=pl.CostEstimate(
            flops=flops * weight, bytes_accessed=moved * weight, transcendentals=0
        ),
    )(*args)


def after(value, *others):
    return lax.optimization_barrier((value,) + others)[0]


def mesh_place():
    return lax.axis_index("rep"), lax.axis_index("fsdp"), lax.axis_index("seq")


def total(refs, read):
    return (read(refs[0]) + read(refs[1])) + (read(refs[2]) + read(refs[3]))


def pack_kernel(*refs):
    qkv, proj, x = refs[0:3]
    vectors, (packed, x_copy, held, sems) = refs[3:-4], refs[-4:]
    rep, _, core = mesh_place()
    mine = (rep * CORES + core) * LANE
    parts = [qkv.at[:, lanes(t * WIDTH + mine, LANE)] for t in range(3)]
    parts.append(proj.at[:, lanes(mine, LANE)])
    targets = [packed.at[pl.ds(0, SHARD), pl.ds(t * LANE, LANE)] for t in range(4)]
    parts += [x] * REPS
    targets += [x_copy.at[pl.ds(k * ROWS, ROWS), :] for k in range(REPS)]
    at = 0
    for v in vectors:
        parts.append(v)
        targets.append(held.at[pl.ds(at, v.shape[0])])
        at += v.shape[0]
    copies = [
        pltpu.make_async_copy(part, target, sems.at[i])
        for i, (part, target) in enumerate(zip(parts, targets))
    ]
    for copy in copies:
        copy.start()
    packed[SHARD:, SHARD:] = jnp.zeros((packed.shape[0] - SHARD, SHARD), bf16)
    for copy in copies:
        copy.wait()
    rows = [held[i * SHARD : (i + 1) * SHARD].astype(f32).reshape(1, SHARD) for i in range(8)]
    biases = [held[i * SHARD : (i + 1) * SHARD].astype(f32).reshape(1, SHARD) for i in range(8, 12)]
    rows.append(
        jnp.where(
            rep < 2,
            jnp.where(rep == 0, biases[0], biases[1]),
            jnp.where(rep == 2, biases[2], biases[3]),
        )
    )
    rows.append(jnp.zeros((16 - len(rows), SHARD), f32))
    packed[SHARD:, 0:SHARD] = jnp.concatenate(rows, 0).astype(bf16)


def unit_kernel(x, unit, scale, unit_own):
    for k in range(REPS):
        at = pl.ds(k * ROWS, ROWS)
        unit[at, :], spread = normalise(x[at, :].astype(f32))
        scale[at, :] = jnp.broadcast_to(spread, (ROWS, LANE))
    own = pl.ds(pl.multiple_of(lax.axis_index("rep") * ROWS, ROWS), ROWS)
    unit_own[0] = unit[own, :]
    unit_own[1, :, 0:LANE] = scale[own, :]
    unit_own[1, :, LANE:] = jnp.zeros((ROWS, WIDTH - LANE), f32)


def qkv_kernel(
    unit, p0, p1, p2, p3, f0, f1, f2, f3, qkv, kv_send, normed, weight, vectors, proj, biases
):
    rep, shard, core = mesh_place()
    for k, (own, far) in enumerate(((p0, f0), (p1, f1), (p2, f2), (p3, f3))):
        at = pl.ds(pl.multiple_of((shard ^ k) * SHARD, SHARD), SHARD)
        weight[at, 0:TRIPLE] = own[0:SHARD, 0:TRIPLE]
        weight[at, TRIPLE : 2 * TRIPLE] = far[0:SHARD, 0:TRIPLE]
        proj[at, :] = own[0:SHARD, TRIPLE:]
        vectors[:, at] = own[SHARD:, 0:SHARD].astype(f32)
    for p in range(CORES):
        for t, at in ((0, 0), (2, 2)):
            start = (at + rep // 2) * SHARD + (core ^ p) * LANE
            even, odd = vectors[2:3, lanes(start, LANE)], vectors[3:4, lanes(start, LANE)]
            biases[:, pl.ds(p * TRIPLE + t * LANE, LANE)] = jnp.broadcast_to(
                jnp.where(rep % 2 == 0, even, odd), (8, LANE)
            )
        biases[:, pl.ds(p * TRIPLE + LANE, LANE)] = jnp.zeros((8, LANE), f32)

    @pl.loop(0, 2)
    def _(block):
        at = pl.ds(pl.multiple_of(block * 2 * ROWS, 2 * ROWS), 2 * ROWS)
        values = (unit[at, :] * vectors[0:1, :] + vectors[1:2, :]).astype(bf16)
        normed[at, :] = values
        mixed = jnp.dot(values, weight[...], preferred_element_type=f32) + biases[0:1, :]
        mixed = mixed.astype(bf16)
        qkv[at, :] = mixed
        kv_send[at, 0 : 2 * LANE] = mixed[:, TRIPLE + LANE : 2 * TRIPLE]
        kv_send[at, 2 * LANE : 4 * LANE] = mixed[:, LANE:TRIPLE]


def dot_rows(left, right):
    return contract(left, right, 1, 1)


def head_scores(query, key_own, key_far, causal, far_seen):
    own = jnp.where(causal, dot_rows(query, key_own) * SCALE, masked_value)
    far = jnp.where(far_seen, dot_rows(query, key_far) * SCALE, masked_value)
    return own, far


def head_masks(core):
    causal = lax.broadcasted_iota(jnp.int32, (ROWS, ROWS), 1) <= lax.broadcasted_iota(
        jnp.int32, (ROWS, ROWS), 0
    )
    far_seen = (lax.broadcasted_iota(jnp.int32, (ROWS, ROWS), 0) * 0 + core) == 1
    first = lax.broadcasted_iota(jnp.int32, (ROWS, LANE), 1) < HEAD_DIM
    return causal, far_seen, first


def attend_kernel(qkv, far, attended, logs):
    core = lax.axis_index("seq")
    causal, far_seen, first = head_masks(core)
    lane = lax.broadcasted_iota(jnp.int32, (ROWS, LANE), 1)

    for sequence in range(REPS):
        at = pl.ds(sequence * ROWS, ROWS)
        for p in range(CORES):
            base = p * TRIPLE
            query = qkv[at, base : base + LANE]
            key_own = qkv[at, base + LANE : base + 2 * LANE]
            value_own = qkv[at, base + 2 * LANE : base + 3 * LANE]
            key_far = far[at, 2 * p * LANE : (2 * p + 1) * LANE]
            value_far = far[at, (2 * p + 1) * LANE : (2 * p + 2) * LANE]
            heads = []
            for h, mask in enumerate((first, ~first)):
                masked = jnp.where(mask, query, jnp.zeros_like(query))
                own, other = head_scores(masked, key_own, key_far, causal, far_seen)
                peak = jnp.max(jnp.maximum(own, other), -1, keepdims=True)
                own, other = jnp.exp(own - peak), jnp.exp(other - peak)
                whole = jnp.sum(own + other, -1, keepdims=True)
                share = 1.0 / whole
                own, other = own * share, other * share
                log = jnp.broadcast_to(peak + jnp.log(whole), (ROWS, LANE))
                kept = log if p + h == 0 else jnp.where(lane == 2 * p + h, log, kept)
                heads.append(
                    jnp.dot(own.astype(bf16), value_own, preferred_element_type=f32)
                    + jnp.dot(other.astype(bf16), value_far, preferred_element_type=f32)
                )
            if p == CORES - 1:
                logs[at, :] = kept
            attended[at, p * LANE : (p + 1) * LANE] = jnp.where(first, *heads).astype(bf16)


def branch_kernel(
    a, p0, p1, p2, p3, f0, f1, f2, f3, x, vectors, middle, unit, scale, normed, proj, joined
):
    rep, _, core = mesh_place()
    for k, pair in enumerate(((p0, f0), (p1, f1), (p2, f2), (p3, f3))):
        for p, piece in enumerate(pair):
            proj[:, lanes(((rep ^ k) * CORES + (core ^ p)) * LANE, LANE)] = piece[...]
    for k in range(REPS):
        for p in range(CORES):
            at = lanes((k * CORES + (core ^ p)) * LANE, LANE)
            joined[:, at] = a[k * ROWS : (k + 1) * ROWS, p * LANE : (p + 1) * LANE]
    branch = jnp.dot(joined[...], proj[...], preferred_element_type=f32)
    values = x[...].astype(f32) + branch + vectors[4:5, :]
    middle[...] = values
    norm, spread = normalise(values)
    unit[...] = norm
    scale[...] = jnp.broadcast_to(spread, (ROWS, LANE))
    low = (norm * vectors[5:6, :] + vectors[6:7, :]).astype(bf16)
    for k in range(REPS):
        normed[k * ROWS : (k + 1) * ROWS, :] = low


def hidden_kernel(h, c0, c1, c2, c3, ff, vectors, back, hidden, pre_grad, c):
    rep = lax.axis_index("rep")
    for k, cot in enumerate((c0, c1, c2, c3)):
        c[pl.ds(pl.multiple_of((rep ^ k) * ROWS, ROWS), ROWS), :] = cot[...]

    @pl.loop(0, 2)
    def _(block):
        at = pl.ds(pl.multiple_of(block * 2 * ROWS, 2 * ROWS), 2 * ROWS)
        for n in range(SHARDS):
            tile = pl.ds(n * 2 * LANE, 2 * LANE)
            pair = pl.ds(n * CORES, CORES)
            fc, out = ff[pair, 0].reshape(-1, WIDTH), ff[pair, 1].reshape(-1, WIDTH)
            preact = dot_rows(h[at, :], fc) + vectors[8:9, tile]
            value, slope = gelu_and_slope(preact)
            hidden[at, tile] = value.astype(bf16)
            grad = dot_rows(c[at, :], out)
            pre_grad[at, tile] = (grad * slope).astype(bf16)
        fc = ff[:, 0].reshape(HIDDEN, WIDTH)
        back[at, :] = jnp.dot(pre_grad[at, :], fc, preferred_element_type=f32).astype(bf16)


def weights_kernel(hidden, pre_grad, h, c, ff, output, grads, sums, held, sems):
    copies = []
    for n in range(SHARDS):
        tile = pl.ds(n * 2 * LANE, 2 * LANE)
        for i, (left, right) in enumerate(((pre_grad, h), (hidden, c))):
            grad = contract(left[:, tile], right[...], 0, 0).astype(bf16)
            for j in range(CORES):
                held[(n * CORES + j) * 2 + i] = grad[j * LANE : (j + 1) * LANE]
        part = pl.ds(n * CORES * 2, CORES * 2)
        copies.append(pltpu.make_async_copy(held.at[part], grads.at[part], sems.at[n]))
        copies[-1].start()
    sums[...] = jnp.broadcast_to(
        jnp.sum(pre_grad[...].astype(f32), 0, keepdims=True), sums.shape
    )

    @pl.loop(0, 2)
    def _(block):
        at = pl.ds(pl.multiple_of(block * 2 * ROWS, 2 * ROWS), 2 * ROWS)
        out = ff[:, 1].reshape(HIDDEN, WIDTH)
        output[at, :] = jnp.dot(hidden[at, :], out, preferred_element_type=f32).astype(bf16)

    for copy in copies:
        copy.wait()


def middle_kernel(
    g, unit, scale, vectors, cot, proj, middle_grad, pairs, sums, low, back
):
    rep, _, core = mesh_place()
    grad = total(range(REPS), lambda k: g[k * ROWS : (k + 1) * ROWS, :].astype(f32))
    part, gain, shift = norm_pull(unit[...], scale[:, 0:1], vectors[5:6, :], grad)
    cots = cot[...].astype(f32)
    values = cots + part
    middle_grad[...] = values
    branch = values.astype(bf16)
    low[...] = branch
    back[...] = dot_rows(branch, proj[...]).astype(bf16)
    rows = [jnp.sum(branch.astype(f32), 0), gain, shift, jnp.sum(cots, 0)]
    for i, row in enumerate(rows):
        sums[i : i + 1, :] = row[None]
    sums[4:8, :] = jnp.zeros((4, WIDTH), f32)
    for k in range(REPS):
        rows = pl.ds(k * ROWS, ROWS)
        for p in range(CORES):
            at = lanes((k * CORES + (core ^ p)) * LANE, LANE)
            pairs[rows, p * LANE : (p + 1) * LANE] = back[:, at]
        pairs[rows, SHARD : 2 * SHARD] = low[:, k * SHARD : (k + 1) * SHARD]


def proj_grad_kernel(a0, a1, a2, a3, pairs, own, far):
    rep, shard, core = mesh_place()
    for k, a in enumerate((a0, a1, a2, a3)):
        grad = contract(a[...], pairs[:, SHARD : 2 * SHARD], 0, 0).astype(bf16)
        mine = jnp.where(core == 0, grad[:, 0:LANE], grad[:, LANE:])
        other = jnp.where(core == 0, grad[:, LANE:], grad[:, 0:LANE])
        for p in range(CORES):
            at = pl.ds(pl.multiple_of((core ^ p) * LANE, LANE), LANE)
            own[rep ^ k ^ shard, at, :] = mine[p * LANE : (p + 1) * LANE]
            far[rep ^ k ^ shard, at, :] = other[p * LANE : (p + 1) * LANE]


def attend_back_kernel(qkv, far, logs, pairs, query_grad, own_grad, far_grad):
    core = lax.axis_index("seq")
    causal, far_seen, first = head_masks(core)

    for sequence in range(REPS):
        at = pl.ds(sequence * ROWS, ROWS)
        for p in range(CORES):
            base = p * TRIPLE
            query = qkv[at, base : base + LANE]
            key_own = qkv[at, base + LANE : base + 2 * LANE]
            value_own = qkv[at, base + 2 * LANE : base + 3 * LANE]
            key_far = far[at, 2 * p * LANE : (2 * p + 1) * LANE]
            value_far = far[at, (2 * p + 1) * LANE : (2 * p + 2) * LANE]
            grad = pairs[at, p * LANE : (p + 1) * LANE]
            queries, sums = [], [0.0] * 4
            for h, mask in enumerate((first, ~first)):
                masked = jnp.where(mask, query, jnp.zeros_like(query))
                back = jnp.where(mask, grad, jnp.zeros_like(grad))
                own, other = head_scores(masked, key_own, key_far, causal, far_seen)
                log = logs[at, 2 * p + h : 2 * p + h + 1]
                own, other = jnp.exp(own - log), jnp.exp(other - log)
                own_back, other_back = dot_rows(back, value_own), dot_rows(back, value_far)
                row = jnp.sum(own * own_back + other * other_back, -1, keepdims=True)
                own_score = (own * (own_back - row)).astype(bf16)
                other_score = (other * (other_back - row)).astype(bf16)
                queries.append(
                    jnp.dot(own_score, key_own, preferred_element_type=f32)
                    + jnp.dot(other_score, key_far, preferred_element_type=f32)
                )
                parts = [
                    contract(own_score, masked, 0, 0) * SCALE,
                    contract(own.astype(bf16), back, 0, 0),
                    contract(other_score, masked, 0, 0) * SCALE,
                    contract(other.astype(bf16), back, 0, 0),
                ]
                sums = [a + b for a, b in zip(sums, parts)]
            query_grad[at, p * LANE : (p + 1) * LANE] = (
                jnp.where(first, *queries) * SCALE
            ).astype(bf16)
            own_at = slice(2 * p * LANE, (2 * p + 1) * LANE)
            own_grad[at, own_at] = sums[0]
            own_grad[at, (2 * p + 1) * LANE : (2 * p + 2) * LANE] = sums[1]
            q = 1 - p
            far_grad[at, 2 * q * LANE : (2 * q + 1) * LANE] = sums[2].astype(bf16)
            far_grad[at, (2 * q + 1) * LANE : (2 * q + 2) * LANE] = sums[3].astype(bf16)


def qkv_back_kernel(
    query_grad,
    own_grad,
    far_grad,
    weight,
    normed,
    unit,
    ff_sums,
    mid_sums,
    proj_own,
    proj_far,
    own,
    far,
    joined,
    small,
    mixed,
    sums,
):
    rep, shard, core = mesh_place()
    for p in range(CORES):
        base = p * TRIPLE
        mixed[:, base : base + LANE] = query_grad[:, p * LANE : (p + 1) * LANE]
        at = slice(2 * p * LANE, (2 * p + 2) * LANE)
        mixed[:, base + LANE : base + 3 * LANE] = (
            own_grad[:, at] + far_grad[:, at].astype(f32)
        ).astype(bf16)
    for k in range(SHARDS):
        at = lanes((shard ^ k) * SHARD, SHARD)
        grad = contract(normed[:, at], mixed[...], 0, 0).astype(bf16)
        own[k, :, 0:TRIPLE] = grad[:, 0:TRIPLE]
        far[k, :, 0:TRIPLE] = grad[:, TRIPLE:]
        own[k, :, TRIPLE:] = proj_own[k]
        far[k, :, TRIPLE:] = proj_far[k]
    gain = jnp.zeros((1, WIDTH), f32)
    shift = jnp.zeros((1, WIDTH), f32)
    for k in range(REPS):
        at = pl.ds(k * ROWS, ROWS)
        back = dot_rows(mixed[at, :], weight[...])
        joined[at, :] = back.astype(bf16)
        gain = gain + jnp.sum(back * unit[at, :], 0, keepdims=True)
        shift = shift + jnp.sum(back, 0, keepdims=True)
    sums[0:1, :] = gain
    sums[1:2, :] = shift
    mixed_sums = jnp.sum(mixed[...].astype(f32), 0, keepdims=True)
    for p in range(CORES):
        for i in range(2):
            start = i * SHARD + (core ^ p) * LANE
            sums[2:3, lanes(start, LANE)] = mixed_sums[
                :, p * TRIPLE + 2 * i * LANE : p * TRIPLE + (2 * i + 1) * LANE
            ]
    for k in range(SHARDS):
        small[k] = jnp.zeros(small.shape[1:], f32)
        at = lanes((shard ^ k) * SHARD, SHARD)
        small[k, 0:1, 0:SHARD] = sums[0:1, at]
        small[k, 1:2, 0:SHARD] = sums[1:2, at]
        queries = jnp.where((shard ^ k) == rep // 2, sums[2:3, 0:SHARD], 0.0)
        values = jnp.where((shard ^ k) == 2 + rep // 2, sums[2:3, SHARD : 2 * SHARD], 0.0)
        small[k, 2:3, 0:SHARD] = jnp.where(rep % 2 == 0, queries + values, 0.0)
        small[k, 3:4, 0:SHARD] = jnp.where(rep % 2 == 1, queries + values, 0.0)
        for i in range(4):
            small[k, 4 + i : 5 + i, 0:SHARD] = mid_sums[i : i + 1, at]
        part = ff_sums[:, at]
        row = lax.broadcasted_iota(jnp.int32, part.shape, 0)
        small[k, 8:16, 0:SHARD] = jnp.where(row == rep, part, 0.0)


def tail_kernel(own, far, small, o0, o1, o2, o3):
    for k, o in enumerate((o0, o1, o2, o3)):
        o[0:SHARD, :] = (own[k].astype(f32) + far[k].astype(f32)).astype(bf16)
        o[SHARD:, :] = small[k].astype(bf16)


def input_kernel(j, unit, vectors, middle_grad, grad):
    back = total(range(REPS), lambda k: j[k * ROWS : (k + 1) * ROWS, :].astype(f32))
    part, _, _ = norm_pull(unit[0], unit[1, :, 0:1], vectors[0:1, :], back)
    grad[...] = middle_grad[...] + part


def block_kernel(j, middle, vectors, block):
    output = total(range(REPS), lambda k: j[k * ROWS : (k + 1) * ROWS, :].astype(f32))
    block[...] = (middle[...] + output + vectors[7:8, :]).astype(bf16)


def joined_sum(pieces):
    pieces = [p.astype(f32) for p in pieces]
    return ((pieces[0] + pieces[1]) + (pieces[2] + pieces[3])).astype(bf16)


def final_kernel(p0, p1, p2, p3, f0, f1, f2, f3, qkv, proj, small):
    rep, _, core = mesh_place()
    for k, pair in enumerate(((p0, f0), (p1, f1), (p2, f2), (p3, f3))):
        for j, piece in enumerate(pair):
            start = ((rep ^ k) * CORES + (core ^ j)) * LANE
            for t in range(3):
                qkv[:, lanes(t * WIDTH + start, LANE)] = piece[
                    0:SHARD, t * LANE : (t + 1) * LANE
                ].astype(f32)
            proj[:, lanes(start, LANE)] = piece[0:SHARD, TRIPLE:].astype(f32)

    def read(pair):
        return pair[0][SHARD:, 0:SHARD].astype(f32) + pair[1][SHARD:, 0:SHARD].astype(f32)

    small[...] = total(((p0, f0), (p1, f1), (p2, f2), (p3, f3)), read)


def spread_kernel(p0, p1, p2, p3, f0, f1, f2, f3, fc, out):
    rep, _, core = mesh_place()
    for k, pair in enumerate(((p0, f0), (p1, f1), (p2, f2), (p3, f3))):
        for j, piece in enumerate(pair):
            at = pl.ds(pl.multiple_of(((rep ^ k) * CORES + (core ^ j)) * LANE, LANE), LANE)
            fc[at, :] = piece[0].astype(f32)
            out[at, :] = piece[1].astype(f32)


def tiled_body(
    block_input,
    ln1_gain,
    ln1_shift,
    qkv_weight,
    qv_bias,
    proj_weight,
    proj_bias,
    ln2_gain,
    ln2_shift,
    fc_weight,
    fc_bias,
    out_weight,
    out_bias,
    cotangent,
):
    rep, _, core = mesh_place()

    def over_rep(pieces):
        return [swap(p, "rep", REPS, k) if k else p for k, p in enumerate(pieces)]

    def over_shards(pieces):
        return [swap(p, "fsdp", SHARDS, k) if k else p for k, p in enumerate(pieces)]

    def over_cores(value):
        return swap(value, "seq", CORES, 1)

    all_rows = REPS * ROWS
    vectors = [
        ln1_gain,
        ln1_shift,
        qv_bias,
        proj_bias,
        ln2_gain,
        ln2_shift,
        out_bias,
        fc_bias,
    ]
    packed, own_rows = vmem_call(
        pack_kernel,
        [((SHARD + 16, TRIPLE + LANE), bf16), ((all_rows, WIDTH), bf16)],
        [qkv_weight, proj_weight, block_input] + vectors,
        hbm=tuple(range(11)),
        scratch=[pltpu.VMEM((12 * SHARD,), bf16), pltpu.SemaphoreType.DMA((16,))],
        limit=56,
    )
    own_packed = over_shards([packed] * SHARDS)
    far_packed = [over_cores(p) for p in own_packed]
    inputs = lax.all_to_all(own_rows, "rep", 0, 0, tiled=True)

    unit_one, _, unit_own = vmem_call(
        unit_kernel,
        [((all_rows, WIDTH), f32), ((all_rows, LANE), f32), ((2, ROWS, WIDTH), f32)],
        [inputs],
    )
    cots = over_rep([cotangent] * REPS)

    mine = rep * CORES + core
    ff = [pick(w.reshape(REPS * CORES, LANE, WIDTH), mine, 0) for w in (fc_weight, out_weight)]
    ff = after(jnp.stack(ff), *own_packed[1:], inputs, *cots[1:])
    ff = lax.all_gather(ff, ("fsdp", "seq"), axis=0)

    qkv, kv_send, normed_one, qkv_mine, vectors, proj_cols = vmem_call(
        qkv_kernel,
        [
            ((all_rows, 2 * TRIPLE), bf16),
            ((all_rows, 4 * LANE), bf16),
            ((all_rows, WIDTH), bf16),
            ((WIDTH, 2 * TRIPLE), bf16),
            ((16, WIDTH), f32),
            ((WIDTH, LANE), bf16),
        ],
        [unit_one] + own_packed + far_packed,
        scratch=[pltpu.VMEM((8, 2 * TRIPLE), f32)],
        flops=2 * all_rows * WIDTH * 2 * TRIPLE,
    )
    kv_far = over_cores(kv_send)
    proj_cols = over_rep([proj_cols] * REPS)
    attended, logs = vmem_call(
        attend_kernel,
        [((all_rows, SHARD), bf16), ((all_rows, LANE), f32)],
        [qkv, kv_far],
        flops=4 * all_rows * 2 * ROWS * SHARD,
    )
    mine = lax.all_to_all(attended, "rep", 0, 0, tiled=True)
    middle, unit_two, scale_two, normed_two, proj_full = vmem_call(
        branch_kernel,
        [
            ((ROWS, WIDTH), f32),
            ((ROWS, WIDTH), f32),
            ((ROWS, LANE), f32),
            ((all_rows, WIDTH), bf16),
            ((WIDTH, WIDTH), bf16),
        ],
        [mine]
        + proj_cols
        + [over_cores(after(p, mine)) for p in proj_cols]
        + [block_input, vectors],
        scratch=[pltpu.VMEM((ROWS, WIDTH), bf16)],
        flops=2 * ROWS * WIDTH * WIDTH,
    )
    normed_two = lax.all_to_all(normed_two, "rep", 0, 0, tiled=True)
    attended_all = over_rep([after(attended, normed_two)] * REPS)

    back, hidden, pre_grad, c_all = vmem_call(
        hidden_kernel,
        [
            ((all_rows, WIDTH), bf16),
            ((all_rows, HIDDEN), bf16),
            ((all_rows, HIDDEN), bf16),
            ((all_rows, WIDTH), bf16),
        ],
        [normed_two] + cots + [ff, vectors],
        flops=6 * all_rows * WIDTH * HIDDEN,
    )
    back = lax.all_to_all(back, "rep", 0, 0, tiled=True)
    output, ff_grads, ff_sums = vmem_call(
        weights_kernel,
        [
            ((all_rows, WIDTH), bf16),
            ((SHARDS * CORES * 2, LANE, WIDTH), bf16),
            ((8, HIDDEN), f32),
        ],
        [after(hidden, *attended_all[1:]), pre_grad, normed_two, c_all, ff],
        scratch=[
            pltpu.VMEM((SHARDS * CORES * 2, LANE, WIDTH), bf16),
            pltpu.SemaphoreType.DMA((SHARDS,)),
        ],
        away=(1,),
        flops=6 * all_rows * WIDTH * HIDDEN,
    )
    ff_piece = lax.psum_scatter(ff_grads, ("fsdp", "seq"), scatter_dimension=0, tiled=True)

    middle_grad, pairs, mid_sums = vmem_call(
        middle_kernel,
        [((ROWS, WIDTH), f32), ((all_rows, 2 * SHARD), bf16), ((8, WIDTH), f32)],
        [back, unit_two, scale_two, vectors, cotangent, proj_full],
        scratch=[pltpu.VMEM((ROWS, WIDTH), bf16)] * 2,
        flops=2 * ROWS * WIDTH * WIDTH,
    )
    pairs = lax.all_to_all(pairs, "rep", 0, 0, tiled=True)
    output = lax.all_to_all(after(output, pairs), "rep", 0, 0, tiled=True)
    (block_output,) = vmem_call(block_kernel, [((ROWS, WIDTH), bf16)], [output, middle, vectors])
    query_grad, own_grad, far_grad = vmem_call(
        attend_back_kernel,
        [
            ((all_rows, SHARD), bf16),
            ((all_rows, 4 * LANE), f32),
            ((all_rows, 4 * LANE), bf16),
        ],
        [qkv, kv_far, logs, pairs],
        weight=1,
        flops=10 * all_rows * 2 * ROWS * SHARD,
    )
    proj_own, proj_far = vmem_call(
        proj_grad_kernel,
        [((SHARDS, SHARD, LANE), bf16)] * 2,
        attended_all + [pairs],
        flops=2 * all_rows * WIDTH * SHARD,
    )
    qkv_own, qkv_far, joined, small = vmem_call(
        qkv_back_kernel,
        [
            ((SHARDS, SHARD, TRIPLE + LANE), bf16),
            ((SHARDS, SHARD, TRIPLE + LANE), bf16),
            ((all_rows, WIDTH), bf16),
            ((SHARDS, 16, TRIPLE + LANE), f32),
        ],
        [query_grad, own_grad, over_cores(far_grad), qkv_mine, normed_one, unit_one, ff_sums, mid_sums]
        + [proj_own, proj_far],
        scratch=[pltpu.VMEM((all_rows, 2 * TRIPLE), bf16), pltpu.VMEM((8, WIDTH), f32)],
        flops=4 * all_rows * WIDTH * 2 * TRIPLE,
    )
    tail = vmem_call(
        tail_kernel,
        [((SHARD + 16, TRIPLE + LANE), bf16)] * SHARDS,
        [qkv_own, over_cores(qkv_far), small],
    )
    tail = over_shards(tail)
    joined = lax.all_to_all(joined, "rep", 0, 0, tiled=True)
    ff_pieces = over_rep([ff_piece] * REPS)
    tail = joined_sum([after(tail[0], joined, block_output)] + tail[1:])
    (input_grad,) = vmem_call(
        input_kernel, [((ROWS, WIDTH), f32)], [joined, unit_own, vectors, middle_grad]
    )
    whole_tail, tail = tail, over_rep([tail] * REPS)
    fc_grads, out_grads = vmem_call(
        spread_kernel,
        [((2 * REPS * LANE, WIDTH), f32)] * 2,
        ff_pieces + [over_cores(after(p, whole_tail)) for p in ff_pieces],
    )
    qkv_grads, proj_grads, small = vmem_call(
        final_kernel,
        [((SHARD, 3 * WIDTH), f32), ((SHARD, WIDTH), f32), ((16, SHARD), f32)],
        tail + [over_cores(after(t, fc_grads, input_grad)) for t in tail],
    )
    return (
        block_output,
        input_grad,
        small[0],
        small[1],
        qkv_grads,
        small[2:4].reshape(-1),
        proj_grads,
        small[4],
        small[5],
        small[6],
        fc_grads,
        small[8:12].reshape(-1),
        out_grads,
        small[7],
    )


def make_body(reps, shards, cores):
    def rep_swap(value, offset):
        return swap(value, "rep", reps, offset) if offset else value

    def shard_swap(value, offset):
        return swap(value, "fsdp", shards, offset) if offset else value

    def core_swap(value):
        return swap(value, "seq", cores, 1)

    def plane_gather(value):
        return [rep_swap(value, k) for k in range(reps)]

    def plane_exchange(pieces):
        return [rep_swap(piece, k) for k, piece in enumerate(pieces)]

    def pair_sum(pieces):
        while len(pieces) > 1:
            pieces = [pieces[i] + pieces[i + 1] for i in range(0, len(pieces), 2)]
        return pieces[0]

    def own_scatter(parts):
        core = lax.axis_index("seq")
        shard = lax.axis_index("fsdp")
        kept = pick(parts, core, 1).astype(f32)
        kept = (kept + core_swap(pick(parts, 1 - core, 1)).astype(f32)).astype(bf16)
        pieces = [shard_swap(pick(kept, shard ^ k, 0), k).astype(f32) for k in range(shards)]
        return pair_sum(pieces).astype(bf16)

    def place_both(pieces):
        core = lax.axis_index("seq")
        rep = lax.axis_index("rep")
        held = jnp.zeros((reps, cores) + pieces[0].shape, pieces[0].dtype)
        zeros = (0,) * pieces[0].ndim
        for k, piece in enumerate(pieces):
            held = lax.dynamic_update_slice(held, piece[None, None], (rep ^ k, core) + zeros)
            far = core_swap(piece)
            held = lax.dynamic_update_slice(held, far[None, None], (rep ^ k, 1 - core) + zeros)
        return held

    def body(
        block_input,
        ln1_gain,
        ln1_shift,
        qkv_weight,
        qv_bias,
        proj_weight,
        proj_bias,
        ln2_gain,
        ln2_shift,
        fc_weight,
        fc_bias,
        out_weight,
        out_bias,
        cotangent,
    ):
        rows, width = block_input.shape
        shard_width = width // shards
        part = width // (reps * cores)
        rep_width = part * cores
        hidden_part = fc_weight.shape[0] // (reps * cores)
        head_scale = HEAD_DIM ** (-0.5)
        rep = lax.axis_index("rep")
        shard = lax.axis_index("fsdp")
        core = lax.axis_index("seq")
        rep_at = [rep ^ k for k in range(reps)]
        shard_at = [shard ^ k for k in range(shards)]

        columns = qkv_weight.reshape(shard_width, 3, reps, cores, part)
        columns = pick(pick(columns, rep, 2), core, 2).reshape(shard_width, 3 * part)
        fc_bias_part = pick(fc_bias.reshape(reps, -1), rep, 0)
        vectors = [
            ln1_gain,
            ln1_shift,
            qv_bias[:shard_width],
            qv_bias[shard_width:],
            proj_bias,
            ln2_gain,
            ln2_shift,
            out_bias,
            fc_bias_part,
        ]
        vectors = [jnp.pad(v, (0, 3 * part - v.shape[0])) for v in vectors]
        vectors = jnp.stack(vectors + [jnp.zeros_like(vectors[0])] * (16 - len(vectors)))
        packed = jnp.concatenate([columns, vectors], 0)
        packed, own_rows = lax.optimization_barrier((packed, block_input))
        packed = place([shard_swap(packed, k) for k in range(shards)], shard_at)
        inputs_all = jnp.concatenate(plane_gather(own_rows), 0)
        columns = packed[:, :shard_width].reshape(width, 3 * part)
        vectors = packed[:, shard_width:, :].astype(f32)

        def vector(index, size):
            return vectors[:, index, :size].reshape(-1)

        gain_one, shift_one = vector(0, shard_width), vector(1, shard_width)
        qv_full = jnp.stack([vectors[:, 2, :shard_width], vectors[:, 3, :shard_width]], 1)
        qv_full = qv_full.reshape(2, reps, cores * part)
        proj_bias_full = vector(4, shard_width)
        gain_two, shift_two = vector(5, shard_width), vector(6, shard_width)
        out_bias_full = vector(7, shard_width)
        fc_bias_mine = vector(8, fc_bias_part.shape[0])
        qkv_mine = place([columns, core_swap(columns)], [core, 1 - core])
        qkv_mine = jnp.transpose(qkv_mine, (1, 0, 2)).reshape(width, cores * 3 * part)

        proj_part = pick(proj_weight.reshape(reps * cores, -1, width), rep * cores + core, 0)
        proj_full = lax.all_gather(proj_part, ("rep", "fsdp", "seq"), axis=0)
        proj_full = proj_full.reshape((reps, shards, cores) + proj_part.shape)
        proj_full = jnp.transpose(proj_full, (1, 0, 2, 3, 4)).reshape(width, width)

        fc_part = pick(fc_weight.reshape(reps * cores, hidden_part, width), rep * cores + core, 0)
        out_part = pick(out_weight.reshape(reps * cores, hidden_part, width), rep * cores + core, 0)
        both_part = jnp.stack([fc_part, out_part])
        both_part, packed = lax.optimization_barrier((both_part, packed))
        both = place([shard_swap(both_part, k) for k in range(shards)], shard_at)
        both = place([both, core_swap(both)], [core, 1 - core])
        fc_mine = jnp.transpose(both[:, :, 0], (1, 0, 2, 3)).reshape(-1, width)
        out_mine = jnp.transpose(both[:, :, 1], (1, 0, 2, 3)).reshape(-1, width)

        own_cot, inputs_all = lax.optimization_barrier((cotangent, inputs_all))
        cot_all = jnp.concatenate(plane_gather(own_cot), 0)

        unit_one, scale_one = normalise(inputs_all.astype(f32))
        normed_all = (unit_one * gain_one + shift_one).astype(bf16)
        mixed = jnp.dot(normed_all, qkv_mine, preferred_element_type=f32)
        mixed = mixed.reshape(reps, rows, cores, 3, part)
        qv_mine = pick(qv_full, rep, 1).reshape(2, cores, part)
        heads = (reps, rows, rep_width // HEAD_DIM, HEAD_DIM)
        queries = (mixed[:, :, :, 0] + qv_mine[0]).astype(bf16).reshape(heads)
        keys = mixed[:, :, :, 1].astype(bf16).reshape(heads)
        values = (mixed[:, :, :, 2] + qv_mine[1]).astype(bf16).reshape(heads)
        far_pair = core_swap(jnp.stack([keys, values]))
        keys_both = jnp.concatenate([keys, far_pair[0]], 1)
        values_both = jnp.concatenate([values, far_pair[1]], 1)

        row_pos = lax.broadcasted_iota(jnp.int32, (rows, 2 * rows), 0)
        col_pos = lax.broadcasted_iota(jnp.int32, (rows, 2 * rows), 1)
        allowed = jnp.where(col_pos < rows, col_pos <= row_pos, core == 1)
        scores = jnp.einsum("sqhd,skhd->shqk", queries, keys_both, preferred_element_type=f32)
        scores = jnp.where(allowed, scores * head_scale, masked_value)
        peak = jnp.max(scores, -1, keepdims=True)
        powers = jnp.exp(scores - peak)
        probs = powers / jnp.sum(powers, -1, keepdims=True)
        probs_low = probs.astype(bf16)
        attended = jnp.einsum("shqk,skhd->sqhd", probs_low, values_both, preferred_element_type=f32)
        attended_low = attended.astype(bf16).reshape(reps, rows, rep_width)
        mine = place(plane_exchange([attended_low[k] for k in range(reps)]), rep_at)
        mine = jnp.transpose(mine, (1, 0, 2)).reshape(rows, width)
        middle = (
            block_input.astype(f32)
            + jnp.dot(mine, proj_full, preferred_element_type=f32)
            + proj_bias_full
        )
        unit_two, scale_two = normalise(middle)
        normed_two = (unit_two * gain_two + shift_two).astype(bf16)
        normed_two_all = jnp.concatenate(plane_gather(normed_two), 0)

        attended_all = place([attended_low[k] for k in range(reps)], rep_at)
        attended_all = lax.all_gather(attended_all.reshape(reps * rows, rep_width), "rep", axis=0)
        attended_all = jnp.transpose(attended_all, (1, 0, 2)).reshape(reps * rows, width)

        hidden_grad = contract(cot_all, out_mine, 1, 1)
        preact = contract(normed_two_all, fc_mine, 1, 1) + fc_bias_mine
        hidden, slope = gelu_and_slope(preact)
        hidden_low = hidden.astype(bf16)
        pre_grad = (hidden_grad * slope).astype(bf16)
        normed_grad = jnp.dot(pre_grad, fc_mine, preferred_element_type=f32).astype(bf16)
        normed_grad = normed_grad.reshape(reps, rows, width)
        normed_grad = plane_exchange([normed_grad[k] for k in range(reps)])
        normed_grad = pair_sum([v.astype(f32) for v in normed_grad])
        output = jnp.dot(hidden_low, out_mine, preferred_element_type=f32).astype(bf16)
        output, normed_grad = lax.optimization_barrier((output, normed_grad))
        output = output.reshape(reps, rows, width)
        output = plane_exchange([output[k] for k in range(reps)])
        output = pair_sum([v.astype(f32) for v in output])
        block_output = (middle + output + out_bias_full).astype(bf16)

        out_grads = contract(hidden_low, cot_all, 0, 0).astype(bf16)
        out_grads = lax.psum_scatter(out_grads, ("fsdp", "seq"), scatter_dimension=0, tiled=True)
        fc_grads = contract(pre_grad, normed_two_all, 0, 0).astype(bf16)
        fc_grads = own_scatter(fc_grads.reshape(shards, cores, hidden_part, width))
        ff_grads = plane_gather(jnp.stack([fc_grads, out_grads]))
        ff_grads = place_both(ff_grads)
        fc_grads = ff_grads[:, :, 0].reshape(-1, width).astype(f32)
        out_grads = ff_grads[:, :, 1].reshape(-1, width).astype(f32)

        middle_part, gain_two_grads, shift_two_grads = norm_pull(
            unit_two, scale_two, gain_two, normed_grad
        )
        middle_grad = cotangent.astype(f32) + middle_part
        branch_grad = middle_grad.astype(bf16)
        attended_grad = contract(branch_grad, proj_full, 1, 1).astype(bf16)
        pair = [v.reshape(rows, reps, rep_width) for v in (attended_grad, branch_grad)]
        pair = jnp.concatenate(pair, 2)
        pair = plane_exchange([pick(pair, i, 1) for i in rep_at])
        attended_grad = jnp.stack([v[:, :rep_width] for v in pair]).reshape(heads)
        branch_cols = place([v[:, rep_width:] for v in pair], rep_at).reshape(-1, rep_width)
        proj_grads = contract(attended_all, branch_cols, 0, 0).astype(bf16)
        proj_grads = proj_grads.reshape(shards, shard_width, cores, part)
        proj_grads = jnp.transpose(proj_grads, (0, 2, 1, 3)).reshape(-1, part)
        proj_grads = lax.psum_scatter(proj_grads, ("fsdp", "seq"), scatter_dimension=0, tiled=True)
        proj_grads = lax.all_gather(proj_grads, ("rep", "seq"), axis=0)
        proj_grads = jnp.transpose(proj_grads, (1, 0, 2)).reshape(shard_width, width).astype(f32)

        prob_grad = jnp.einsum("sqhd,skhd->shqk", attended_grad, values_both, preferred_element_type=f32)
        row_total = jnp.sum(probs * prob_grad, -1, keepdims=True)
        score_low = (probs * (prob_grad - row_total)).astype(bf16)
        query_grad = (
            jnp.einsum("shqk,skhd->sqhd", score_low, keys_both, preferred_element_type=f32)
            * head_scale
        )
        key_grad = (
            jnp.einsum("shqk,sqhd->skhd", score_low, queries, preferred_element_type=f32)
            * head_scale
        )
        value_grad = jnp.einsum("shqk,sqhd->skhd", probs_low, attended_grad, preferred_element_type=f32)
        far_grads = core_swap(jnp.stack([key_grad[:, rows:], value_grad[:, rows:]]).astype(bf16))
        key_grad = key_grad[:, :rows] + far_grads[0].astype(f32)
        value_grad = value_grad[:, :rows] + far_grads[1].astype(f32)
        mixed_grad = jnp.stack(
            [
                g.astype(bf16).reshape(reps * rows, cores, part)
                for g in (query_grad, key_grad, value_grad)
            ],
            2,
        ).reshape(reps * rows, cores * 3 * part)
        qkv_grads = contract(normed_all, mixed_grad, 0, 0).astype(bf16)
        normed_one_grad = contract(mixed_grad, qkv_mine, 1, 1)
        joined = normed_one_grad.astype(bf16).reshape(reps, rows, width)
        joined = plane_exchange([joined[k] for k in range(reps)])
        joined = pair_sum([v.astype(f32) for v in joined])
        input_part = norm_pull(unit_one[:rows], scale_one[:rows], gain_one, joined)[0]
        input_grad = middle_grad + input_part

        gain_one_grads = jnp.sum(normed_one_grad * unit_one, 0)
        shift_one_grads = jnp.sum(normed_one_grad, 0)
        mixed_sums = jnp.sum(mixed_grad.astype(f32), 0).reshape(cores, 3, part)
        qv_sums = jnp.stack([mixed_sums[:, 0].reshape(-1), mixed_sums[:, 2].reshape(-1)])
        qv_sums = lax.dynamic_update_index_in_dim(
            jnp.zeros((2, reps, rep_width), f32), qv_sums, rep, 1
        )
        fc_sums = jnp.sum(pre_grad.astype(f32), 0).reshape(shards, -1)
        fc_sums = lax.dynamic_update_index_in_dim(
            jnp.zeros((shards, reps, fc_sums.shape[1]), f32), fc_sums, rep, 1
        )
        small = [
            gain_one_grads,
            shift_one_grads,
            qv_sums,
            jnp.sum(branch_grad.astype(f32), 0),
            gain_two_grads,
            shift_two_grads,
            jnp.sum(cotangent.astype(f32), 0),
            fc_sums,
        ]
        small = jnp.concatenate([v.reshape(shards, -1) for v in small], 1).astype(bf16)
        small_size = small.shape[1]
        small_rows = -(-small_size // (16 * 3 * part)) * 16
        small = jnp.pad(small, ((0, 0), (0, small_rows * 3 * part - small_size)))
        small = small.reshape(shards, small_rows, 3 * part)

        qkv_grads = qkv_grads.reshape(shards, shard_width, cores, 3 * part)
        tail = pick(qkv_grads, core, 2).astype(f32)
        tail = (tail + core_swap(pick(qkv_grads, 1 - core, 2)).astype(f32)).astype(bf16)
        tail = jnp.concatenate([tail, small], 1)
        tail = [shard_swap(pick(tail, i, 0), k).astype(f32) for k, i in enumerate(shard_at)]
        tail = place_both(plane_gather(pair_sum(tail).astype(bf16)))
        qkv_grads = tail[:, :, :shard_width].reshape(reps * cores, shard_width, 3, part)
        qkv_grads = jnp.transpose(qkv_grads, (1, 2, 0, 3)).reshape(shard_width, 3 * width)
        qkv_grads = qkv_grads.astype(f32)
        small = jnp.sum(tail[:, :, shard_width:].astype(f32), (0, 1)).reshape(-1)
        sizes = [1, 1, 2, 1, 1, 1, 1]
        ends = [0]
        for size in sizes:
            ends.append(ends[-1] + size * shard_width)
        one = [small[a:b] for a, b in zip(ends[:-1], ends[1:])] + [small[ends[-1] : small_size]]
        return (
            block_output,
            input_grad,
            one[0],
            one[1],
            qkv_grads,
            one[2],
            proj_grads,
            one[3],
            one[4],
            one[5],
            fc_grads,
            one[7],
            out_grads,
            one[6],
        )

    return body


def solution(mesh):
    line, block = P("fsdp"), P("fsdp", None)
    tokens = P(("rep", "fsdp", "seq"), None)
    in_specs = (
        tokens,
        line,
        line,
        block,
        line,
        block,
        line,
        line,
        line,
        block,
        line,
        block,
        line,
        tokens,
    )
    out_specs = (
        tokens,
        tokens,
        line,
        line,
        block,
        line,
        block,
        line,
        line,
        line,
        block,
        line,
        block,
        line,
    )
    sizes = mesh.shape["rep"], mesh.shape["fsdp"], mesh.shape["seq"]
    general = make_body(*sizes)

    def body(*args):
        tiled = sizes == (REPS, SHARDS, CORES) and args[0].shape == (ROWS, WIDTH)
        return tiled_body(*args) if tiled else general(*args)

    return jax.shard_map(body, mesh=mesh, in_specs=in_specs, out_specs=out_specs, check_vma=False)
```

```python
import math

import jax
import jax.numpy as jnp
from jax import lax
from jax.experimental import pallas as pl
from jax.experimental.pallas import tpu as pltpu
from jax.sharding import PartitionSpec as P

HEADS = 16
HEAD_DIM = 64

norm_eps = 1e-05
masked_value = -1e30
f32 = jnp.float32
bf16 = jnp.bfloat16

REPS, SHARDS, CORES = 4, 4, 2
LANE, ROWS, WIDTH, SHARD, TRIPLE, HIDDEN = 128, 128, 1024, 256, 384, 1024
SCALE = HEAD_DIM ** (-0.5)


def normalise(values):
    centre = jnp.mean(values, -1, keepdims=True)
    offsets = values - centre
    spread = jnp.mean(offsets * offsets, -1, keepdims=True)
    scale = lax.rsqrt(spread + norm_eps)
    return offsets * scale, scale


def norm_pull(unit, scale, gain, grad):
    inner = grad * gain
    first = jnp.mean(inner, -1, keepdims=True)
    second = jnp.mean(inner * unit, -1, keepdims=True)
    return scale * (inner - first - unit * second), jnp.sum(grad * unit, 0), jnp.sum(grad, 0)


def gelu_and_slope(values):
    rate = 0.7978845608028654
    squared = values * values
    bent = jnp.tanh(rate * (values + 0.044715 * values * squared))
    half = 0.5 * (1.0 + bent)
    slope = half + 0.5 * values * (1.0 - bent * bent) * (rate * (1.0 + 3.0 * 0.044715 * squared))
    return values * half, slope


def contract(left, right, left_axis, right_axis):
    return lax.dot_general(
        left, right, (((left_axis,), (right_axis,)), ((), ())), preferred_element_type=f32
    )


def swap(value, axis, size, offset):
    return lax.ppermute(value, axis, [(i, i ^ offset) for i in range(size)])


def pick(array, index, axis):
    return lax.dynamic_index_in_dim(array, index, axis, keepdims=False)


def place(pieces, positions):
    stacked = jnp.zeros((len(pieces),) + pieces[0].shape, pieces[0].dtype)
    for piece, position in zip(pieces, positions):
        stacked = lax.dynamic_update_index_in_dim(stacked, piece, position, 0)
    return stacked


def lanes(start, size):
    return pl.ds(pl.multiple_of(start, LANE), size)


def vmem_call(kernel, outs, args, hbm=(), staged=(), scratch=(), flops=0, limit=16, away=(), weight=24):
    moved = sum(a.size * a.dtype.itemsize for a in args)
    moved += sum(math.prod(s) * jnp.dtype(t).itemsize for s, t in outs)
    whole = pl.BlockSpec(memory_space=pltpu.VMEM)
    far = pl.BlockSpec(memory_space=pltpu.HBM)
    n, m, k = len(args), len(outs), len(staged)

    def body(*refs):
        ins, rest, held, sems = list(refs[:n]), refs[n:], refs[n + m : n + m + k], refs[n + m + k]
        copies = [
            pltpu.make_async_copy(ins[i], held[j], sems.at[j]) for j, i in enumerate(staged)
        ]
        for copy in copies:
            copy.start()
        for copy in copies:
            copy.wait()
        for j, i in enumerate(staged):
            ins[i] = held[j]
        kernel(*ins, *rest[:m], *rest[m + k + 1 :])

    copied = [pltpu.VMEM(args[i].shape, args[i].dtype) for i in staged]
    if staged:
        copied.append(pltpu.SemaphoreType.DMA((k,)))
    return pl.pallas_call(
        body if staged else kernel,
        out_shape=[jax.ShapeDtypeStruct(s, t) for s, t in outs],
        in_specs=[far if i in hbm or i in staged else whole for i in range(n)],
        out_specs=[far if i in away else whole for i in range(m)],
        scratch_shapes=copied + list(scratch),
        compiler_params=pltpu.CompilerParams(vmem_limit_bytes=limit * 1024 * 1024),
        cost_estimate=pl.CostEstimate(
            flops=flops * weight, bytes_accessed=moved * weight, transcendentals=0
        ),
    )(*args)


def after(value, *others):
    return lax.optimization_barrier((value,) + others)[0]


def mesh_place():
    return lax.axis_index("rep"), lax.axis_index("fsdp"), lax.axis_index("seq")


def total(refs, read):
    return (read(refs[0]) + read(refs[1])) + (read(refs[2]) + read(refs[3]))


def pack_kernel(*refs):
    qkv, proj, x = refs[0:3]
    vectors, (packed, x_copy, held, sems) = refs[3:-4], refs[-4:]
    rep, _, core = mesh_place()
    mine = (rep * CORES + core) * LANE
    parts = [qkv.at[:, lanes(t * WIDTH + mine, LANE)] for t in range(3)]
    parts.append(proj.at[:, lanes(mine, LANE)])
    targets = [packed.at[pl.ds(0, SHARD), pl.ds(t * LANE, LANE)] for t in range(4)]
    parts += [x] * REPS
    targets += [x_copy.at[pl.ds(k * ROWS, ROWS), :] for k in range(REPS)]
    at = 0
    for v in vectors:
        parts.append(v)
        targets.append(held.at[pl.ds(at, v.shape[0])])
        at += v.shape[0]
    copies = [
        pltpu.make_async_copy(part, target, sems.at[i])
        for i, (part, target) in enumerate(zip(parts, targets))
    ]
    for copy in copies:
        copy.start()
    packed[SHARD:, SHARD:] = jnp.zeros((packed.shape[0] - SHARD, SHARD), bf16)
    for copy in copies:
        copy.wait()
    rows = [held[i * SHARD : (i + 1) * SHARD].astype(f32).reshape(1, SHARD) for i in range(8)]
    biases = [held[i * SHARD : (i + 1) * SHARD].astype(f32).reshape(1, SHARD) for i in range(8, 12)]
    rows.append(
        jnp.where(
            rep < 2,
            jnp.where(rep == 0, biases[0], biases[1]),
            jnp.where(rep == 2, biases[2], biases[3]),
        )
    )
    rows.append(jnp.zeros((16 - len(rows), SHARD), f32))
    packed[SHARD:, 0:SHARD] = jnp.concatenate(rows, 0).astype(bf16)


def unit_kernel(x, unit, scale, unit_own):
    for k in range(REPS):
        at = pl.ds(k * ROWS, ROWS)
        unit[at, :], spread = normalise(x[at, :].astype(f32))
        scale[at, :] = jnp.broadcast_to(spread, (ROWS, LANE))
    own = pl.ds(pl.multiple_of(lax.axis_index("rep") * ROWS, ROWS), ROWS)
    unit_own[0] = unit[own, :]
    unit_own[1, :, 0:LANE] = scale[own, :]
    unit_own[1, :, LANE:] = jnp.zeros((ROWS, WIDTH - LANE), f32)


def qkv_kernel(
    unit, p0, p1, p2, p3, f0, f1, f2, f3, qkv, kv_send, normed, weight, vectors, proj, biases
):
    rep, shard, core = mesh_place()
    for k, (own, far) in enumerate(((p0, f0), (p1, f1), (p2, f2), (p3, f3))):
        at = pl.ds(pl.multiple_of((shard ^ k) * SHARD, SHARD), SHARD)
        weight[at, 0:TRIPLE] = own[0:SHARD, 0:TRIPLE]
        weight[at, TRIPLE : 2 * TRIPLE] = far[0:SHARD, 0:TRIPLE]
        proj[at, :] = own[0:SHARD, TRIPLE:]
        vectors[:, at] = own[SHARD:, 0:SHARD].astype(f32)
    for p in range(CORES):
        for t, at in ((0, 0), (2, 2)):
            start = (at + rep // 2) * SHARD + (core ^ p) * LANE
            even, odd = vectors[2:3, lanes(start, LANE)], vectors[3:4, lanes(start, LANE)]
            biases[:, pl.ds(p * TRIPLE + t * LANE, LANE)] = jnp.broadcast_to(
                jnp.where(rep % 2 == 0, even, odd), (8, LANE)
            )
        biases[:, pl.ds(p * TRIPLE + LANE, LANE)] = jnp.zeros((8, LANE), f32)

    @pl.loop(0, 2)
    def _(block):
        at = pl.ds(pl.multiple_of(block * 2 * ROWS, 2 * ROWS), 2 * ROWS)
        values = (unit[at, :] * vectors[0:1, :] + vectors[1:2, :]).astype(bf16)
        normed[at, :] = values
        mixed = jnp.dot(values, weight[...], preferred_element_type=f32) + biases[0:1, :]
        mixed = mixed.astype(bf16)
        qkv[at, :] = mixed
        kv_send[at, 0 : 2 * LANE] = mixed[:, TRIPLE + LANE : 2 * TRIPLE]
        kv_send[at, 2 * LANE : 4 * LANE] = mixed[:, LANE:TRIPLE]


def dot_rows(left, right):
    return contract(left, right, 1, 1)


def head_scores(query, key_own, key_far, causal, far_seen):
    own = jnp.where(causal, dot_rows(query, key_own) * SCALE, masked_value)
    far = jnp.where(far_seen, dot_rows(query, key_far) * SCALE, masked_value)
    return own, far


def head_masks(core):
    causal = lax.broadcasted_iota(jnp.int32, (ROWS, ROWS), 1) <= lax.broadcasted_iota(
        jnp.int32, (ROWS, ROWS), 0
    )
    far_seen = (lax.broadcasted_iota(jnp.int32, (ROWS, ROWS), 0) * 0 + core) == 1
    first = lax.broadcasted_iota(jnp.int32, (ROWS, LANE), 1) < HEAD_DIM
    return causal, far_seen, first


def attend_kernel(qkv, far, attended, logs):
    core = lax.axis_index("seq")
    causal, far_seen, first = head_masks(core)
    lane = lax.broadcasted_iota(jnp.int32, (ROWS, LANE), 1)

    for sequence in range(REPS):
        at = pl.ds(sequence * ROWS, ROWS)
        for p in range(CORES):
            base = p * TRIPLE
            query = qkv[at, base : base + LANE]
            key_own = qkv[at, base + LANE : base + 2 * LANE]
            value_own = qkv[at, base + 2 * LANE : base + 3 * LANE]
            key_far = far[at, 2 * p * LANE : (2 * p + 1) * LANE]
            value_far = far[at, (2 * p + 1) * LANE : (2 * p + 2) * LANE]
            heads = []
            for h, mask in enumerate((first, ~first)):
                masked = jnp.where(mask, query, jnp.zeros_like(query))
                own, other = head_scores(masked, key_own, key_far, causal, far_seen)
                peak = jnp.max(jnp.maximum(own, other), -1, keepdims=True)
                own, other = jnp.exp(own - peak), jnp.exp(other - peak)
                whole = jnp.sum(own + other, -1, keepdims=True)
                share = 1.0 / whole
                own, other = own * share, other * share
                log = jnp.broadcast_to(peak + jnp.log(whole), (ROWS, LANE))
                kept = log if p + h == 0 else jnp.where(lane == 2 * p + h, log, kept)
                heads.append(
                    jnp.dot(own.astype(bf16), value_own, preferred_element_type=f32)
                    + jnp.dot(other.astype(bf16), value_far, preferred_element_type=f32)
                )
            if p == CORES - 1:
                logs[at, :] = kept
            attended[at, p * LANE : (p + 1) * LANE] = jnp.where(first, *heads).astype(bf16)


def branch_kernel(
    a, p0, p1, p2, p3, f0, f1, f2, f3, x, vectors, middle, unit, scale, normed, proj, joined
):
    rep, _, core = mesh_place()
    for k, pair in enumerate(((p0, f0), (p1, f1), (p2, f2), (p3, f3))):
        for p, piece in enumerate(pair):
            proj[:, lanes(((rep ^ k) * CORES + (core ^ p)) * LANE, LANE)] = piece[...]
    for k in range(REPS):
        for p in range(CORES):
            at = lanes((k * CORES + (core ^ p)) * LANE, LANE)
            joined[:, at] = a[k * ROWS : (k + 1) * ROWS, p * LANE : (p + 1) * LANE]
    branch = jnp.dot(joined[...], proj[...], preferred_element_type=f32)
    values = x[...].astype(f32) + branch + vectors[4:5, :]
    middle[...] = values
    norm, spread = normalise(values)
    unit[...] = norm
    scale[...] = jnp.broadcast_to(spread, (ROWS, LANE))
    low = (norm * vectors[5:6, :] + vectors[6:7, :]).astype(bf16)
    for k in range(REPS):
        normed[k * ROWS : (k + 1) * ROWS, :] = low


def hidden_kernel(h, c0, c1, c2, c3, ff, vectors, back, hidden, pre_grad, c):
    rep = lax.axis_index("rep")
    for k, cot in enumerate((c0, c1, c2, c3)):
        c[pl.ds(pl.multiple_of((rep ^ k) * ROWS, ROWS), ROWS), :] = cot[...]

    @pl.loop(0, 2)
    def _(block):
        at = pl.ds(pl.multiple_of(block * 2 * ROWS, 2 * ROWS), 2 * ROWS)
        for n in range(SHARDS):
            tile = pl.ds(n * 2 * LANE, 2 * LANE)
            pair = pl.ds(n * CORES, CORES)
            fc, out = ff[pair, 0].reshape(-1, WIDTH), ff[pair, 1].reshape(-1, WIDTH)
            preact = dot_rows(h[at, :], fc) + vectors[8:9, tile]
            value, slope = gelu_and_slope(preact)
            hidden[at, tile] = value.astype(bf16)
            grad = dot_rows(c[at, :], out)
            pre_grad[at, tile] = (grad * slope).astype(bf16)
        fc = ff[:, 0].reshape(HIDDEN, WIDTH)
        back[at, :] = jnp.dot(pre_grad[at, :], fc, preferred_element_type=f32).astype(bf16)


def weights_kernel(hidden, pre_grad, h, c, ff, output, grads, sums, held, sems):
    copies = []
    for n in range(SHARDS):
        tile = pl.ds(n * 2 * LANE, 2 * LANE)
        for i, (left, right) in enumerate(((pre_grad, h), (hidden, c))):
            grad = contract(left[:, tile], right[...], 0, 0).astype(bf16)
            for j in range(CORES):
                held[(n * CORES + j) * 2 + i] = grad[j * LANE : (j + 1) * LANE]
        part = pl.ds(n * CORES * 2, CORES * 2)
        copies.append(pltpu.make_async_copy(held.at[part], grads.at[part], sems.at[n]))
        copies[-1].start()
    sums[...] = jnp.broadcast_to(
        jnp.sum(pre_grad[...].astype(f32), 0, keepdims=True), sums.shape
    )

    @pl.loop(0, 2)
    def _(block):
        at = pl.ds(pl.multiple_of(block * 2 * ROWS, 2 * ROWS), 2 * ROWS)
        out = ff[:, 1].reshape(HIDDEN, WIDTH)
        output[at, :] = jnp.dot(hidden[at, :], out, preferred_element_type=f32).astype(bf16)

    for copy in copies:
        copy.wait()


def middle_kernel(
    g, unit, scale, vectors, cot, proj, middle_grad, pairs, sums, low, back
):
    rep, _, core = mesh_place()
    grad = total(range(REPS), lambda k: g[k * ROWS : (k + 1) * ROWS, :].astype(f32))
    part, gain, shift = norm_pull(unit[...], scale[:, 0:1], vectors[5:6, :], grad)
    cots = cot[...].astype(f32)
    values = cots + part
    middle_grad[...] = values
    branch = values.astype(bf16)
    low[...] = branch
    back[...] = dot_rows(branch, proj[...]).astype(bf16)
    rows = [jnp.sum(branch.astype(f32), 0), gain, shift, jnp.sum(cots, 0)]
    for i, row in enumerate(rows):
        sums[i : i + 1, :] = row[None]
    sums[4:8, :] = jnp.zeros((4, WIDTH), f32)
    for k in range(REPS):
        rows = pl.ds(k * ROWS, ROWS)
        for p in range(CORES):
            at = lanes((k * CORES + (core ^ p)) * LANE, LANE)
            pairs[rows, p * LANE : (p + 1) * LANE] = back[:, at]
        pairs[rows, SHARD : 2 * SHARD] = low[:, k * SHARD : (k + 1) * SHARD]


def proj_grad_kernel(a0, a1, a2, a3, pairs, own, far):
    rep, shard, core = mesh_place()
    for k, a in enumerate((a0, a1, a2, a3)):
        grad = contract(a[...], pairs[:, SHARD : 2 * SHARD], 0, 0).astype(bf16)
        mine = jnp.where(core == 0, grad[:, 0:LANE], grad[:, LANE:])
        other = jnp.where(core == 0, grad[:, LANE:], grad[:, 0:LANE])
        for p in range(CORES):
            at = pl.ds(pl.multiple_of((core ^ p) * LANE, LANE), LANE)
            own[rep ^ k ^ shard, at, :] = mine[p * LANE : (p + 1) * LANE]
            far[rep ^ k ^ shard, at, :] = other[p * LANE : (p + 1) * LANE]


def attend_back_kernel(qkv, far, logs, pairs, query_grad, own_grad, far_grad):
    core = lax.axis_index("seq")
    causal, far_seen, first = head_masks(core)

    for sequence in range(REPS):
        at = pl.ds(sequence * ROWS, ROWS)
        for p in range(CORES):
            base = p * TRIPLE
            query = qkv[at, base : base + LANE]
            key_own = qkv[at, base + LANE : base + 2 * LANE]
            value_own = qkv[at, base + 2 * LANE : base + 3 * LANE]
            key_far = far[at, 2 * p * LANE : (2 * p + 1) * LANE]
            value_far = far[at, (2 * p + 1) * LANE : (2 * p + 2) * LANE]
            grad = pairs[at, p * LANE : (p + 1) * LANE]
            queries, sums = [], [0.0] * 4
            for h, mask in enumerate((first, ~first)):
                masked = jnp.where(mask, query, jnp.zeros_like(query))
                back = jnp.where(mask, grad, jnp.zeros_like(grad))
                own, other = head_scores(masked, key_own, key_far, causal, far_seen)
                log = logs[at, 2 * p + h : 2 * p + h + 1]
                own, other = jnp.exp(own - log), jnp.exp(other - log)
                own_back, other_back = dot_rows(back, value_own), dot_rows(back, value_far)
                row = jnp.sum(own * own_back + other * other_back, -1, keepdims=True)
                own_score = (own * (own_back - row)).astype(bf16)
                other_score = (other * (other_back - row)).astype(bf16)
                queries.append(
                    jnp.dot(own_score, key_own, preferred_element_type=f32)
                    + jnp.dot(other_score, key_far, preferred_element_type=f32)
                )
                parts = [
                    contract(own_score, masked, 0, 0) * SCALE,
                    contract(own.astype(bf16), back, 0, 0),
                    contract(other_score, masked, 0, 0) * SCALE,
                    contract(other.astype(bf16), back, 0, 0),
                ]
                sums = [a + b for a, b in zip(sums, parts)]
            query_grad[at, p * LANE : (p + 1) * LANE] = (
                jnp.where(first, *queries) * SCALE
            ).astype(bf16)
            own_at = slice(2 * p * LANE, (2 * p + 1) * LANE)
            own_grad[at, own_at] = sums[0]
            own_grad[at, (2 * p + 1) * LANE : (2 * p + 2) * LANE] = sums[1]
            q = 1 - p
            far_grad[at, 2 * q * LANE : (2 * q + 1) * LANE] = sums[2].astype(bf16)
            far_grad[at, (2 * q + 1) * LANE : (2 * q + 2) * LANE] = sums[3].astype(bf16)


def qkv_back_kernel(
    query_grad,
    own_grad,
    far_grad,
    weight,
    normed,
    unit,
    ff_sums,
    mid_sums,
    proj_own,
    proj_far,
    own,
    far,
    joined,
    small,
    mixed,
    sums,
):
    rep, shard, core = mesh_place()
    for p in range(CORES):
        base = p * TRIPLE
        mixed[:, base : base + LANE] = query_grad[:, p * LANE : (p + 1) * LANE]
        at = slice(2 * p * LANE, (2 * p + 2) * LANE)
        mixed[:, base + LANE : base + 3 * LANE] = (
            own_grad[:, at] + far_grad[:, at].astype(f32)
        ).astype(bf16)
    for k in range(SHARDS):
        at = lanes((shard ^ k) * SHARD, SHARD)
        grad = contract(normed[:, at], mixed[...], 0, 0).astype(bf16)
        own[k, :, 0:TRIPLE] = grad[:, 0:TRIPLE]
        far[k, :, 0:TRIPLE] = grad[:, TRIPLE:]
        own[k, :, TRIPLE:] = proj_own[k]
        far[k, :, TRIPLE:] = proj_far[k]
    gain = jnp.zeros((1, WIDTH), f32)
    shift = jnp.zeros((1, WIDTH), f32)
    for k in range(2):
        at = pl.ds(k * 2 * ROWS, 2 * ROWS)
        back = dot_rows(mixed[at, :], weight[...])
        joined[at, :] = back.astype(bf16)
        gain = gain + jnp.sum(back * unit[at, :], 0, keepdims=True)
        shift = shift + jnp.sum(back, 0, keepdims=True)
    sums[0:1, :] = gain
    sums[1:2, :] = shift
    mixed_sums = jnp.sum(mixed[...].astype(f32), 0, keepdims=True)
    for p in range(CORES):
        for i in range(2):
            start = i * SHARD + (core ^ p) * LANE
            sums[2:3, lanes(start, LANE)] = mixed_sums[
                :, p * TRIPLE + 2 * i * LANE : p * TRIPLE + (2 * i + 1) * LANE
            ]
    for k in range(SHARDS):
        small[k] = jnp.zeros(small.shape[1:], f32)
        at = lanes((shard ^ k) * SHARD, SHARD)
        small[k, 0:1, 0:SHARD] = sums[0:1, at]
        small[k, 1:2, 0:SHARD] = sums[1:2, at]
        queries = jnp.where((shard ^ k) == rep // 2, sums[2:3, 0:SHARD], 0.0)
        values = jnp.where((shard ^ k) == 2 + rep // 2, sums[2:3, SHARD : 2 * SHARD], 0.0)
        small[k, 2:3, 0:SHARD] = jnp.where(rep % 2 == 0, queries + values, 0.0)
        small[k, 3:4, 0:SHARD] = jnp.where(rep % 2 == 1, queries + values, 0.0)
        for i in range(4):
            small[k, 4 + i : 5 + i, 0:SHARD] = mid_sums[i : i + 1, at]
        part = ff_sums[:, at]
        row = lax.broadcasted_iota(jnp.int32, part.shape, 0)
        small[k, 8:16, 0:SHARD] = jnp.where(row == rep, part, 0.0)


def tail_kernel(own, far, small, o0, o1, o2, o3):
    for k, o in enumerate((o0, o1, o2, o3)):
        o[0:SHARD, :] = (own[k].astype(f32) + far[k].astype(f32)).astype(bf16)
        o[SHARD:, :] = small[k].astype(bf16)


def input_kernel(j, unit, vectors, middle_grad, grad):
    back = total(range(REPS), lambda k: j[k * ROWS : (k + 1) * ROWS, :].astype(f32))
    part, _, _ = norm_pull(unit[0], unit[1, :, 0:1], vectors[0:1, :], back)
    grad[...] = middle_grad[...] + part


def block_kernel(j, middle, vectors, block):
    output = total(range(REPS), lambda k: j[k * ROWS : (k + 1) * ROWS, :].astype(f32))
    block[...] = (middle[...] + output + vectors[7:8, :]).astype(bf16)


def joined_sum(pieces):
    pieces = [p.astype(f32) for p in pieces]
    return ((pieces[0] + pieces[1]) + (pieces[2] + pieces[3])).astype(bf16)


def final_kernel(p0, p1, p2, p3, f0, f1, f2, f3, qkv, proj, small):
    rep, _, core = mesh_place()
    for k, pair in enumerate(((p0, f0), (p1, f1), (p2, f2), (p3, f3))):
        for j, piece in enumerate(pair):
            start = ((rep ^ k) * CORES + (core ^ j)) * LANE
            for t in range(3):
                qkv[:, lanes(t * WIDTH + start, LANE)] = piece[
                    0:SHARD, t * LANE : (t + 1) * LANE
                ].astype(f32)
            proj[:, lanes(start, LANE)] = piece[0:SHARD, TRIPLE:].astype(f32)

    def read(pair):
        return pair[0][SHARD:, 0:SHARD].astype(f32) + pair[1][SHARD:, 0:SHARD].astype(f32)

    small[...] = total(((p0, f0), (p1, f1), (p2, f2), (p3, f3)), read)


def spread_kernel(p0, p1, p2, p3, f0, f1, f2, f3, fc, out):
    rep, _, core = mesh_place()
    for k, pair in enumerate(((p0, f0), (p1, f1), (p2, f2), (p3, f3))):
        for j, piece in enumerate(pair):
            at = pl.ds(pl.multiple_of(((rep ^ k) * CORES + (core ^ j)) * LANE, LANE), LANE)
            fc[at, :] = piece[0].astype(f32)
            out[at, :] = piece[1].astype(f32)


def tiled_body(
    block_input,
    ln1_gain,
    ln1_shift,
    qkv_weight,
    qv_bias,
    proj_weight,
    proj_bias,
    ln2_gain,
    ln2_shift,
    fc_weight,
    fc_bias,
    out_weight,
    out_bias,
    cotangent,
):
    rep, _, core = mesh_place()

    def over_rep(pieces):
        return [swap(p, "rep", REPS, k) if k else p for k, p in enumerate(pieces)]

    def over_shards(pieces):
        return [swap(p, "fsdp", SHARDS, k) if k else p for k, p in enumerate(pieces)]

    def over_cores(value):
        return swap(value, "seq", CORES, 1)

    all_rows = REPS * ROWS
    vectors = [
        ln1_gain,
        ln1_shift,
        qv_bias,
        proj_bias,
        ln2_gain,
        ln2_shift,
        out_bias,
        fc_bias,
    ]
    packed, own_rows = vmem_call(
        pack_kernel,
        [((SHARD + 16, TRIPLE + LANE), bf16), ((all_rows, WIDTH), bf16)],
        [qkv_weight, proj_weight, block_input] + vectors,
        hbm=tuple(range(11)),
        scratch=[pltpu.VMEM((12 * SHARD,), bf16), pltpu.SemaphoreType.DMA((16,))],
        limit=56,
    )
    own_packed = over_shards([packed] * SHARDS)
    far_packed = [over_cores(p) for p in own_packed]
    inputs = lax.all_to_all(own_rows, "rep", 0, 0, tiled=True)

    unit_one, _, unit_own = vmem_call(
        unit_kernel,
        [((all_rows, WIDTH), f32), ((all_rows, LANE), f32), ((2, ROWS, WIDTH), f32)],
        [inputs],
    )
    cots = over_rep([cotangent] * REPS)

    mine = rep * CORES + core
    ff = [pick(w.reshape(REPS * CORES, LANE, WIDTH), mine, 0) for w in (fc_weight, out_weight)]
    ff = after(jnp.stack(ff), *own_packed[1:], inputs, *cots[1:])
    ff = lax.all_gather(ff, ("fsdp", "seq"), axis=0)

    qkv, kv_send, normed_one, qkv_mine, vectors, proj_cols = vmem_call(
        qkv_kernel,
        [
            ((all_rows, 2 * TRIPLE), bf16),
            ((all_rows, 4 * LANE), bf16),
            ((all_rows, WIDTH), bf16),
            ((WIDTH, 2 * TRIPLE), bf16),
            ((16, WIDTH), f32),
            ((WIDTH, LANE), bf16),
        ],
        [unit_one] + own_packed + far_packed,
        scratch=[pltpu.VMEM((8, 2 * TRIPLE), f32)],
        flops=2 * all_rows * WIDTH * 2 * TRIPLE,
    )
    kv_far = over_cores(kv_send)
    proj_cols = over_rep([proj_cols] * REPS)
    attended, logs = vmem_call(
        attend_kernel,
        [((all_rows, SHARD), bf16), ((all_rows, LANE), f32)],
        [qkv, kv_far],
        flops=4 * all_rows * 2 * ROWS * SHARD,
    )
    mine = lax.all_to_all(attended, "rep", 0, 0, tiled=True)
    middle, unit_two, scale_two, normed_two, proj_full = vmem_call(
        branch_kernel,
        [
            ((ROWS, WIDTH), f32),
            ((ROWS, WIDTH), f32),
            ((ROWS, LANE), f32),
            ((all_rows, WIDTH), bf16),
            ((WIDTH, WIDTH), bf16),
        ],
        [mine]
        + proj_cols
        + [over_cores(after(p, mine)) for p in proj_cols]
        + [block_input, vectors],
        scratch=[pltpu.VMEM((ROWS, WIDTH), bf16)],
        flops=2 * ROWS * WIDTH * WIDTH,
    )
    normed_two = lax.all_to_all(normed_two, "rep", 0, 0, tiled=True)
    attended_all = over_rep([after(attended, normed_two)] * REPS)

    back, hidden, pre_grad, c_all = vmem_call(
        hidden_kernel,
        [
            ((all_rows, WIDTH), bf16),
            ((all_rows, HIDDEN), bf16),
            ((all_rows, HIDDEN), bf16),
            ((all_rows, WIDTH), bf16),
        ],
        [normed_two] + cots + [ff, vectors],
        flops=6 * all_rows * WIDTH * HIDDEN,
    )
    back = lax.all_to_all(back, "rep", 0, 0, tiled=True)
    output, ff_grads, ff_sums = vmem_call(
        weights_kernel,
        [
            ((all_rows, WIDTH), bf16),
            ((SHARDS * CORES * 2, LANE, WIDTH), bf16),
            ((8, HIDDEN), f32),
        ],
        [after(hidden, *attended_all[1:]), pre_grad, normed_two, c_all, ff],
        scratch=[
            pltpu.VMEM((SHARDS * CORES * 2, LANE, WIDTH), bf16),
            pltpu.SemaphoreType.DMA((SHARDS,)),
        ],
        away=(1,),
        flops=6 * all_rows * WIDTH * HIDDEN,
    )
    ff_piece = lax.psum_scatter(ff_grads, ("fsdp", "seq"), scatter_dimension=0, tiled=True)

    middle_grad, pairs, mid_sums = vmem_call(
        middle_kernel,
        [((ROWS, WIDTH), f32), ((all_rows, 2 * SHARD), bf16), ((8, WIDTH), f32)],
        [back, unit_two, scale_two, vectors, cotangent, proj_full],
        scratch=[pltpu.VMEM((ROWS, WIDTH), bf16)] * 2,
        flops=2 * ROWS * WIDTH * WIDTH,
    )
    pairs = lax.all_to_all(pairs, "rep", 0, 0, tiled=True)
    output = lax.all_to_all(after(output, pairs), "rep", 0, 0, tiled=True)
    (block_output,) = vmem_call(block_kernel, [((ROWS, WIDTH), bf16)], [output, middle, vectors])
    query_grad, own_grad, far_grad = vmem_call(
        attend_back_kernel,
        [
            ((all_rows, SHARD), bf16),
            ((all_rows, 4 * LANE), f32),
            ((all_rows, 4 * LANE), bf16),
        ],
        [qkv, kv_far, logs, pairs],
        weight=1,
        flops=10 * all_rows * 2 * ROWS * SHARD,
    )
    proj_own, proj_far = vmem_call(
        proj_grad_kernel,
        [((SHARDS, SHARD, LANE), bf16)] * 2,
        attended_all + [pairs],
        flops=2 * all_rows * WIDTH * SHARD,
    )
    qkv_own, qkv_far, joined, small = vmem_call(
        qkv_back_kernel,
        [
            ((SHARDS, SHARD, TRIPLE + LANE), bf16),
            ((SHARDS, SHARD, TRIPLE + LANE), bf16),
            ((all_rows, WIDTH), bf16),
            ((SHARDS, 16, TRIPLE + LANE), f32),
        ],
        [query_grad, own_grad, over_cores(far_grad), qkv_mine, normed_one, unit_one, ff_sums, mid_sums]
        + [proj_own, proj_far],
        scratch=[pltpu.VMEM((all_rows, 2 * TRIPLE), bf16), pltpu.VMEM((8, WIDTH), f32)],
        flops=4 * all_rows * WIDTH * 2 * TRIPLE,
    )
    tail = vmem_call(
        tail_kernel,
        [((SHARD + 16, TRIPLE + LANE), bf16)] * SHARDS,
        [qkv_own, over_cores(qkv_far), small],
    )
    tail = over_shards(tail)
    joined = lax.all_to_all(joined, "rep", 0, 0, tiled=True)
    ff_pieces = over_rep([ff_piece] * REPS)
    tail = joined_sum([after(tail[0], joined, block_output)] + tail[1:])
    (input_grad,) = vmem_call(
        input_kernel, [((ROWS, WIDTH), f32)], [joined, unit_own, vectors, middle_grad]
    )
    whole_tail, tail = tail, over_rep([tail] * REPS)
    fc_grads, out_grads = vmem_call(
        spread_kernel,
        [((2 * REPS * LANE, WIDTH), f32)] * 2,
        ff_pieces + [over_cores(after(p, whole_tail)) for p in ff_pieces],
    )
    qkv_grads, proj_grads, small = vmem_call(
        final_kernel,
        [((SHARD, 3 * WIDTH), f32), ((SHARD, WIDTH), f32), ((16, SHARD), f32)],
        tail + [over_cores(after(t, fc_grads, input_grad)) for t in tail],
    )
    return (
        block_output,
        input_grad,
        small[0],
        small[1],
        qkv_grads,
        small[2:4].reshape(-1),
        proj_grads,
        small[4],
        small[5],
        small[6],
        fc_grads,
        small[8:12].reshape(-1),
        out_grads,
        small[7],
    )


def make_body(reps, shards, cores):
    def rep_swap(value, offset):
        return swap(value, "rep", reps, offset) if offset else value

    def shard_swap(value, offset):
        return swap(value, "fsdp", shards, offset) if offset else value

    def core_swap(value):
        return swap(value, "seq", cores, 1)

    def plane_gather(value):
        return [rep_swap(value, k) for k in range(reps)]

    def plane_exchange(pieces):
        return [rep_swap(piece, k) for k, piece in enumerate(pieces)]

    def pair_sum(pieces):
        while len(pieces) > 1:
            pieces = [pieces[i] + pieces[i + 1] for i in range(0, len(pieces), 2)]
        return pieces[0]

    def own_scatter(parts):
        core = lax.axis_index("seq")
        shard = lax.axis_index("fsdp")
        kept = pick(parts, core, 1).astype(f32)
        kept = (kept + core_swap(pick(parts, 1 - core, 1)).astype(f32)).astype(bf16)
        pieces = [shard_swap(pick(kept, shard ^ k, 0), k).astype(f32) for k in range(shards)]
        return pair_sum(pieces).astype(bf16)

    def place_both(pieces):
        core = lax.axis_index("seq")
        rep = lax.axis_index("rep")
        held = jnp.zeros((reps, cores) + pieces[0].shape, pieces[0].dtype)
        zeros = (0,) * pieces[0].ndim
        for k, piece in enumerate(pieces):
            held = lax.dynamic_update_slice(held, piece[None, None], (rep ^ k, core) + zeros)
            far = core_swap(piece)
            held = lax.dynamic_update_slice(held, far[None, None], (rep ^ k, 1 - core) + zeros)
        return held

    def body(
        block_input,
        ln1_gain,
        ln1_shift,
        qkv_weight,
        qv_bias,
        proj_weight,
        proj_bias,
        ln2_gain,
        ln2_shift,
        fc_weight,
        fc_bias,
        out_weight,
        out_bias,
        cotangent,
    ):
        rows, width = block_input.shape
        shard_width = width // shards
        part = width // (reps * cores)
        rep_width = part * cores
        hidden_part = fc_weight.shape[0] // (reps * cores)
        head_scale = HEAD_DIM ** (-0.5)
        rep = lax.axis_index("rep")
        shard = lax.axis_index("fsdp")
        core = lax.axis_index("seq")
        rep_at = [rep ^ k for k in range(reps)]
        shard_at = [shard ^ k for k in range(shards)]

        columns = qkv_weight.reshape(shard_width, 3, reps, cores, part)
        columns = pick(pick(columns, rep, 2), core, 2).reshape(shard_width, 3 * part)
        fc_bias_part = pick(fc_bias.reshape(reps, -1), rep, 0)
        vectors = [
            ln1_gain,
            ln1_shift,
            qv_bias[:shard_width],
            qv_bias[shard_width:],
            proj_bias,
            ln2_gain,
            ln2_shift,
            out_bias,
            fc_bias_part,
        ]
        vectors = [jnp.pad(v, (0, 3 * part - v.shape[0])) for v in vectors]
        vectors = jnp.stack(vectors + [jnp.zeros_like(vectors[0])] * (16 - len(vectors)))
        packed = jnp.concatenate([columns, vectors], 0)
        packed, own_rows = lax.optimization_barrier((packed, block_input))
        packed = place([shard_swap(packed, k) for k in range(shards)], shard_at)
        inputs_all = jnp.concatenate(plane_gather(own_rows), 0)
        columns = packed[:, :shard_width].reshape(width, 3 * part)
        vectors = packed[:, shard_width:, :].astype(f32)

        def vector(index, size):
            return vectors[:, index, :size].reshape(-1)

        gain_one, shift_one = vector(0, shard_width), vector(1, shard_width)
        qv_full = jnp.stack([vectors[:, 2, :shard_width], vectors[:, 3, :shard_width]], 1)
        qv_full = qv_full.reshape(2, reps, cores * part)
        proj_bias_full = vector(4, shard_width)
        gain_two, shift_two = vector(5, shard_width), vector(6, shard_width)
        out_bias_full = vector(7, shard_width)
        fc_bias_mine = vector(8, fc_bias_part.shape[0])
        qkv_mine = place([columns, core_swap(columns)], [core, 1 - core])
        qkv_mine = jnp.transpose(qkv_mine, (1, 0, 2)).reshape(width, cores * 3 * part)

        proj_part = pick(proj_weight.reshape(reps * cores, -1, width), rep * cores + core, 0)
        proj_full = lax.all_gather(proj_part, ("rep", "fsdp", "seq"), axis=0)
        proj_full = proj_full.reshape((reps, shards, cores) + proj_part.shape)
        proj_full = jnp.transpose(proj_full, (1, 0, 2, 3, 4)).reshape(width, width)

        fc_part = pick(fc_weight.reshape(reps * cores, hidden_part, width), rep * cores + core, 0)
        out_part = pick(out_weight.reshape(reps * cores, hidden_part, width), rep * cores + core, 0)
        both_part = jnp.stack([fc_part, out_part])
        both_part, packed = lax.optimization_barrier((both_part, packed))
        both = place([shard_swap(both_part, k) for k in range(shards)], shard_at)
        both = place([both, core_swap(both)], [core, 1 - core])
        fc_mine = jnp.transpose(both[:, :, 0], (1, 0, 2, 3)).reshape(-1, width)
        out_mine = jnp.transpose(both[:, :, 1], (1, 0, 2, 3)).reshape(-1, width)

        own_cot, inputs_all = lax.optimization_barrier((cotangent, inputs_all))
        cot_all = jnp.concatenate(plane_gather(own_cot), 0)

        unit_one, scale_one = normalise(inputs_all.astype(f32))
        normed_all = (unit_one * gain_one + shift_one).astype(bf16)
        mixed = jnp.dot(normed_all, qkv_mine, preferred_element_type=f32)
        mixed = mixed.reshape(reps, rows, cores, 3, part)
        qv_mine = pick(qv_full, rep, 1).reshape(2, cores, part)
        heads = (reps, rows, rep_width // HEAD_DIM, HEAD_DIM)
        queries = (mixed[:, :, :, 0] + qv_mine[0]).astype(bf16).reshape(heads)
        keys = mixed[:, :, :, 1].astype(bf16).reshape(heads)
        values = (mixed[:, :, :, 2] + qv_mine[1]).astype(bf16).reshape(heads)
        far_pair = core_swap(jnp.stack([keys, values]))
        keys_both = jnp.concatenate([keys, far_pair[0]], 1)
        values_both = jnp.concatenate([values, far_pair[1]], 1)

        row_pos = lax.broadcasted_iota(jnp.int32, (rows, 2 * rows), 0)
        col_pos = lax.broadcasted_iota(jnp.int32, (rows, 2 * rows), 1)
        allowed = jnp.where(col_pos < rows, col_pos <= row_pos, core == 1)
        scores = jnp.einsum("sqhd,skhd->shqk", queries, keys_both, preferred_element_type=f32)
        scores = jnp.where(allowed, scores * head_scale, masked_value)
        peak = jnp.max(scores, -1, keepdims=True)
        powers = jnp.exp(scores - peak)
        probs = powers / jnp.sum(powers, -1, keepdims=True)
        probs_low = probs.astype(bf16)
        attended = jnp.einsum("shqk,skhd->sqhd", probs_low, values_both, preferred_element_type=f32)
        attended_low = attended.astype(bf16).reshape(reps, rows, rep_width)
        mine = place(plane_exchange([attended_low[k] for k in range(reps)]), rep_at)
        mine = jnp.transpose(mine, (1, 0, 2)).reshape(rows, width)
        middle = (
            block_input.astype(f32)
            + jnp.dot(mine, proj_full, preferred_element_type=f32)
            + proj_bias_full
        )
        unit_two, scale_two = normalise(middle)
        normed_two = (unit_two * gain_two + shift_two).astype(bf16)
        normed_two_all = jnp.concatenate(plane_gather(normed_two), 0)

        attended_all = place([attended_low[k] for k in range(reps)], rep_at)
        attended_all = lax.all_gather(attended_all.reshape(reps * rows, rep_width), "rep", axis=0)
        attended_all = jnp.transpose(attended_all, (1, 0, 2)).reshape(reps * rows, width)

        hidden_grad = contract(cot_all, out_mine, 1, 1)
        preact = contract(normed_two_all, fc_mine, 1, 1) + fc_bias_mine
        hidden, slope = gelu_and_slope(preact)
        hidden_low = hidden.astype(bf16)
        pre_grad = (hidden_grad * slope).astype(bf16)
        normed_grad = jnp.dot(pre_grad, fc_mine, preferred_element_type=f32).astype(bf16)
        normed_grad = normed_grad.reshape(reps, rows, width)
        normed_grad = plane_exchange([normed_grad[k] for k in range(reps)])
        normed_grad = pair_sum([v.astype(f32) for v in normed_grad])
        output = jnp.dot(hidden_low, out_mine, preferred_element_type=f32).astype(bf16)
        output, normed_grad = lax.optimization_barrier((output, normed_grad))
        output = output.reshape(reps, rows, width)
        output = plane_exchange([output[k] for k in range(reps)])
        output = pair_sum([v.astype(f32) for v in output])
        block_output = (middle + output + out_bias_full).astype(bf16)

        out_grads = contract(hidden_low, cot_all, 0, 0).astype(bf16)
        out_grads = lax.psum_scatter(out_grads, ("fsdp", "seq"), scatter_dimension=0, tiled=True)
        fc_grads = contract(pre_grad, normed_two_all, 0, 0).astype(bf16)
        fc_grads = own_scatter(fc_grads.reshape(shards, cores, hidden_part, width))
        ff_grads = plane_gather(jnp.stack([fc_grads, out_grads]))
        ff_grads = place_both(ff_grads)
        fc_grads = ff_grads[:, :, 0].reshape(-1, width).astype(f32)
        out_grads = ff_grads[:, :, 1].reshape(-1, width).astype(f32)

        middle_part, gain_two_grads, shift_two_grads = norm_pull(
            unit_two, scale_two, gain_two, normed_grad
        )
        middle_grad = cotangent.astype(f32) + middle_part
        branch_grad = middle_grad.astype(bf16)
        attended_grad = contract(branch_grad, proj_full, 1, 1).astype(bf16)
        pair = [v.reshape(rows, reps, rep_width) for v in (attended_grad, branch_grad)]
        pair = jnp.concatenate(pair, 2)
        pair = plane_exchange([pick(pair, i, 1) for i in rep_at])
        attended_grad = jnp.stack([v[:, :rep_width] for v in pair]).reshape(heads)
        branch_cols = place([v[:, rep_width:] for v in pair], rep_at).reshape(-1, rep_width)
        proj_grads = contract(attended_all, branch_cols, 0, 0).astype(bf16)
        proj_grads = proj_grads.reshape(shards, shard_width, cores, part)
        proj_grads = jnp.transpose(proj_grads, (0, 2, 1, 3)).reshape(-1, part)
        proj_grads = lax.psum_scatter(proj_grads, ("fsdp", "seq"), scatter_dimension=0, tiled=True)
        proj_grads = lax.all_gather(proj_grads, ("rep", "seq"), axis=0)
        proj_grads = jnp.transpose(proj_grads, (1, 0, 2)).reshape(shard_width, width).astype(f32)

        prob_grad = jnp.einsum("sqhd,skhd->shqk", attended_grad, values_both, preferred_element_type=f32)
        row_total = jnp.sum(probs * prob_grad, -1, keepdims=True)
        score_low = (probs * (prob_grad - row_total)).astype(bf16)
        query_grad = (
            jnp.einsum("shqk,skhd->sqhd", score_low, keys_both, preferred_element_type=f32)
            * head_scale
        )
        key_grad = (
            jnp.einsum("shqk,sqhd->skhd", score_low, queries, preferred_element_type=f32)
            * head_scale
        )
        value_grad = jnp.einsum("shqk,sqhd->skhd", probs_low, attended_grad, preferred_element_type=f32)
        far_grads = core_swap(jnp.stack([key_grad[:, rows:], value_grad[:, rows:]]).astype(bf16))
        key_grad = key_grad[:, :rows] + far_grads[0].astype(f32)
        value_grad = value_grad[:, :rows] + far_grads[1].astype(f32)
        mixed_grad = jnp.stack(
            [
                g.astype(bf16).reshape(reps * rows, cores, part)
                for g in (query_grad, key_grad, value_grad)
            ],
            2,
        ).reshape(reps * rows, cores * 3 * part)
        qkv_grads = contract(normed_all, mixed_grad, 0, 0).astype(bf16)
        normed_one_grad = contract(mixed_grad, qkv_mine, 1, 1)
        joined = normed_one_grad.astype(bf16).reshape(reps, rows, width)
        joined = plane_exchange([joined[k] for k in range(reps)])
        joined = pair_sum([v.astype(f32) for v in joined])
        input_part = norm_pull(unit_one[:rows], scale_one[:rows], gain_one, joined)[0]
        input_grad = middle_grad + input_part

        gain_one_grads = jnp.sum(normed_one_grad * unit_one, 0)
        shift_one_grads = jnp.sum(normed_one_grad, 0)
        mixed_sums = jnp.sum(mixed_grad.astype(f32), 0).reshape(cores, 3, part)
        qv_sums = jnp.stack([mixed_sums[:, 0].reshape(-1), mixed_sums[:, 2].reshape(-1)])
        qv_sums = lax.dynamic_update_index_in_dim(
            jnp.zeros((2, reps, rep_width), f32), qv_sums, rep, 1
        )
        fc_sums = jnp.sum(pre_grad.astype(f32), 0).reshape(shards, -1)
        fc_sums = lax.dynamic_update_index_in_dim(
            jnp.zeros((shards, reps, fc_sums.shape[1]), f32), fc_sums, rep, 1
        )
        small = [
            gain_one_grads,
            shift_one_grads,
            qv_sums,
            jnp.sum(branch_grad.astype(f32), 0),
            gain_two_grads,
            shift_two_grads,
            jnp.sum(cotangent.astype(f32), 0),
            fc_sums,
        ]
        small = jnp.concatenate([v.reshape(shards, -1) for v in small], 1).astype(bf16)
        small_size = small.shape[1]
        small_rows = -(-small_size // (16 * 3 * part)) * 16
        small = jnp.pad(small, ((0, 0), (0, small_rows * 3 * part - small_size)))
        small = small.reshape(shards, small_rows, 3 * part)

        qkv_grads = qkv_grads.reshape(shards, shard_width, cores, 3 * part)
        tail = pick(qkv_grads, core, 2).astype(f32)
        tail = (tail + core_swap(pick(qkv_grads, 1 - core, 2)).astype(f32)).astype(bf16)
        tail = jnp.concatenate([tail, small], 1)
        tail = [shard_swap(pick(tail, i, 0), k).astype(f32) for k, i in enumerate(shard_at)]
        tail = place_both(plane_gather(pair_sum(tail).astype(bf16)))
        qkv_grads = tail[:, :, :shard_width].reshape(reps * cores, shard_width, 3, part)
        qkv_grads = jnp.transpose(qkv_grads, (1, 2, 0, 3)).reshape(shard_width, 3 * width)
        qkv_grads = qkv_grads.astype(f32)
        small = jnp.sum(tail[:, :, shard_width:].astype(f32), (0, 1)).reshape(-1)
        sizes = [1, 1, 2, 1, 1, 1, 1]
        ends = [0]
        for size in sizes:
            ends.append(ends[-1] + size * shard_width)
        one = [small[a:b] for a, b in zip(ends[:-1], ends[1:])] + [small[ends[-1] : small_size]]
        return (
            block_output,
            input_grad,
            one[0],
            one[1],
            qkv_grads,
            one[2],
            proj_grads,
            one[3],
            one[4],
            one[5],
            fc_grads,
            one[7],
            out_grads,
            one[6],
        )

    return body


def solution(mesh):
    line, block = P("fsdp"), P("fsdp", None)
    tokens = P(("rep", "fsdp", "seq"), None)
    in_specs = (
        tokens,
        line,
        line,
        block,
        line,
        block,
        line,
        line,
        line,
        block,
        line,
        block,
        line,
        tokens,
    )
    out_specs = (
        tokens,
        tokens,
        line,
        line,
        block,
        line,
        block,
        line,
        line,
        line,
        block,
        line,
        block,
        line,
    )
    sizes = mesh.shape["rep"], mesh.shape["fsdp"], mesh.shape["seq"]
    general = make_body(*sizes)

    def body(*args):
        tiled = sizes == (REPS, SHARDS, CORES) and args[0].shape == (ROWS, WIDTH)
        return tiled_body(*args) if tiled else general(*args)

    return jax.shard_map(body, mesh=mesh, in_specs=in_specs, out_specs=out_specs, check_vma=False)
```
